32 devices in a mesh: items: 16 (over z, y, core), heads: 2 (over x).
Axes of the slice: x: 2, y: 2, z: 4, core: 2. Of those that a mesh axis runs over, the one named last changes fastest.
Arguments:
- hidden_in: bfloat16 [16384, 768], P('items'), may hold values from -6 to 6
- cluster_order: int32 [12, 16, 1024], P('heads', 'items'), may hold values from 0 to 1023, as said below
- qkv_weight: bfloat16 [3, 768, 768], P(None, None, 'heads'), may hold values from -0.21875 to 0.21875
- qv_bias: float32 [2, 768], P(None, 'heads'), may hold values from -3 to 3
- out_weight: bfloat16 [768, 768], P('heads'), may hold values from -0.875 to 0.875
- out_bias: float32 [768], replicated, may hold values from -2 to 2
- norm1_gain: float32 [768], replicated, may hold values from 0.5 to 1.5
- norm1_bias: float32 [768], replicated, may hold values from -2 to 2
- up_weight: bfloat16 [768, 3072], P(None, 'heads'), may hold values from -0.21875 to 0.21875
- up_bias: float32 [3072], P('heads'), may hold values from -2 to 2
- down_weight: bfloat16 [3072, 768], P('heads'), may hold values from -0.109375 to 0.109375
- down_bias: float32 [768], replicated, may hold values from -2 to 2
- norm2_gain: float32 [768], replicated, may hold values from 0.5 to 1.5
- norm2_bias: float32 [768], replicated, may hold values from -2 to 2
- cotangent: bfloat16 [16384, 768], P('items'), may hold values from -6 to 6
Outputs:
- mixed: bfloat16 [16384, 768], P('items')
- input_grad: bfloat16 [16384, 768], P('items')
- qkv_weight_grad: float32 [3, 768, 768], P(None, 'items', 'heads')
- qv_bias_grad: float32 [2, 768], P(None, 'heads')
- out_weight_grad: float32 [768, 768], P('heads', 'items')
- out_bias_grad: float32 [768], replicated
- norm1_gain_grad: float32 [768], replicated
- norm1_bias_grad: float32 [768], replicated
- up_weight_grad: float32 [768, 3072], P('items', 'heads')
- up_bias_grad: float32 [3072], P('heads')
- down_weight_grad: float32 [3072, 768], P('heads', 'items')
- down_bias_grad: float32 [768], replicated
- norm2_gain_grad: float32 [768], replicated
- norm2_bias_grad: float32 [768], replicated
The draws below stay inside these ranges and needn't reach their ends.
Inputs may be any that keep to these rules, and one draw needn't show every extreme that they name: `cluster_order`: for each head and each device's block of 1024 tokens, an ordering of the block's positions 0 to 1023. A block holds one item of 1024 tokens or items of 512 tokens (the last one shorter where 512 does not divide 1024); an item's positions stand together in the ordering, in an order of their own for every head.
All inputs are finite; a program needn't handle non-finite values.
Results may differ from the reference program's by a relative error of at most 0.012.
Values sent between devices are 32-bit elements; how exact they have to be, the bound alone decides.
No kernel may reach another device: no remote copies, remote signals or barrier semaphores. Data moves between devices by JAX's collectives and lax.ppermute only.
A program may use at most 128 MiB of HBM per device.

```python
import jax
import jax.numpy as jnp
from jax import lax

D = 768
HEADS = 12
HEAD_DIM = 64
FF = 3072
CLUSTER = 128
SHORT = 512
TOK_DEV = 1024
TOKENS = 16384
N_ITEMS = 16


def draw_cluster_order(key, part):
    key = jax.random.fold_in(key, 11)
    blocks = TOKENS // TOK_DEV
    choose_key, rank_key = jax.random.split(key)
    single = jax.random.randint(choose_key, (blocks, 1), 0, 5) == 0
    positions = jnp.arange(TOK_DEV, dtype=jnp.int32)[None, :]
    member = jnp.where(single, 0, positions // SHORT)
    many_keys = jax.random.split(rank_key, HEADS * blocks)
    ranking = jax.vmap(lambda one_key: jax.random.permutation(one_key, TOK_DEV))(many_keys)
    ranking = ranking.astype(jnp.int32).reshape(HEADS, blocks, TOK_DEV)
    totals = member[None, :, :] * TOK_DEV + ranking
    return jnp.argsort(totals, axis=-1, stable=True).astype(jnp.int32)


def spiked(values, own_key, source, target, parts, factor):
    owner, partner = [(jnp.arange(values.shape[position]) // (values.shape[position] // parts)).reshape([-1 if axis == position else 1 for axis in range(values.ndim)]) for position in (source, target)]
    chosen = jax.random.permutation(own_key, parts)[partner]
    strong = (owner == chosen) | (owner == (partner + parts // 2) % parts)
    return jnp.where(strong, factor * values, values)


def block_scale(own_key, shape, cuts, smallest, largest):
    gain, own = 1.0, jax.random.fold_in(own_key, 6)
    for position, parts in cuts:
        heights = jnp.exp(jax.random.uniform(jax.random.fold_in(own, position), (parts,), jnp.float32, smallest / len(cuts), largest / len(cuts)))
        gain = gain * jnp.repeat(heights, shape[position] // parts).reshape([-1 if axis == position else 1 for axis in range(len(shape))])
    return gain


def scatter_about(rng, shape, scale, bound, pieces=(), held_as=jnp.bfloat16):
    values = scale * jax.random.normal(rng, shape, jnp.float32)
    if pieces:
        values = values * block_scale(rng, shape, pieces, -0.22, 0.18)
    return jnp.clip(values, -bound, bound).astype(held_as)


def noise_with(stream_key, dims, width, bound, shards, heavy, kind=jnp.bfloat16):
    array = width * jax.random.normal(stream_key, dims, jnp.float32)
    if shards:
        array = array * block_scale(stream_key, dims, shards, -0.22, 0.18)
    return jnp.clip(spiked(array, jax.random.fold_in(stream_key, 3), *heavy), -bound, bound).astype(kind)


def setup_inputs(seed: int = 0) -> dict:
    keys = jax.random.split(jax.random.key(seed), 16)
    hidden_in = scatter_about(keys[0], (TOKENS, D), 1.0, 6.0, ((0, 16),))
    cluster_order = draw_cluster_order(jax.random.fold_in(keys[15], 71), 0)
    qkv_weight = scatter_about(keys[2], (3, D, D), D ** -0.5, 0.21875, ((2, 2),))
    qv_bias = scatter_about(keys[3], (2, D), 0.5, 3.0, ((1, 2),), jnp.float32)
    out_weight = scatter_about(keys[4], (D, D), (D // 16) ** -0.5, 0.875, ((0, 2),))
    out_bias = scatter_about(keys[5], (D,), 0.3, 2.0, (), jnp.float32)
    norm1_gain = jnp.clip(1.0 + 0.1 * jax.random.normal(keys[6], (D,), jnp.float32), 0.5, 1.5)
    norm1_bias = scatter_about(keys[7], (D,), 0.3, 2.0, (), jnp.float32)
    up_weight = scatter_about(keys[8], (D, FF), D ** -0.5, 0.21875, ((1, 2),))
    up_bias = scatter_about(keys[9], (FF,), 0.3, 2.0, ((0, 2),), jnp.float32)
    down_weight = scatter_about(keys[10], (FF, D), FF ** -0.5, 0.109375, ((0, 2),))
    down_bias = scatter_about(keys[11], (D,), 0.3, 2.0, (), jnp.float32)
    norm2_gain = jnp.clip(1.0 + 0.1 * jax.random.normal(keys[12], (D,), jnp.float32), 0.5, 1.5)
    norm2_bias = scatter_about(keys[13], (D,), 0.3, 2.0, (), jnp.float32)
    cotangent = noise_with(keys[14], (TOKENS, D), 1.0, 6.0, ((0, 16),), (0, 1, 16, 2.0))
    return {"hidden_in": hidden_in, "cluster_order": cluster_order, "qkv_weight": qkv_weight, "qv_bias": qv_bias, "out_weight": out_weight, "out_bias": out_bias, "norm1_gain": norm1_gain, "norm1_bias": norm1_bias, "up_weight": up_weight, "up_bias": up_bias, "down_weight": down_weight, "down_bias": down_bias, "norm2_gain": norm2_gain, "norm2_bias": norm2_bias, "cotangent": cotangent}


@jax.custom_vjp
def low(v):
    return lax.optimization_barrier(v.astype(jnp.bfloat16)).astype(jnp.float32)

@jax.custom_vjp
def low_back(v):
    return v

def low_keep(v):
    return (low(v), None)

def low_pass(kept, grad):
    return (grad,)

def back_keep(v):
    return (v, None)

def back_low(kept, grad):
    return (low(grad),)
low.defvjp(low_keep, low_pass)
low_back.defvjp(back_keep, back_low)
EPSILON = 1e-05
HIGHEST = lax.Precision.HIGHEST

def matmul(left_side, right_side):
    return jnp.dot(left_side, right_side, precision=HIGHEST)

def layer_norm(values, scale_vec, shift_vec):
    centred = values - lax.optimization_barrier(jnp.mean(values, axis=-1, keepdims=True))
    spread = lax.optimization_barrier(jnp.mean(centred * centred, axis=-1, keepdims=True))
    return centred * lax.rsqrt(spread + EPSILON) * scale_vec + shift_vec

def round_both(values):
    return low(low_back(values))

def attend(query_rows, key_rows, value_rows, ordering):

    def clustered(values):
        by_head = values.reshape(TOK_DEV, HEADS, HEAD_DIM).transpose(1, 0, 2)
        moved_rows = jnp.take_along_axis(by_head, ordering[:, :, None], axis=1)
        return moved_rows.reshape(HEADS, TOK_DEV // CLUSTER, CLUSTER, HEAD_DIM)
    scores = jnp.einsum('hbqd,hbkd->hbqk', clustered(query_rows), clustered(key_rows), precision=HIGHEST) * HEAD_DIM ** (-0.5)
    scores = low_back(scores)
    shifted = jnp.exp(scores - lax.optimization_barrier(jnp.max(scores, axis=-1, keepdims=True)))
    weights = low(shifted / lax.optimization_barrier(jnp.sum(shifted, axis=-1, keepdims=True)))
    mixed_rows = jnp.einsum('hbqk,hbkd->hbqd', weights, clustered(value_rows), precision=HIGHEST)
    mixed_rows = mixed_rows.reshape(HEADS, TOK_DEV, HEAD_DIM)
    head_index = jnp.arange(HEADS, dtype=jnp.int32)[:, None]
    placed = jnp.zeros_like(mixed_rows).at[head_index, ordering].set(mixed_rows)
    return placed.transpose(1, 0, 2).reshape(TOK_DEV, D)

def block(inputs, ordering, params):
    qkv_weight, qv_bias, out_weight, out_bias, norm1_gain, norm1_bias, up_weight, up_bias, down_weight, down_bias, norm2_gain, norm2_bias = params
    query_rows = round_both(matmul(inputs, qkv_weight[0]) + qv_bias[0])
    key_rows = round_both(matmul(inputs, qkv_weight[1]))
    value_rows = round_both(matmul(inputs, qkv_weight[2]) + qv_bias[1])
    context = round_both(attend(query_rows, key_rows, value_rows, ordering))
    attention = low_back(matmul(context, out_weight) + out_bias)
    normed = layer_norm(inputs + attention, norm1_gain, norm1_bias)
    hidden = low_back(matmul(low(normed), up_weight) + up_bias)
    active = low(jax.nn.gelu(hidden))
    feed_out = low_back(matmul(active, down_weight) + down_bias)
    return layer_norm(normed + feed_out, norm2_gain, norm2_bias)

def reference(hidden_in, cluster_order, qkv_weight, qv_bias, out_weight, out_bias, norm1_gain, norm1_bias, up_weight, up_bias, down_weight, down_bias, norm2_gain, norm2_bias, cotangent):
    inputs = hidden_in.astype(jnp.float32).reshape(N_ITEMS, TOK_DEV, D)
    orderings = jnp.transpose(cluster_order, (1, 0, 2))
    params = tuple((value.astype(jnp.float32) for value in (qkv_weight, qv_bias, out_weight, out_bias, norm1_gain, norm1_bias, up_weight, up_bias, down_weight, down_bias, norm2_gain, norm2_bias)))

    def forward(values, weights):
        step_fn = jax.checkpoint(lambda pair_in: block(pair_in[0], pair_in[1], weights))
        return lax.map(step_fn, (values, orderings))
    result, pull_back = jax.vjp(forward, inputs, params)
    input_grad, weight_grads = pull_back(cotangent.astype(jnp.float32).reshape(N_ITEMS, TOK_DEV, D))
    return (result.reshape(TOKENS, D).astype(jnp.bfloat16), input_grad.reshape(TOKENS, D).astype(jnp.bfloat16), weight_grads[0], weight_grads[1], weight_grads[2], weight_grads[3], weight_grads[4], weight_grads[5], weight_grads[6], weight_grads[7], weight_grads[8], weight_grads[9], weight_grads[10], weight_grads[11])
```

```python
import jax
import jax.numpy as jnp
from jax import lax
from jax.experimental import pallas as pl
from jax.experimental.pallas import tpu as pltpu
from jax.sharding import PartitionSpec as P

HEAD_DIM = 64
CLUSTER = 128
SCALE = HEAD_DIM**-0.5
EPSILON = 1e-05
VMEM_LIMIT = 60 * 1024 * 1024
BF16 = jnp.bfloat16
F32 = jnp.float32


def dot(left, right):
    return jnp.dot(left, right, preferred_element_type=F32)


def dot_nt(left, right):
    return lax.dot_general(left, right, (((1,), (1,)), ((), ())), preferred_element_type=F32)


def dot_tn(left, right):
    return lax.dot_general(left, right, (((0,), (0,)), ((), ())), preferred_element_type=F32)


def params_of(**more):
    return pltpu.CompilerParams(vmem_limit_bytes=VMEM_LIMIT, **more)


def cost(flops, bytes_accessed):
    return pl.CostEstimate(flops=int(flops), bytes_accessed=int(bytes_accessed), transcendentals=0)


def shape(dims, dtype):
    return jax.ShapeDtypeStruct(dims, dtype)


def whole(*dims):
    return pl.BlockSpec(dims, lambda *_: (0,) * len(dims), pipeline_mode=pl.Buffered(1))


def swapped(values):
    return lax.ppermute(values, "heads", [(0, 1), (1, 0)])


def traded(values, step, n_items):
    return lax.ppermute(values, "items", [(i, i ^ step) for i in range(n_items)])


def all_sum(values, n_items):
    step = 1
    while step < n_items:
        values = values + traded(values, step, n_items)
        step *= 2
    return values


def scattered(values, n_items, axis, order):
    item = lax.axis_index("items")
    dims = values.shape
    bits = list(range(n_items.bit_length() - 1))
    rows = dims[axis] // n_items
    values = values.reshape(dims[:axis] + (2,) * len(bits) + (rows,) + dims[axis + 1 :])
    left = bits[::-1]
    for bit in order(bits):
        place = axis + left.index(bit)
        mine = (item >> bit) & 1
        send = lax.dynamic_index_in_dim(values, 1 - mine, place, keepdims=False)
        keep = lax.dynamic_index_in_dim(values, mine, place, keepdims=False)
        values = keep + traded(send, 1 << bit, n_items)
        left.remove(bit)
    return values


def picked(columns, lanes):
    return jnp.where(columns == lanes, 1.0, 0.0).astype(BF16)


def attend_kernel(
    x_ref, w_ref, bias_ref, row_ref, col_ref, ctx_ref, sent_ref, moved_ref, probs_ref, sel_ref, cen_ref
):
    rows = x_ref.shape[0]
    step = 256
    halves = []
    for h in range(2):
        cut = slice(h * HEAD_DIM, (h + 1) * HEAD_DIM)
        weight = jnp.concatenate([w_ref[c][:, cut] for c in range(3)], axis=1)
        bias = jnp.concatenate(
            [bias_ref[0:1, cut], jnp.zeros((1, HEAD_DIM), F32), bias_ref[1:2, cut]], axis=1
        )
        lanes = lax.broadcasted_iota(jnp.int32, (step, rows), 1)
        for r in range(0, rows, step):
            sel_ref[r : r + step, :] = picked(col_ref[0, r : r + step, h : h + 1], lanes)
        qkv = (dot(x_ref[...], weight) + bias).astype(BF16)
        moved_ref[h] = dot(sel_ref[...], qkv).astype(BF16)
        for c in range(rows // CLUSTER):
            span = slice(c * CLUSTER, (c + 1) * CLUSTER)
            query = moved_ref[h, span, :HEAD_DIM]
            key = moved_ref[h, span, HEAD_DIM : 2 * HEAD_DIM]
            value = moved_ref[h, span, 2 * HEAD_DIM :]
            scores = dot_nt(query, key) * SCALE
            shifted = jnp.exp(scores - jnp.max(scores, axis=-1, keepdims=True))
            probs = shifted / jnp.sum(shifted, axis=-1, keepdims=True)
            probs_ref[h, c] = probs
            cen_ref[span, :] = dot(probs.astype(BF16), value).astype(BF16)
        for r in range(0, rows, step):
            subs = lax.broadcasted_iota(jnp.int32, (step, rows), 0) + r
            sel_ref[r : r + step, :] = picked(row_ref[0, h : h + 1, :], subs)
        halves.append(dot(sel_ref[...], cen_ref[...]))
    context = jnp.concatenate(halves, axis=1).astype(BF16)
    ctx_ref[...] = context
    sent_ref[...] = context.astype(F32)


def attend(x, weight, bias, order_rows, order_cols):
    rows, width = x.shape
    pairs = order_rows.shape[0]
    local = weight.shape[2]
    clusters = rows // CLUSTER
    return pl.pallas_call(
        attend_kernel,
        grid=(pairs,),
        in_specs=[
            whole(rows, width),
            pl.BlockSpec((3, width, 128), lambda p: (0, 0, p)),
            pl.BlockSpec((2, 128), lambda p: (0, p)),
            pl.BlockSpec((1, 2, rows), lambda p: (p, 0, 0)),
            pl.BlockSpec((1, rows, 2), lambda p: (p, 0, 0)),
        ],
        out_specs=[
            pl.BlockSpec((rows, 128), lambda p: (0, p)),
            pl.BlockSpec((rows, 128), lambda p: (0, p)),
            pl.BlockSpec((2, rows, 3 * HEAD_DIM), lambda p: (p, 0, 0)),
            pl.BlockSpec((2, clusters, CLUSTER, CLUSTER), lambda p: (p, 0, 0, 0)),
        ],
        out_shape=[
            shape((rows, local), BF16),
            shape((rows, local), F32),
            shape((2 * pairs, rows, 3 * HEAD_DIM), BF16),
            shape((2 * pairs, clusters, CLUSTER, CLUSTER), F32),
        ],
        scratch_shapes=[pltpu.VMEM((rows, rows), BF16), pltpu.VMEM((rows, HEAD_DIM), BF16)],
        compiler_params=params_of(),
        cost_estimate=cost(12e9, 12e6),
        name="attend",
    )(x, weight, bias, order_rows, order_cols)


def attend_back_kernel(
    xt_ref, da_ref, ow_ref, ctx_ref, w_ref, row_ref, col_ref, moved_ref, probs_ref,
    part_ref, grad_ref, bias_ref, sel_ref, cen_ref,
):
    rows = da_ref.shape[0]
    step = 256
    d_attn = da_ref[...]
    d_context = dot_nt(d_attn, ow_ref[...]).astype(BF16)
    grad_ref[3] = dot(ctx_ref[...].T, d_attn).T
    found = []
    for h in range(2):
        lanes = lax.broadcasted_iota(jnp.int32, (step, rows), 1)
        for r in range(0, rows, step):
            sel_ref[r : r + step, :] = picked(col_ref[0, r : r + step, h : h + 1], lanes)
        d_moved = dot(sel_ref[...], d_context[:, h * HEAD_DIM : (h + 1) * HEAD_DIM]).astype(BF16)
        for c in range(rows // CLUSTER):
            span = slice(c * CLUSTER, (c + 1) * CLUSTER)
            query = moved_ref[h, span, :HEAD_DIM]
            key = moved_ref[h, span, HEAD_DIM : 2 * HEAD_DIM]
            value = moved_ref[h, span, 2 * HEAD_DIM :]
            probs = probs_ref[h, c]
            above = d_moved[span, :]
            d_value = dot_tn(probs.astype(BF16), above)
            d_probs = dot_nt(above, value)
            inner = jnp.sum(probs * d_probs, axis=-1, keepdims=True)
            d_scores = (probs * (d_probs - inner)).astype(BF16)
            d_query = dot(d_scores, key) * SCALE
            d_key = dot_tn(d_scores, query) * SCALE
            cen_ref[span, :] = jnp.concatenate([d_query, d_key, d_value], axis=1).astype(BF16)
        for r in range(0, rows, step):
            subs = lax.broadcasted_iota(jnp.int32, (step, rows), 0) + r
            sel_ref[r : r + step, :] = picked(row_ref[0, h : h + 1, :], subs)
        found.append(dot(sel_ref[...], cen_ref[...]))
    d_qkv = jnp.concatenate(
        [f[:, c * HEAD_DIM : (c + 1) * HEAD_DIM] for c in range(3) for f in found], axis=1
    ).astype(BF16)
    sums = jnp.sum(d_qkv.astype(F32), axis=0, keepdims=True)
    bias_ref[0:1, :] = sums[:, :128]
    bias_ref[1:2, :] = sums[:, 256:]
    grads = dot(xt_ref[...], d_qkv)
    for c in range(3):
        grad_ref[c] = grads[:, c * 128 : (c + 1) * 128]
    part = dot_nt(d_qkv, jnp.concatenate([w_ref[c] for c in range(3)], axis=1))

    @pl.when(pl.program_id(0) == 0)
    def _():
        part_ref[...] = part

    @pl.when(pl.program_id(0) > 0)
    def _():
        part_ref[...] += part


def attend_back(xt, d_attn, out_weight, context, weight, order_rows, order_cols, moved, probs):
    width, rows = xt.shape
    pairs = order_rows.shape[0]
    local = weight.shape[2]
    clusters = rows // CLUSTER
    return pl.pallas_call(
        attend_back_kernel,
        grid=(pairs,),
        in_specs=[
            whole(width, rows),
            whole(rows, width),
            pl.BlockSpec((128, width), lambda p: (p, 0)),
            pl.BlockSpec((rows, 128), lambda p: (0, p)),
            pl.BlockSpec((3, width, 128), lambda p: (0, 0, p)),
            pl.BlockSpec((1, 2, rows), lambda p: (p, 0, 0)),
            pl.BlockSpec((1, rows, 2), lambda p: (p, 0, 0)),
            pl.BlockSpec((2, rows, 3 * HEAD_DIM), lambda p: (p, 0, 0)),
            pl.BlockSpec((2, clusters, CLUSTER, CLUSTER), lambda p: (p, 0, 0, 0)),
        ],
        out_specs=[
            pl.BlockSpec((rows, width), lambda p: (0, 0)),
            pl.BlockSpec((4, width, 128), lambda p: (0, 0, p)),
            pl.BlockSpec((2, 128), lambda p: (0, p)),
        ],
        out_shape=[
            shape((rows, width), F32),
            shape((4, width, local), F32),
            shape((2, local), F32),
        ],
        scratch_shapes=[pltpu.VMEM((rows, rows), BF16), pltpu.VMEM((rows, 3 * HEAD_DIM), BF16)],
        compiler_params=params_of(),
        cost_estimate=cost(20e9, 20e6),
        name="attend_back",
    )(xt, d_attn, out_weight, context, weight, order_rows, order_cols, moved, probs)


def gelu_both(hidden):
    scale = 0.7978845608028654
    square = hidden * hidden
    bent = jnp.tanh(hidden * (scale + (scale * 0.044715) * square))
    half = 0.5 + 0.5 * bent
    active = hidden * half
    slope = half + 0.5 * hidden * (1.0 - bent * bent) * (scale + (3 * scale * 0.044715) * square)
    return active.astype(BF16), slope.astype(BF16)


def normalized(values):
    centred = values - jnp.mean(values, axis=-1, keepdims=True)
    factor = lax.rsqrt(jnp.mean(centred * centred, axis=-1, keepdims=True) + EPSILON)
    return centred * factor, factor


def norm_back(grad, unit, factor):
    mean = jnp.mean(grad, axis=-1, keepdims=True)
    inner = jnp.mean(grad * unit, axis=-1, keepdims=True)
    return factor * (grad - mean - unit * inner)


def lead_kernel(
    x_ref, ctx_ref, far_ctx_ref, out_ref, far_out_ref, vec_ref, up_ref, up_bias_ref, down_ref,
    unit_ref, factor_ref, nb_ref, act_ref, slope_ref, feed_ref,
):
    attention = dot(ctx_ref[...], out_ref[...])
    attention += dot(far_ctx_ref[...].astype(BF16), far_out_ref[...].astype(BF16))
    unit, factor = normalized(x_ref[...].astype(F32) + attention + vec_ref[0:1, :])
    unit_ref[...] = unit
    factor_ref[...] = factor
    nb = (unit * vec_ref[1:2, :] + vec_ref[2:3, :]).astype(BF16)
    nb_ref[...] = nb
    active, slope = gelu_both(dot(nb, up_ref[...]) + up_bias_ref[...])
    act_ref[...] = active
    slope_ref[...] = slope
    feed_ref[...] = dot(active, down_ref[...])


def lead(x, context, far_context, out_weight, far_small, vectors, up, up_bias, down):
    rows, width = x.shape
    local, units = out_weight.shape[0], up.shape[1]
    tile = 256
    across = lambda cols: pl.BlockSpec((tile, cols), lambda i: (i, 0))
    return pl.pallas_call(
        lead_kernel,
        grid=(rows // tile,),
        in_specs=[
            across(width), across(local), across(local), whole(local, width), whole(local, width),
            whole(8, width), whole(width, units), whole(1, units), whole(units, width),
        ],
        out_specs=[
            across(width), across(1), across(width), across(units), across(units), across(width),
        ],
        out_shape=[
            shape((rows, width), F32), shape((rows, 1), F32), shape((rows, width), BF16),
            shape((rows, units), BF16), shape((rows, units), BF16), shape((rows, width), F32),
        ],
        compiler_params=params_of(),
        cost_estimate=cost(6e9, 20e6),
        name="lead",
    )(x, context, far_context, out_weight, far_small, vectors, up, up_bias, down)


def middle_kernel(
    unit_ref, factor_ref, feed_ref, slope_ref, cot_ref, vec_ref, far_ref, far_bias_ref, up_ref, down_ref,
    mixed_ref, d_feed_ref, d_hidden_ref, d_pre_ref, d_attn_ref, sums_ref, up_sums_ref, up_s, down_s,
):
    width, units = up_ref.shape
    first = pl.program_id(0) == 0

    @pl.when(first)
    def _():
        for i in range(units // width):
            up_s[:, i * width : (i + 1) * width] = far_ref[i * width : (i + 1) * width].astype(BF16)
        down_s[...] = far_ref[units:, :].astype(BF16)
        sums_ref[...] = jnp.zeros_like(sums_ref)
        up_sums_ref[...] = jnp.zeros_like(up_sums_ref)

    unit1 = unit_ref[...]
    normed = unit1 * vec_ref[1:2, :] + vec_ref[2:3, :]
    nb = normed.astype(BF16)
    far_bias = jnp.concatenate(
        [far_bias_ref[i : i + 1, :] for i in range(units // width)], axis=1
    )
    far_active, far_slope = gelu_both(dot(nb, up_s[...]) + far_bias)
    feed = feed_ref[...] + dot(far_active, down_s[...]) + vec_ref[3:4, :]
    unit2, factor2 = normalized(normed + feed)
    mixed_ref[...] = (unit2 * vec_ref[4:5, :] + vec_ref[5:6, :]).astype(BF16)
    grad = cot_ref[...].astype(F32)
    sums_ref[0:1, :] += jnp.sum(grad * unit2, axis=0, keepdims=True)
    sums_ref[1:2, :] += jnp.sum(grad, axis=0, keepdims=True)
    d_sum = norm_back(grad * vec_ref[4:5, :], unit2, factor2)
    d_feed = d_sum.astype(BF16)
    d_feed_ref[...] = d_feed
    sums_ref[2:3, :] += jnp.sum(d_feed.astype(F32), axis=0, keepdims=True)
    d_hidden = (dot_nt(d_feed, down_ref[...]) * slope_ref[...].astype(F32)).astype(BF16)
    d_hidden_ref[...] = d_hidden
    up_sums_ref[...] += jnp.sum(d_hidden.astype(F32), axis=0, keepdims=True)
    far_d_hidden = (dot_nt(d_feed, down_s[...]) * far_slope.astype(F32)).astype(BF16)
    d_normed = d_sum + dot_nt(d_hidden, up_ref[...]) + dot_nt(far_d_hidden, up_s[...])
    sums_ref[3:4, :] += jnp.sum(d_normed * unit1, axis=0, keepdims=True)
    sums_ref[4:5, :] += jnp.sum(d_normed, axis=0, keepdims=True)
    d_pre = norm_back(d_normed * vec_ref[1:2, :], unit1, factor_ref[...])
    d_pre_ref[...] = d_pre
    d_attn = d_pre.astype(BF16)
    d_attn_ref[...] = d_attn
    sums_ref[5:6, :] += jnp.sum(d_attn.astype(F32), axis=0, keepdims=True)


def middle(unit, factor, feed, slope, cotangent, vectors, far, far_small, up, down):
    rows, width = unit.shape
    units = up.shape[1]
    tile = 256
    across = lambda cols: pl.BlockSpec((tile, cols), lambda i: (i, 0))
    return pl.pallas_call(
        middle_kernel,
        grid=(rows // tile,),
        in_specs=[
            across(width), across(1), across(width), across(units), across(width), whole(8, width),
            whole(2 * units, width),
            pl.BlockSpec((8, width), lambda i: (far_small.shape[0] // 8 - 1, 0)),
            whole(width, units), whole(units, width),
        ],
        out_specs=[
            across(width), across(width), across(units), across(width), across(width),
            pl.BlockSpec((8, width), lambda i: (0, 0)), pl.BlockSpec((1, units), lambda i: (0, 0)),
        ],
        out_shape=[
            shape((rows, width), BF16), shape((rows, width), BF16), shape((rows, units), BF16),
            shape((rows, width), F32), shape((rows, width), BF16),
            shape((8, width), F32), shape((1, units), F32),
        ],
        scratch_shapes=[pltpu.VMEM((width, units), BF16), pltpu.VMEM((units, width), BF16)],
        compiler_params=params_of(),
        cost_estimate=cost(15e9, 30e6),
        name="middle",
    )(unit, factor, feed, slope, cotangent, vectors, far, far_small, up, down)


def feed_grads_kernel(nb_ref, d_feed_ref, act_ref, d_hidden_ref, up_ref, down_ref, nbt_s, d_feedt_s):
    @pl.when(pl.program_id(0) == 0)
    def _():
        nbt_s[...] = nb_ref[...].T
        d_feedt_s[...] = d_feed_ref[...].T

    down_ref[...] = dot(d_feedt_s[...], act_ref[...])
    up_ref[...] = dot(nbt_s[...], d_hidden_ref[...])


def feed_grads(nb, d_feed, active, d_hidden):
    rows, width = nb.shape
    units = active.shape[1]
    tile = 256
    along = lambda height: pl.BlockSpec((height, tile), lambda j: (0, j))
    return pl.pallas_call(
        feed_grads_kernel,
        grid=(units // tile,),
        in_specs=[whole(rows, width), whole(rows, width), along(rows), along(rows)],
        out_specs=[along(width), along(width)],
        out_shape=[shape((width, units), F32), shape((width, units), F32)],
        scratch_shapes=[pltpu.VMEM((width, rows), BF16), pltpu.VMEM((width, rows), BF16)],
        compiler_params=params_of(),
        cost_estimate=cost(5e9, 20e6),
        name="feed_grads",
    )(nb, d_feed, active, d_hidden)


def make_body(n_items):
    def body(
        hidden_in,
        cluster_order,
        qkv_weight,
        qv_bias,
        out_weight,
        out_bias,
        norm1_gain,
        norm1_bias,
        up_weight,
        up_bias,
        down_weight,
        down_bias,
        norm2_gain,
        norm2_bias,
        cotangent,
    ):
        rows, width = hidden_in.shape
        units = up_weight.shape[1]
        local = out_weight.shape[0]
        item = lax.axis_index("items")

        stacked = jnp.concatenate(
            [up_weight[:, i : i + width] for i in range(0, units, width)] + [down_weight], axis=0
        )
        piece_rows = stacked.shape[0] // n_items
        piece = lax.dynamic_slice_in_dim(stacked, item * piece_rows, piece_rows, 0)
        far = lax.all_gather(swapped(piece.astype(F32)), "items", axis=0, tiled=True)
        bias_rows = jnp.zeros((8 * width,), F32).at[:units].set(up_bias).reshape(8, width)
        far_small = swapped(jnp.concatenate([out_weight.astype(F32), bias_rows], axis=0))
        zero = jnp.zeros_like(out_bias)
        vectors = jnp.stack(
            [out_bias, norm1_gain, norm1_bias, down_bias, norm2_gain, norm2_bias, zero, zero]
        )

        ordering = cluster_order[:, 0, :]
        order_rows = ordering.reshape(-1, 2, rows)
        order_cols = jnp.transpose(order_rows, (0, 2, 1))
        context, sent, moved, probs = attend(
            hidden_in, qkv_weight, qv_bias, order_rows, order_cols
        )
        far_context = swapped(sent)
        unit, factor, nb, active, slope, feed = lead(
            hidden_in, context, far_context, out_weight, far_small, vectors, up_weight,
            up_bias.reshape(1, units), down_weight,
        )
        mixed, d_feed, d_hidden, d_pre, d_attn, sums, up_sums = middle(
            unit, factor, feed, slope, cotangent, vectors, far, far_small, up_weight, down_weight
        )
        grad_up, grad_down = feed_grads(nb, d_feed, active, d_hidden)
        in_order = lambda bits: bits
        turned = lambda bits: bits[:1] + bits[2:] + bits[1:2]
        summed_down = scattered(grad_down, n_items, 0, in_order)
        summed_up = scattered(grad_up, n_items, 0, turned)
        part, grad_rest, grad_qv = attend_back(
            hidden_in.T, d_attn, out_weight, context, qkv_weight, order_rows, order_cols, moved, probs
        )
        grad_inputs = d_pre + part + swapped(part)
        summed_rest = scattered(grad_rest, n_items, 1, in_order)

        parts = [sums.reshape(-1), up_sums.reshape(-1), grad_qv.reshape(-1)]
        sizes = [piece_of.shape[0] for piece_of in parts]
        total = sum(sizes)
        padded = -(-total // 1024) * 1024
        packed = jnp.concatenate(parts + [jnp.zeros((padded - total,), F32)])
        packed = all_sum(packed.reshape(8, padded // 8), n_items).reshape(-1)
        small = packed[: 8 * width].reshape(8, width)
        up_small = packed[sizes[0] : sizes[0] + units]
        qv_small = packed[sizes[0] + units : total].reshape(2, local)
        return (
            mixed,
            grad_inputs.astype(BF16),
            summed_rest[:3],
            qv_small,
            summed_rest[3].T,
            small[5],
            small[3],
            small[4],
            summed_up,
            up_small,
            summed_down.T,
            small[2],
            small[0],
            small[1],
        )

    return body


def solution(mesh):
    return jax.shard_map(
        make_body(mesh.shape["items"]),
        mesh=mesh,
        in_specs=(
            P("items", None),
            P("heads", "items", None),
            P(None, None, "heads"),
            P(None, "heads"),
            P("heads", None),
            P(),
            P(),
            P(),
            P(None, "heads"),
            P("heads"),
            P("heads", None),
            P(),
            P(),
            P(),
            P("items", None),
        ),
        out_specs=(
            P("items", None),
            P("items", None),
            P(None, "items", "heads"),
            P(None, "heads"),
            P("heads", "items"),
            P(),
            P(),
            P(),
            P("items", "heads"),
            P("heads"),
            P("heads", "items"),
            P(),
            P(),
            P(),
        ),
        check_vma=False,
    )
```

```python
import functools

import jax
import jax.numpy as jnp
from jax import lax
from jax.experimental import pallas as pl
from jax.experimental.pallas import tpu as pltpu
from jax.sharding import PartitionSpec as P

HEAD_DIM = 64
CLUSTER = 128
SCALE = HEAD_DIM**-0.5
EPSILON = 1e-05
ROW_TILE = 512
UNIT_TILE = 512
BF16 = jnp.bfloat16
F32 = jnp.float32


def dot(left, right):
    return jnp.dot(left, right, preferred_element_type=F32)


def dot_nt(left, right):
    return lax.dot_general(left, right, (((1,), (1,)), ((), ())), preferred_element_type=F32)


def dot_tn(left, right):
    return lax.dot_general(left, right, (((0,), (0,)), ((), ())), preferred_element_type=F32)


def dot_tt(left, right):
    return lax.dot_general(left, right, (((0,), (1,)), ((), ())), preferred_element_type=F32)


def params_of(mib):
    return pltpu.CompilerParams(vmem_limit_bytes=mib * 1024 * 1024)


def cost(flops, bytes_accessed):
    return pl.CostEstimate(flops=int(flops) // 1000, bytes_accessed=int(bytes_accessed) // 1000, transcendentals=0)


def shape(dims, dtype):
    return jax.ShapeDtypeStruct(dims, dtype)


def whole(*dims):
    return pl.BlockSpec(dims, lambda *_: (0,) * len(dims), pipeline_mode=pl.Buffered(1))


def swapped(values):
    return lax.ppermute(values, "heads", [(0, 1), (1, 0)])


def traded(values, step, n_items):
    return lax.ppermute(values, "items", [(i, i ^ step) for i in range(n_items)])


def all_sum(values, n_items):
    step = 1
    while step < n_items:
        values = values + traded(values, step, n_items)
        step *= 2
    return values


def scattered(values, n_items, axis):
    item = lax.axis_index("items")
    size = n_items
    for bit in range(n_items.bit_length() - 1):
        dims = values.shape
        size //= 2
        halves = values.reshape(dims[:axis] + (size, 2, dims[axis] // (2 * size)) + dims[axis + 1 :])
        mine = (item >> bit) & 1
        send = lax.dynamic_index_in_dim(halves, 1 - mine, axis + 1, keepdims=False)
        keep = lax.dynamic_index_in_dim(halves, mine, axis + 1, keepdims=False)
        values = keep + traded(send, 1 << bit, n_items)
        values = values.reshape(dims[:axis] + (-1,) + dims[axis + 1 :])
    return values


class Halving:
    def __init__(self, keep, send, order, n_items, extra=None):
        self.values, self.order, self.n_items = keep, list(order), n_items
        self.send, self.extra, self.bit = send, extra, 0

    def trade(self):
        step = 1 << self.bit
        if self.extra is not None and self.bit > 0:
            cols = self.send.shape[-1]
            rows = self.send.size // cols
            both = jnp.concatenate([self.send.reshape(rows, cols), self.extra.reshape(-1, cols)])
            self.send = both
            got = traded(both, step, self.n_items)
            self.got, self.more = got[:rows].reshape(self.values.shape), got[rows:]
        else:
            self.got = traded(self.send, step, self.n_items)
            if self.extra is not None:
                self.more = traded(self.extra, step, self.n_items)
        return self

    def add(self, *before):
        total = self.values + after(self.got, *before)
        if self.extra is not None:
            self.extra = self.extra + self.more.reshape(self.extra.shape)
        if not self.order:
            self.values = total.reshape(total.shape[1:])
            return self.values
        self.bit = self.order.pop(0)
        halves = total.reshape((2, total.shape[0] // 2) + total.shape[1:])
        mine = (lax.axis_index("items") >> self.bit) & 1
        self.send = lax.dynamic_index_in_dim(halves, 1 - mine, 0, keepdims=False)
        self.values = lax.dynamic_index_in_dim(halves, mine, 0, keepdims=False)
        return self.send


class Gather:
    def __init__(self, values, slot, n_items):
        self.values, self.slots, self.n_items = values, [slot], n_items

    def trade(self, step):
        self.got = traded(self.values, step, self.n_items)
        self.slots = self.slots + [slot ^ step for slot in self.slots]
        return self.values

    def join(self, *before):
        self.values = jnp.concatenate([self.values, after(self.got, *before)], axis=0)

    def place(self, *before):
        return placed(self.slots, [self.values, after(self.got, *before)])


def after(values, *others):
    return lax.optimization_barrier((values,) + others)[0]


def placed_kernel(slots_ref, *refs):
    *part_refs, out_ref = refs
    index = 0
    for part_ref in part_refs:
        count, rows, _ = part_ref.shape
        for k in range(count):
            start = pl.multiple_of(slots_ref[index] * rows, rows)
            out_ref[pl.ds(start, rows), :] = part_ref[k].astype(BF16)
            index += 1


def placed(slots, parts):
    rows, cols = parts[0].shape[1:]
    total = sum(part.shape[0] for part in parts) * rows
    whole_array = pl.BlockSpec(memory_space=pltpu.VMEM)
    return pl.pallas_call(
        placed_kernel,
        in_specs=[pl.BlockSpec(memory_space=pltpu.SMEM)] + [whole_array] * len(parts),
        out_specs=whole_array,
        out_shape=shape((total, cols), BF16),
        compiler_params=params_of(8),
        cost_estimate=cost(1e6, 6 * total * cols),
        name="placed",
    )(jnp.stack(slots).astype(jnp.int32), *parts)


def selector(row_ref, h, sel_ref, slot):
    rows = sel_ref.shape[1]
    step = 256
    for r in range(0, rows, step):
        subs = lax.broadcasted_iota(jnp.int32, (step, rows), 0) + r
        found = jnp.where(row_ref[0, h : h + 1, :] == subs, 1.0, 0.0)
        sel_ref[slot, r : r + step, :] = found.astype(BF16)


def spans_of(rows):
    return [slice(c, c + CLUSTER) for c in range(0, rows, CLUSTER)]


def attend_kernel(xt_ref, w_ref, bias_ref, row_ref, ctx_ref, moved_ref, probs_ref, sel_ref):
    rows = xt_ref.shape[1]
    spans = spans_of(rows)
    for h in range(2):
        selector(row_ref, h, sel_ref, h)
    weight = jnp.concatenate([w_ref[c] for c in range(3)], axis=1)
    flat = dot_tn(weight, xt_ref[...])
    parts = [flat[:128] + bias_ref[:, 0:1], flat[128:256], flat[256:] + bias_ref[:, 1:2]]
    parts = [part.astype(BF16) for part in parts]
    for h in range(2):
        cut = slice(h * HEAD_DIM, (h + 1) * HEAD_DIM)
        qkv = jnp.concatenate([part[cut] for part in parts], axis=0)
        moved = dot(qkv, sel_ref[h]).astype(BF16)
        moved_ref[h] = moved
        query, key, value = moved[:HEAD_DIM], moved[HEAD_DIM : 2 * HEAD_DIM], moved[2 * HEAD_DIM :]
        scores = jnp.concatenate([dot_tn(query[:, s], key[:, s]) for s in spans], axis=0) * SCALE
        shifted = jnp.exp(scores - jnp.max(scores, axis=-1, keepdims=True))
        probs = shifted / jnp.sum(shifted, axis=-1, keepdims=True)
        probs_ref[h] = probs
        probs_b = probs.astype(BF16)
        mixed = jnp.concatenate([dot_nt(value[:, s], probs_b[s]) for s in spans], axis=1)
        context = dot_nt(mixed.astype(BF16), sel_ref[h])
        ctx_ref[cut, :] = context.astype(BF16)


def attend(xt, weight, bias_cols, order_rows):
    width, rows = xt.shape
    pairs = order_rows.shape[0]
    local = weight.shape[2]
    return pl.pallas_call(
        attend_kernel,
        grid=(pairs,),
        in_specs=[
            whole(width, rows),
            pl.BlockSpec((3, width, 128), lambda p: (0, 0, p)),
            pl.BlockSpec((128, 2), lambda p: (p, 0)),
            pl.BlockSpec((1, 2, rows), lambda p: (p, 0, 0)),
        ],
        out_specs=[
            pl.BlockSpec((128, rows), lambda p: (p, 0)),
            pl.BlockSpec((2, 3 * HEAD_DIM, rows), lambda p: (p, 0, 0)),
            pl.BlockSpec((2, rows, CLUSTER), lambda p: (p, 0, 0)),
        ],
        out_shape=[
            shape((local, rows), BF16),
            shape((2 * pairs, 3 * HEAD_DIM, rows), BF16),
            shape((2 * pairs, rows, CLUSTER), F32),
        ],
        scratch_shapes=[pltpu.VMEM((2, rows, rows), BF16)],
        compiler_params=params_of(20),
        cost_estimate=cost(12e9, 12e6),
        name="attend",
    )(xt, weight, bias_cols, order_rows)


def block_place(j, order):
    place = 0
    for bit in order:
        place = 2 * place + ((j >> bit) & 1)
    return place


def write_halves(values, keep_ref, send_ref, mine, order, at):
    blocks = 2 ** (len(order) + 1)
    rows = values.shape[0] // blocks
    for j in range(0, blocks, 2):
        even, odd = values[j * rows : (j + 1) * rows], values[(j + 1) * rows : (j + 2) * rows]
        place = (block_place(j, order),) + at
        keep_ref[place] = jnp.where(mine == 0, even, odd)
        send_ref[place] = jnp.where(mine == 0, odd, even)


def attend_back_kernel(order, has_part, *refs):
    if order:
        core_ref, *refs = refs
    xt_ref, da_ref, ow_ref, ctx_ref, w_ref, row_ref, moved_ref, probs_ref, *refs = refs
    if has_part:
        old_ref, *refs = refs
        refs = refs[2 if order else 1 :]
        refs = refs[1:]
    part_ref, *grad_refs, bias_ref, sel_ref = refs
    rows = da_ref.shape[0]
    spans = spans_of(rows)
    for h in range(2):
        selector(row_ref, h, sel_ref, h)
    d_attn = da_ref[...]
    d_context = dot_nt(ow_ref[...], d_attn).astype(BF16)
    d_out = dot_tt(d_attn, ctx_ref[...])
    found = []
    for h in range(2):
        d_moved = dot(d_context[h * HEAD_DIM : (h + 1) * HEAD_DIM], sel_ref[h]).astype(BF16)
        moved = moved_ref[h]
        query, key, value = moved[:HEAD_DIM], moved[HEAD_DIM : 2 * HEAD_DIM], moved[2 * HEAD_DIM :]
        probs = probs_ref[h]
        probs_b = probs.astype(BF16)
        d_value = jnp.concatenate([dot(d_moved[:, s], probs_b[s]) for s in spans], axis=1)
        d_probs = jnp.concatenate([dot_tn(d_moved[:, s], value[:, s]) for s in spans], axis=0)
        inner = jnp.sum(probs * d_probs, axis=-1, keepdims=True)
        d_scores = (probs * (d_probs - inner)).astype(BF16)
        d_query = jnp.concatenate([dot_nt(key[:, s], d_scores[s]) for s in spans], axis=1) * SCALE
        d_key = jnp.concatenate([dot(query[:, s], d_scores[s]) for s in spans], axis=1) * SCALE
        three = jnp.concatenate([d_query, d_key, d_value], axis=0).astype(BF16)
        found.append(dot_nt(three, sel_ref[h]).astype(BF16))
    d_qkv = jnp.concatenate(
        [f[c * HEAD_DIM : (c + 1) * HEAD_DIM] for c in range(3) for f in found], axis=0
    )
    sums = dot_nt(jnp.ones((8, rows), BF16), d_qkv)
    bias_ref[0:1, :] = sums[0:1, :128]
    bias_ref[1:2, :] = sums[0:1, 256:]
    grads = dot_nt(xt_ref[...], d_qkv)
    for c in range(4):
        values = grads[:, c * 128 : (c + 1) * 128] if c < 3 else d_out
        if order:
            write_halves(values, *grad_refs, core_ref[0], order, (c,))
        else:
            grad_refs[0][c] = values
    part = dot_tt(d_qkv, jnp.concatenate([w_ref[c] for c in range(3)], axis=1))
    part_ref[...] = old_ref[...] + part if has_part else part


def attend_back(pair, order, core, xt, d_attn, out_weight, context, weight, order_rows, moved, probs, old):
    width, rows = xt.shape
    local = weight.shape[2]
    one = lambda dims, place: pl.BlockSpec(dims, lambda i: place)
    if order:
        blocks = 2 ** len(order)
        height = width // (2 * blocks)
        grad_specs = [one((blocks, 4, height, 128), (0, 0, 0, pair))] * 2
        grad_shapes = [shape((blocks, 4, height, local), F32)] * 2
        first, first_specs = [core], [pl.BlockSpec(memory_space=pltpu.SMEM)]
    else:
        grad_specs = [one((4, width, 128), (0, 0, pair))]
        grad_shapes = [shape((4, width, local), F32)]
        first, first_specs = [], []
    count = len(first) + 8
    olds = list(old) if old else []
    aliases = {count + k: k for k in range(len(olds))}
    anywhere = pl.BlockSpec(memory_space=pl.ANY)
    return pl.pallas_call(
        functools.partial(attend_back_kernel, order, bool(olds)),
        grid=(1,),
        in_specs=first_specs + [
            whole(width, rows),
            whole(rows, width),
            one((128, width), (pair, 0)),
            one((128, rows), (pair, 0)),
            one((3, width, 128), (0, 0, pair)),
            one((1, 2, rows), (pair, 0, 0)),
            one((2, 3 * HEAD_DIM, rows), (pair, 0, 0)),
            one((2, rows, CLUSTER), (pair, 0, 0)),
        ] + ([whole(rows, width)] + [anywhere] * (len(olds) - 1) if olds else []),
        out_specs=[whole(rows, width)] + grad_specs + [one((2, 128), (0, pair))],
        out_shape=[shape((rows, width), F32)] + grad_shapes + [shape((2, local), F32)],
        input_output_aliases=aliases,
        scratch_shapes=[pltpu.VMEM((2, rows, rows), BF16)],
        compiler_params=params_of(24),
        cost_estimate=cost(7e9, 7e6),
        name="attend_back",
    )(*first, xt, d_attn, out_weight, context, weight, order_rows, moved, probs, *olds)


def gelu_both(hidden):
    scale = 0.7978845608028654
    square = hidden * hidden
    bent = jnp.tanh(hidden * (scale + (scale * 0.044715) * square))
    half = 0.5 + 0.5 * bent
    active = hidden * half
    slope = half + 0.5 * hidden * (1.0 - bent * bent) * (scale + (3 * scale * 0.044715) * square)
    return active.astype(BF16), slope.astype(BF16)


def normalized(values):
    centred = values - jnp.mean(values, axis=-1, keepdims=True)
    factor = lax.rsqrt(jnp.mean(centred * centred, axis=-1, keepdims=True) + EPSILON)
    return centred * factor, factor


def norm_back(grad, unit, factor):
    mean = jnp.mean(grad, axis=-1, keepdims=True)
    inner = jnp.mean(grad * unit, axis=-1, keepdims=True)
    return factor * (grad - mean - unit * inner)


def unit_cuts(units):
    return [slice(u, u + UNIT_TILE) for u in range(0, units, UNIT_TILE)]


def lead_kernel(
    x_ref, ctx_ref, far0_ref, far1_ref, far2_ref, out_ref, far_out_ref, vec_ref, up_ref, up_bias_ref, down_ref,
    unit_ref, factor_ref, nb_ref, act_ref, slope_ref, feed_ref,
):
    attention = dot_tn(ctx_ref[...], out_ref[...])
    far_ctx = jnp.concatenate([ref[...].astype(BF16) for ref in (far0_ref, far1_ref, far2_ref)], axis=0)
    attention += dot_tn(far_ctx, far_out_ref[...])
    unit, factor = normalized(x_ref[...].astype(F32) + attention + vec_ref[0:1, :])
    unit_ref[...] = unit
    factor_ref[...] = factor
    nb = (unit * vec_ref[1:2, :] + vec_ref[2:3, :]).astype(BF16)
    nb_ref[...] = nb
    feed = None
    for cut in unit_cuts(up_ref.shape[1]):
        active, slope = gelu_both(dot(nb, up_ref[:, cut]) + up_bias_ref[:, cut])
        act_ref[:, cut] = active
        slope_ref[:, cut] = slope
        term = dot(active, down_ref[cut, :])
        feed = term if feed is None else feed + term
    feed_ref[...] = feed


def lead(x, context, far_context, out_weight, far_out, vectors, up, up_bias, down):
    rows, width = x.shape
    local, units = out_weight.shape[0], up.shape[1]
    tile = ROW_TILE
    across = lambda cols: pl.BlockSpec((tile, cols), lambda i: (i, 0))
    along = lambda height: pl.BlockSpec((height, tile), lambda i: (0, i))
    return pl.pallas_call(
        lead_kernel,
        grid=(rows // tile,),
        in_specs=[
            across(width), along(local), *[along(part.shape[0]) for part in far_context], whole(local, width), whole(local, width),
            whole(8, width), whole(width, units), whole(1, units), whole(units, width),
        ],
        out_specs=[
            across(width), across(1), across(width), across(units), across(units), across(width),
        ],
        out_shape=[
            shape((rows, width), F32), shape((rows, 1), F32), shape((rows, width), BF16),
            shape((rows, units), BF16), shape((rows, units), BF16), shape((rows, width), F32),
        ],
        compiler_params=params_of(20),
        cost_estimate=cost(6e9, 20e6),
        name="lead",
    )(x, context, *far_context, out_weight, far_out, vectors, up, up_bias, down)


def middle_kernel(
    unit_ref, factor_ref, feed_ref, slope_ref, cot_ref, vec_ref, far_up_ref, far_down_ref, far_bias_ref, up_ref, down_ref,
    mixed_ref, d_feed_ref, d_hidden_ref, d_pre_ref, d_attn_ref, sums_ref, up_sums_ref,
):
    width, units = up_ref.shape
    first = pl.program_id(0) == 0

    @pl.when(first)
    def _():
        sums_ref[...] = jnp.zeros_like(sums_ref)
        up_sums_ref[...] = jnp.zeros_like(up_sums_ref)

    unit1 = unit_ref[...]
    normed = unit1 * vec_ref[1:2, :] + vec_ref[2:3, :]
    nb = normed.astype(BF16)
    far_bias = jnp.concatenate(
        [far_bias_ref[i : i + 1, :] for i in range(units // width)], axis=1
    )
    feed = feed_ref[...] + vec_ref[3:4, :]
    far_slopes = []
    for cut in unit_cuts(units):
        far_active, far_slope = gelu_both(dot(nb, far_up_ref[:, cut]) + far_bias[:, cut])
        far_slopes.append(far_slope)
        feed = feed + dot(far_active, far_down_ref[cut, :])
    unit2, factor2 = normalized(normed + feed)
    mixed_ref[...] = (unit2 * vec_ref[4:5, :] + vec_ref[5:6, :]).astype(BF16)
    grad = cot_ref[...].astype(F32)
    sums_ref[0:1, :] += jnp.sum(grad * unit2, axis=0, keepdims=True)
    sums_ref[1:2, :] += jnp.sum(grad, axis=0, keepdims=True)
    d_sum = norm_back(grad * vec_ref[4:5, :], unit2, factor2)
    d_feed = d_sum.astype(BF16)
    d_feed_ref[...] = d_feed
    sums_ref[2:3, :] += jnp.sum(d_feed.astype(F32), axis=0, keepdims=True)
    d_normed = d_sum
    for cut, far_slope in zip(unit_cuts(units), far_slopes):
        d_active = dot_nt(d_feed, down_ref[cut, :])
        d_hidden = (d_active * slope_ref[:, cut].astype(F32)).astype(BF16)
        d_hidden_ref[:, cut] = d_hidden
        up_sums_ref[:, cut] += jnp.sum(d_hidden.astype(F32), axis=0, keepdims=True)
        d_normed = d_normed + dot_nt(d_hidden, up_ref[:, cut])
        far_d_active = dot_nt(d_feed, far_down_ref[cut, :])
        far_d_hidden = (far_d_active * far_slope.astype(F32)).astype(BF16)
        d_normed = d_normed + dot_nt(far_d_hidden, far_up_ref[:, cut])
    sums_ref[3:4, :] += jnp.sum(d_normed * unit1, axis=0, keepdims=True)
    sums_ref[4:5, :] += jnp.sum(d_normed, axis=0, keepdims=True)
    d_pre = norm_back(d_normed * vec_ref[1:2, :], unit1, factor_ref[...])
    d_pre_ref[...] = d_pre
    d_attn = d_pre.astype(BF16)
    d_attn_ref[...] = d_attn
    sums_ref[5:6, :] += jnp.sum(d_attn.astype(F32), axis=0, keepdims=True)


def middle(unit, factor, feed, slope, cotangent, vectors, far_up, far_down, far_small, up, down):
    rows, width = unit.shape
    units = up.shape[1]
    tile = ROW_TILE
    across = lambda cols: pl.BlockSpec((tile, cols), lambda i: (i, 0))
    return pl.pallas_call(
        middle_kernel,
        grid=(rows // tile,),
        in_specs=[
            across(width), across(1), across(width), across(units), across(width), whole(8, width),
            whole(width, units), whole(units, width),
            pl.BlockSpec((8, width), lambda i: (far_small.shape[0] // 8 - 1, 0)),
            whole(width, units), whole(units, width),
        ],
        out_specs=[
            across(width), across(width), across(units), across(width), across(width),
            pl.BlockSpec((8, width), lambda i: (0, 0)), pl.BlockSpec((1, units), lambda i: (0, 0)),
        ],
        out_shape=[
            shape((rows, width), BF16), shape((rows, width), BF16), shape((rows, units), BF16),
            shape((rows, width), F32), shape((rows, width), BF16),
            shape((8, width), F32), shape((1, units), F32),
        ],
        compiler_params=params_of(28),
        cost_estimate=cost(15e9, 30e6),
        name="middle",
    )(unit, factor, feed, slope, cotangent, vectors, far_up, far_down, far_small, up, down)


def feed_grads_kernel(orders, *refs):
    if orders:
        core_ref, *refs = refs
    nb_ref, d_feed_ref, act_ref, d_hidden_ref, *out_refs = refs
    values = dot_tn(d_feed_ref[...], act_ref[...])
    if orders:
        write_halves(values, *out_refs[:2], core_ref[0], orders[0], ())
    else:
        out_refs[0][...] = values
    values = dot_tn(nb_ref[...], d_hidden_ref[...])
    if orders:
        write_halves(values, *out_refs[2:], core_ref[0], orders[1], ())
    else:
        out_refs[1][...] = values


def feed_grads(orders, core, nb, d_feed, active, d_hidden):
    rows, width = nb.shape
    units = active.shape[1]
    tile = UNIT_TILE
    along = lambda height: pl.BlockSpec((height, tile), lambda j: (0, j))
    if orders:
        blocks = 2 ** len(orders[0])
        height = width // (2 * blocks)
        out_specs = [pl.BlockSpec((blocks, height, tile), lambda j: (0, 0, j))] * 4
        out_shape = [shape((blocks, height, units), F32)] * 4
        first, first_specs = [core], [pl.BlockSpec(memory_space=pltpu.SMEM)]
    else:
        out_specs, out_shape = [along(width)] * 2, [shape((width, units), F32)] * 2
        first, first_specs = [], []
    return pl.pallas_call(
        functools.partial(feed_grads_kernel, orders),
        grid=(units // tile,),
        in_specs=first_specs + [whole(rows, width), whole(rows, width), along(rows), along(rows)],
        out_specs=out_specs,
        out_shape=out_shape,
        compiler_params=params_of(20),
        cost_estimate=cost(5e9, 20e6),
        name="feed_grads",
    )(*first, nb, d_feed, active, d_hidden)


def make_body(n_items):
    def body(
        hidden_in,
        cluster_order,
        qkv_weight,
        qv_bias,
        out_weight,
        out_bias,
        norm1_gain,
        norm1_bias,
        up_weight,
        up_bias,
        down_weight,
        down_bias,
        norm2_gain,
        norm2_bias,
        cotangent,
    ):
        rows, width = hidden_in.shape
        units = up_weight.shape[1]
        local = out_weight.shape[0]
        item = lax.axis_index("items")
        core = item & 1
        group = 8
        place = item % group

        def piece(values):
            count = values.shape[0] // group
            return lax.dynamic_slice_in_dim(values, place * count, count, 0).astype(F32)[None]

        up_piece = piece(up_weight)
        down_piece = piece(after(down_weight, up_piece))
        half = local // 2
        out_piece = lax.dynamic_slice_in_dim(after(out_weight, down_piece), core * half, half, 0)
        bias_rows = jnp.zeros((8 * width,), F32).at[:units].set(up_bias).reshape(8, width)
        small_piece = jnp.concatenate([out_piece.astype(F32), bias_rows], axis=0)
        far_up = swapped(up_piece)
        far_down = swapped(down_piece)
        far_small = swapped(small_piece)
        zero = jnp.zeros_like(out_bias)
        vectors = jnp.concatenate(
            [out_bias, norm1_gain, norm1_bias, down_bias, norm2_gain, norm2_bias, zero, zero]
        ).reshape(8, width)
        turned_in = after(hidden_in, up_piece, down_piece, small_piece).T

        ordering = cluster_order[:, 0, :]
        order_rows = ordering.reshape(-1, 2, rows)
        context, moved, probs = attend(turned_in, qkv_weight, qv_bias.T, order_rows)
        pairs = order_rows.shape[0]
        far_context = [
            swapped(context[p * 128 : (p + 1) * 128].astype(F32)) for p in range(pairs)
        ]

        pair_up = Gather(after(far_up, context), place, n_items)
        last = pair_up.trade(4)
        pair_down = Gather(after(far_down, last), place, n_items)
        last = pair_down.trade(4)
        far_context[0] = after(far_context[0], last)
        pair_up.join(far_context[0])
        last = pair_up.trade(2)
        far_context[1] = after(far_context[1], last)
        pair_down.join(far_context[1])
        last = pair_down.trade(2)
        far_half = after(far_small, last)[None, :half]
        other_half = traded(far_half, 1, n_items)
        far_out = placed([core, 1 - core], [far_half, other_half])
        far_context[2] = after(far_context[2], far_out)
        unit, factor, nb, active, slope, feed = lead(
            hidden_in, context, far_context, out_weight, far_out, vectors, up_weight,
            up_bias.reshape(1, units), down_weight,
        )
        pair_up.join(feed)
        last = pair_up.trade(1)
        pair_down.join(last)
        last = pair_down.trade(1)
        far_up = pair_up.place(last)
        far_down = pair_down.place(far_up)
        mixed, d_feed, d_hidden, d_pre, d_attn, sums, up_sums = middle(
            unit, factor, feed, slope, cotangent, vectors, far_up, far_down, far_small, up_weight,
            down_weight,
        )

        split = width % (8 * n_items) == 0
        bits = tuple(range(1, n_items.bit_length() - 1))
        late_y = bits[1:] + bits[:1]
        which = core.astype(jnp.int32).reshape(1)
        grads_of = lambda d_feed: feed_grads(
            (late_y, bits) if split else None, which, nb, d_feed, active, d_hidden
        )
        back = lambda pair, d_attn, old: attend_back(
            pair, bits if split else None, which, turned_in, d_attn, out_weight, context, qkv_weight,
            order_rows, moved, probs, old,
        )

        def packed_of(grad_qv):
            return jnp.concatenate(
                [sums, up_sums.reshape(-1, width), grad_qv.reshape(-1, width)], axis=0
            )

        old = None
        for pair in range(pairs):
            old = back(pair, d_attn, old)
        if split:
            part, keep, send, grad_qv = old
            far_part = swapped(part)
            rest_sum = Halving(keep, send, bits, n_items, packed_of(grad_qv)).trade()
            grads = grads_of(after(d_feed, part))
            down_sum = Halving(*grads[:2], late_y, n_items).trade()
            up_sum = Halving(*grads[2:], bits, n_items).trade()
            last = rest_sum.add(*grads)
            rest_sum.trade()
            last = down_sum.add(rest_sum.send)
            down_sum.trade()
            last = up_sum.add(last)
            up_sum.trade()
            last = rest_sum.add(last)
            rest_sum.trade()
            last = down_sum.add(rest_sum.send)
            down_sum.trade()
            last = rest_sum.add(last)
            rest_sum.trade()
            last = up_sum.add(rest_sum.send)
            up_sum.trade()
            last = summed_rest = rest_sum.add(last)
            grad_inputs = (d_pre + part + after(far_part, last)).astype(BF16)
            last = down_sum.add(grad_inputs)
            down_sum.trade()
            last = up_sum.add(last)
            up_sum.trade()
            summed_down = down_sum.add(last)
            summed_up = up_sum.add(summed_down)
            packed = rest_sum.extra
        else:
            part, grad_rest, grad_qv = old
            grads = grads_of(d_feed)
            grad_inputs = (d_pre + part + swapped(part)).astype(BF16)
            summed_down = scattered(grads[0], n_items, 0)
            summed_up = scattered(grads[1], n_items, 0)
            summed_rest = scattered(grad_rest, n_items, 1)
            packed = all_sum(packed_of(grad_qv), n_items)
        small = packed[:8]
        up_small = packed[8 : 8 + units // width].reshape(units)
        qv_small = packed[8 + units // width :].reshape(2, local)
        return (
            mixed,
            grad_inputs,
            summed_rest[:3],
            qv_small,
            summed_rest[3].T,
            small[5],
            small[3],
            small[4],
            summed_up,
            up_small,
            summed_down.T,
            small[2],
            small[0],
            small[1],
        )

    return body


def solution(mesh):
    return jax.shard_map(
        make_body(mesh.shape["items"]),
        mesh=mesh,
        in_specs=(
            P("items", None),
            P("heads", "items", None),
            P(None, None, "heads"),
            P(None, "heads"),
            P("heads", None),
            P(),
            P(),
            P(),
            P(None, "heads"),
            P("heads"),
            P("heads", None),
            P(),
            P(),
            P(),
            P("items", None),
        ),
        out_specs=(
            P("items", None),
            P("items", None),
            P(None, "items", "heads"),
            P(None, "heads"),
            P("heads", "items"),
            P(),
            P(),
            P(),
            P("items", "heads"),
            P("heads"),
            P("heads", "items"),
            P(),
            P(),
            P(),
        ),
        check_vma=False,
    )
```

```python
import functools

import jax
import jax.numpy as jnp
from jax import lax
from jax.experimental import pallas as pl
from jax.experimental.pallas import tpu as pltpu
from jax.sharding import PartitionSpec as P

HEAD_DIM = 64
CLUSTER = 128
SCALE = HEAD_DIM**-0.5
EPSILON = 1e-05
ROW_TILE = 512
LAG = 1
GRAD_TILE = 512
UNIT_TILE = 768
BF16 = jnp.bfloat16
F32 = jnp.float32


def dot(left, right):
    return jnp.dot(left, right, preferred_element_type=F32)


def dot_nt(left, right):
    return lax.dot_general(left, right, (((1,), (1,)), ((), ())), preferred_element_type=F32)


def dot_tn(left, right):
    return lax.dot_general(left, right, (((0,), (0,)), ((), ())), preferred_element_type=F32)


def dot_tt(left, right):
    return lax.dot_general(left, right, (((0,), (1,)), ((), ())), preferred_element_type=F32)


def params_of(mib):
    return pltpu.CompilerParams(vmem_limit_bytes=mib * 1024 * 1024)


def cost(flops, bytes_accessed):
    return pl.CostEstimate(flops=int(flops) // 1000, bytes_accessed=int(bytes_accessed) // 1000, transcendentals=0)


def shape(dims, dtype):
    return jax.ShapeDtypeStruct(dims, dtype)


def whole(*dims):
    return pl.BlockSpec(dims, lambda *_: (0,) * len(dims), pipeline_mode=pl.Buffered(1))


def swapped(values):
    return lax.ppermute(values, "heads", [(0, 1), (1, 0)])


def traded(values, step, n_items):
    return lax.ppermute(values, "items", [(i, i ^ step) for i in range(n_items)])


def all_sum(values, n_items):
    step = 1
    while step < n_items:
        values = values + traded(values, step, n_items)
        step *= 2
    return values


def scattered(values, n_items, axis):
    item = lax.axis_index("items")
    size = n_items
    for bit in range(n_items.bit_length() - 1):
        dims = values.shape
        size //= 2
        halves = values.reshape(dims[:axis] + (size, 2, dims[axis] // (2 * size)) + dims[axis + 1 :])
        mine = (item >> bit) & 1
        send = lax.dynamic_index_in_dim(halves, 1 - mine, axis + 1, keepdims=False)
        keep = lax.dynamic_index_in_dim(halves, mine, axis + 1, keepdims=False)
        values = keep + traded(send, 1 << bit, n_items)
        values = values.reshape(dims[:axis] + (-1,) + dims[axis + 1 :])
    return values


class Halving:
    def __init__(self, keep, send, order, n_items):
        self.terms, self.order, self.n_items = [keep], list(order), n_items
        self.send, self.extra, self.bit = send, None, 0

    def trade(self):
        self.got = traded(self.send, 1 << self.bit, self.n_items)
        if self.extra is not None:
            self.more = traded(self.extra, 1 << self.bit, self.n_items)
        return self

    def add(self):
        terms = self.terms + [self.got]
        if self.extra is not None:
            self.extra = self.extra + self.more
        if not self.order:
            return sum(term.reshape(term.shape[1:]) for term in terms)
        self.bit = self.order.pop(0)
        mine = (lax.axis_index("items") >> self.bit) & 1
        terms = [v.reshape((2, v.shape[0] // 2) + v.shape[1:]) for v in terms]
        part = lambda k: [lax.dynamic_index_in_dim(v, k, 0, keepdims=False) for v in terms]
        self.send, self.terms = sum(part(1 - mine)), part(mine)
        return self.send


def arrived(sums, *before):
    got = [one.got for one in sums] + [one.more for one in sums if one.extra is not None]
    got = list(lax.optimization_barrier(tuple(got) + before))
    for one in sums:
        one.got = got.pop(0)
    for one in sums:
        if one.extra is not None:
            one.more = got.pop(0)
    return [one.add() for one in sums]


def after(values, *others):
    return lax.optimization_barrier((values,) + others)[0]


def selector(row_ref, h, sel_ref, slot):
    rows = sel_ref.shape[1]
    step = 256
    for r in range(0, rows, step):
        subs = lax.broadcasted_iota(jnp.int32, (step, rows), 0) + r
        found = jnp.where(row_ref[0, h : h + 1, :] == subs, 1.0, 0.0)
        sel_ref[slot, r : r + step, :] = found.astype(BF16)


def spans_of(rows):
    return [slice(c, c + CLUSTER) for c in range(0, rows, CLUSTER)]


def attend_kernel(x_ref, w_ref, bias_ref, row_ref, ctx_ref, moved_ref, probs_ref, sel_ref):
    rows = x_ref.shape[0]
    spans = spans_of(rows)
    for h in range(2):
        selector(row_ref, h, sel_ref, h)
    weight = jnp.concatenate([w_ref[c] for c in range(3)], axis=1)
    flat = dot_tt(weight, x_ref[...])
    parts = [flat[:128] + bias_ref[:, 0:1], flat[128:256], flat[256:] + bias_ref[:, 1:2]]
    parts = [part.astype(BF16) for part in parts]
    for h in range(2):
        cut = slice(h * HEAD_DIM, (h + 1) * HEAD_DIM)
        qkv = jnp.concatenate([part[cut] for part in parts], axis=0)
        moved = dot(qkv, sel_ref[h]).astype(BF16)
        moved_ref[h] = moved
        query, key, value = moved[:HEAD_DIM], moved[HEAD_DIM : 2 * HEAD_DIM], moved[2 * HEAD_DIM :]
        scores = jnp.concatenate([dot_tn(query[:, s], key[:, s]) for s in spans], axis=0) * SCALE
        shifted = jnp.exp(scores - jnp.max(scores, axis=-1, keepdims=True))
        probs = shifted / jnp.sum(shifted, axis=-1, keepdims=True)
        probs_b = probs.astype(BF16)
        probs_ref[h] = probs_b
        mixed = jnp.concatenate([dot_nt(value[:, s], probs_b[s]) for s in spans], axis=1)
        context = dot_nt(mixed.astype(BF16), sel_ref[h])
        ctx_ref[cut, :] = context.astype(BF16)


def attend(x, weight, bias_cols, order_rows):
    rows, width = x.shape
    pairs = order_rows.shape[0]
    local = weight.shape[2]
    return pl.pallas_call(
        attend_kernel,
        grid=(pairs,),
        in_specs=[
            whole(rows, width),
            pl.BlockSpec((3, width, 128), lambda p: (0, 0, p)),
            pl.BlockSpec((128, 2), lambda p: (p, 0)),
            pl.BlockSpec((1, 2, rows), lambda p: (p, 0, 0)),
        ],
        out_specs=[
            pl.BlockSpec((128, rows), lambda p: (p, 0)),
            pl.BlockSpec((2, 3 * HEAD_DIM, rows), lambda p: (p, 0, 0)),
            pl.BlockSpec((2, rows, CLUSTER), lambda p: (p, 0, 0)),
        ],
        out_shape=[
            shape((local, rows), BF16),
            shape((2 * pairs, 3 * HEAD_DIM, rows), BF16),
            shape((2 * pairs, rows, CLUSTER), BF16),
        ],
        scratch_shapes=[pltpu.VMEM((2, rows, rows), BF16)],
        compiler_params=params_of(40),
        cost_estimate=cost(12e9, 12e6),
        name="attend",
    )(x, weight, bias_cols, order_rows)


def block_place(j, order):
    place = 0
    for bit in order:
        place = 2 * place + ((j >> bit) & 1)
    return place


def write_halves(values, keep_ref, send_ref, mine, order, at):
    blocks = 2 ** (len(order) + 1)
    rows = values.shape[0] // blocks
    for j in range(0, blocks, 2):
        even, odd = values[j * rows : (j + 1) * rows], values[(j + 1) * rows : (j + 2) * rows]
        place = (block_place(j, order),) + at
        keep_ref[place] = jnp.where(mine == 0, even, odd)
        send_ref[place] = jnp.where(mine == 0, odd, even)


def attend_back_kernel(
    orders, core_ref, x_ref, da_ref, ow_ref, ctx_ref, w_ref, row_ref, moved_ref, probs_ref, part_ref, bias_ref, *refs
):
    *grad_refs, sel_ref = refs
    rows = da_ref.shape[0]
    spans = spans_of(rows)
    for h in range(2):
        selector(row_ref, h, sel_ref, h)
    d_attn = da_ref[...]
    d_context = dot_nt(ow_ref[...], d_attn).astype(BF16)
    d_out = dot_tt(d_attn, ctx_ref[...])
    found = []
    for h in range(2):
        d_moved = dot(d_context[h * HEAD_DIM : (h + 1) * HEAD_DIM], sel_ref[h]).astype(BF16)
        moved = moved_ref[h]
        query, key, value = moved[:HEAD_DIM], moved[HEAD_DIM : 2 * HEAD_DIM], moved[2 * HEAD_DIM :]
        probs_b = probs_ref[h]
        probs = probs_b.astype(F32)
        d_value = jnp.concatenate([dot(d_moved[:, s], probs_b[s]) for s in spans], axis=1)
        d_probs = jnp.concatenate([dot_tn(d_moved[:, s], value[:, s]) for s in spans], axis=0)
        inner = jnp.sum(probs * d_probs, axis=-1, keepdims=True)
        d_scores = (probs * (d_probs - inner)).astype(BF16)
        d_query = jnp.concatenate([dot_nt(key[:, s], d_scores[s]) for s in spans], axis=1) * SCALE
        d_key = jnp.concatenate([dot(query[:, s], d_scores[s]) for s in spans], axis=1) * SCALE
        three = jnp.concatenate([d_query, d_key, d_value], axis=0).astype(BF16)
        found.append(dot_nt(three, sel_ref[h]).astype(BF16))
    d_qkv = jnp.concatenate(
        [f[c * HEAD_DIM : (c + 1) * HEAD_DIM] for c in range(3) for f in found], axis=0
    )
    sums = dot_nt(jnp.ones((8, rows), BF16), d_qkv)
    bias_ref[0:1, :] = sums[0:1, :128]
    bias_ref[1:2, :] = sums[0:1, 256:]
    grads = dot_tt(x_ref[...], d_qkv)
    for c in range(4):
        values = grads[:, c * 128 : (c + 1) * 128] if c < 3 else d_out
        if orders:
            write_halves(values, *grad_refs[c // 2 * 2 :][:2], core_ref[0], orders[c // 2], (c % 2,))
        else:
            grad_refs[0][c] = values
    part = dot_tt(d_qkv, jnp.concatenate([w_ref[c] for c in range(3)], axis=1))

    @pl.when(pl.program_id(0) == 0)
    def _():
        part_ref[...] = part

    @pl.when(pl.program_id(0) > 0)
    def _():
        part_ref[...] += part


def attend_back(orders, core, x, d_attn, out_weight, context, weight, order_rows, moved, probs):
    rows, width = x.shape
    local = weight.shape[2]
    pairs = order_rows.shape[0]
    if orders:
        blocks = 2 ** len(orders[0])
        height = width // (2 * blocks)
        grad_specs = [pl.BlockSpec((blocks, 2, height, 128), lambda p: (0, 0, 0, p))] * 4
        grad_shapes = [shape((blocks, 2, height, local), F32)] * 4
    else:
        grad_specs = [pl.BlockSpec((4, width, 128), lambda p: (0, 0, p))]
        grad_shapes = [shape((4, width, local), F32)]
    return pl.pallas_call(
        functools.partial(attend_back_kernel, orders),
        grid=(pairs,),
        in_specs=[
            pl.BlockSpec(memory_space=pltpu.SMEM),
            whole(rows, width),
            whole(rows, width),
            pl.BlockSpec((128, width), lambda p: (p, 0)),
            pl.BlockSpec((128, rows), lambda p: (p, 0)),
            pl.BlockSpec((3, width, 128), lambda p: (0, 0, p)),
            pl.BlockSpec((1, 2, rows), lambda p: (p, 0, 0)),
            pl.BlockSpec((2, 3 * HEAD_DIM, rows), lambda p: (p, 0, 0)),
            pl.BlockSpec((2, rows, CLUSTER), lambda p: (p, 0, 0)),
        ],
        out_specs=[
            pl.BlockSpec((rows, width), lambda p: (0, 0)), pl.BlockSpec((2, 128), lambda p: (0, p)), *grad_specs
        ],
        out_shape=[shape((rows, width), F32), shape((2, local), F32), *grad_shapes],
        scratch_shapes=[pltpu.VMEM((2, rows, rows), BF16)],
        compiler_params=params_of(30),
        cost_estimate=cost(20e9, 20e6),
        name="attend_back",
    )(core, x, d_attn, out_weight, context, weight, order_rows, moved, probs)


def gelu_both(hidden):
    scale = 0.7978845608028654
    square = hidden * hidden
    bent = jnp.tanh(hidden * (scale + (scale * 0.044715) * square))
    half = 0.5 + 0.5 * bent
    active = hidden * half
    slope = half + 0.5 * hidden * (1.0 - bent * bent) * (scale + (3 * scale * 0.044715) * square)
    return active.astype(BF16), slope.astype(BF16)


def normalized(values):
    centred = values - jnp.mean(values, axis=-1, keepdims=True)
    factor = lax.rsqrt(jnp.mean(centred * centred, axis=-1, keepdims=True) + EPSILON)
    return centred * factor, factor


def norm_back(grad, unit, factor):
    mean = jnp.mean(grad, axis=-1, keepdims=True)
    inner = jnp.mean(grad * unit, axis=-1, keepdims=True)
    return factor * (grad - mean - unit * inner)


def unit_cuts(units):
    return [slice(u, u + UNIT_TILE) for u in range(0, units, UNIT_TILE)]


def narrow_copies(parts, stage, sems, places, out_s):
    depth = stage.shape[0]
    rows = stage.shape[1]

    def copy(k):
        return pltpu.make_async_copy(parts[k].at[0], stage.at[k % depth], sems.at[k % depth])

    def start():
        for k in range(min(depth, len(parts))):
            copy(k).start()

    def finish():
        for k in range(len(parts)):
            copy(k).wait()
            place = pl.multiple_of(places[k] * rows, rows)
            out_s[pl.ds(place, rows), :] = stage[k % depth].astype(BF16)
            if k + depth < len(parts):
                copy(k + depth).start()

    return start, finish


def placed_kernel(count, slots_ref, *refs):
    up_parts, down_parts, refs = refs[:count], refs[count : 2 * count], refs[2 * count :]
    up_ref, down_ref, up_stage, down_stage, up_sems, down_sems = refs
    places = [slots_ref[k] for k in range(count)]
    start_up, finish_up = narrow_copies(up_parts, up_stage, up_sems, places, up_ref)
    start_down, finish_down = narrow_copies(down_parts, down_stage, down_sems, places, down_ref)
    start_up()
    start_down()
    finish_up()
    finish_down()


def placed(slots, ups, downs, group):
    count = len(ups)
    scalars = pl.BlockSpec(memory_space=pltpu.SMEM)
    anywhere = pl.BlockSpec(memory_space=pl.ANY)
    out_shape = [
        shape((group * part[0].shape[1], part[0].shape[2]), BF16) for part in (ups, downs)
    ]
    return pl.pallas_call(
        functools.partial(placed_kernel, count),
        grid=(1,),
        in_specs=[scalars] + [anywhere] * (2 * count),
        out_specs=[whole(*out.shape) for out in out_shape],
        out_shape=out_shape,
        scratch_shapes=[
            pltpu.VMEM((count,) + ups[0].shape[1:], F32), pltpu.VMEM((count,) + downs[0].shape[1:], F32),
            pltpu.SemaphoreType.DMA((count,)), pltpu.SemaphoreType.DMA((count,)),
        ],
        compiler_params=params_of(20),
        cost_estimate=cost(1e6, 1e6),
        name="placed",
    )(slots, *ups, *downs)


def feed_rows(
    here, x_ref, cot_ref, ctx_ref, far_ctx_refs, vectors, ready, out_s, far_out_s, up_s, down_s, far_up_s, far_down_s,
    mixed_ref, d_pre_ref, d_attn_ref, sums_ref, up_sums_ref, nb_s, act_s, d_feed_s, d_hidden_s, far_slope_s,
):
    units = up_s.shape[1]
    out_bias, gain1, bias1, down_bias, gain2, bias2, up_bias, far_bias = vectors
    attention = dot_tn(ctx_ref[:, here], out_s[...])
    far_ctx = jnp.concatenate([ref[:, here].astype(BF16) for ref in far_ctx_refs], axis=0)
    attention += dot_tn(far_ctx, far_out_s[...])
    yield
    unit1, factor1 = normalized(x_ref[here, :].astype(F32) + attention + out_bias)
    normed = unit1 * gain1 + bias1
    nb = normed.astype(BF16)
    nb_s[here, :] = nb
    total = normed + down_bias
    yield
    ready("near")
    for cut in unit_cuts(units):
        active, slope = gelu_both(dot(nb, up_s[:, cut]) + up_bias[:, cut])
        act_s[here, cut] = active
        d_hidden_s[here, cut] = slope
        total = total + dot(active, down_s[cut, :])
        yield
    ready("far")
    for cut in unit_cuts(units):
        far_active, far_slope = gelu_both(dot(nb, far_up_s[:, cut]) + far_bias[:, cut])
        far_slope_s[here, cut] = far_slope
        total = total + dot(far_active, far_down_s[cut, :])
        yield
    unit2, factor2 = normalized(total)
    mixed_ref[here, :] = (unit2 * gain2 + bias2).astype(BF16)
    grad = cot_ref[here, :].astype(F32)
    sums_ref[0:1, :] += jnp.sum(grad * unit2, axis=0, keepdims=True)
    sums_ref[1:2, :] += jnp.sum(grad, axis=0, keepdims=True)
    d_sum = norm_back(grad * gain2, unit2, factor2)
    d_feed = d_sum.astype(BF16)
    d_feed_s[here, :] = d_feed
    sums_ref[2:3, :] += jnp.sum(d_feed.astype(F32), axis=0, keepdims=True)
    yield
    d_normed = d_sum
    for cut in unit_cuts(units):
        d_active = dot_nt(d_feed, down_s[cut, :])
        d_hidden = (d_active * d_hidden_s[here, cut].astype(F32)).astype(BF16)
        d_hidden_s[here, cut] = d_hidden
        up_sums_ref[:, cut] += jnp.sum(d_hidden.astype(F32), axis=0, keepdims=True)
        d_normed = d_normed + dot_nt(d_hidden, up_s[:, cut])
        yield
    for cut in unit_cuts(units):
        far_d_active = dot_nt(d_feed, far_down_s[cut, :])
        far_d_hidden = (far_d_active * far_slope_s[here, cut].astype(F32)).astype(BF16)
        d_normed = d_normed + dot_nt(far_d_hidden, far_up_s[:, cut])
        yield
    sums_ref[3:4, :] += jnp.sum(d_normed * unit1, axis=0, keepdims=True)
    sums_ref[4:5, :] += jnp.sum(d_normed, axis=0, keepdims=True)
    d_pre = norm_back(d_normed * gain1, unit1, factor1)
    d_pre_ref[here, :] = d_pre
    d_attn = d_pre.astype(BF16)
    d_attn_ref[here, :] = d_attn
    sums_ref[5:6, :] += jnp.sum(d_attn.astype(F32), axis=0, keepdims=True)


def in_turn(programs, lag):
    waiting = [k * lag for k in range(len(programs))]
    while any(wait is not None for wait in waiting):
        for k, wait in enumerate(waiting):
            if wait == 0:
                if next(programs[k], "end") == "end":
                    waiting[k] = None
            elif wait is not None:
                waiting[k] = wait - 1


def feed_kernel(orders, late_count, core_ref, slots_ref, x_ref, cot_ref, ctx_ref, far0_ref, far1_ref, far2_ref, *refs):
    vector_refs, refs = refs[:8], refs[8:]
    out_hbm, near_half_hbm, far_half_hbm, up_hbm, down_hbm, far_up_hbm, far_down_hbm, *refs = refs
    up_parts, down_parts, refs = refs[:late_count], refs[late_count : 2 * late_count], refs[2 * late_count :]
    mixed_ref, d_pre_ref, d_attn_ref, sums_ref, up_sums_ref, *refs = refs
    count = 4 if orders else 2
    grad_refs, refs = refs[:count], refs[count:]
    nb_s, act_s, d_feed_s, d_hidden_s, far_slope_s, out_s, far_out_s, up_s, down_s, far_up_s, far_down_s, *refs = refs
    half_stage, up_stage, down_stage, sems, up_sems, down_sems = refs
    step = pl.program_id(0)
    rows = x_ref.shape[0]
    tiles = 1

    @pl.when(step == 0)
    def _():
        copies = [
            pltpu.make_async_copy(source, target, sems.at[k])
            for k, (source, target) in enumerate((
                (out_hbm, out_s), (near_half_hbm, half_stage.at[0]), (far_half_hbm, half_stage.at[1]),
                (up_hbm, up_s), (down_hbm, down_s), (far_up_hbm, far_up_s), (far_down_hbm, far_down_s),
            ))
        ]
        places = [slots_ref[k] for k in range(late_count)]
        start_up, finish_up = narrow_copies(up_parts, up_stage, up_sems, places, far_up_s)
        start_down, finish_down = narrow_copies(down_parts, down_stage, down_sems, places, far_down_s)
        for copy in copies:
            copy.start()
        start_up()
        start_down()
        sums_ref[...] = jnp.zeros_like(sums_ref)
        up_sums_ref[...] = jnp.zeros_like(up_sums_ref)
        for copy in copies[:3]:
            copy.wait()
        half = half_stage.shape[1]
        for k in range(2):
            place = pl.multiple_of((core_ref[0] ^ k) * half, half)
            far_out_s[pl.ds(place, half), :] = half_stage[k].astype(BF16)
        done = []

        def ready(what):
            if what in done:
                return
            done.append(what)
            for copy in copies[3:5] if what == "near" else copies[5:]:
                copy.wait()
            if what == "far":
                finish_up()
                finish_down()

        vectors = [ref[...].reshape(1, ref.shape[0]) for ref in vector_refs]
        in_turn(
            [
                feed_rows(
                    slice(r, r + ROW_TILE), x_ref, cot_ref, ctx_ref, (far0_ref, far1_ref, far2_ref), vectors, ready,
                    out_s, far_out_s, up_s, down_s, far_up_s, far_down_s, mixed_ref, d_pre_ref, d_attn_ref, sums_ref,
                    up_sums_ref, nb_s, act_s, d_feed_s, d_hidden_s, far_slope_s,
                )
                for r in range(0, rows, ROW_TILE)
            ],
            LAG,
        )

    @pl.when(step >= tiles)
    def _():
        there = pl.ds(pl.multiple_of((step - tiles) * GRAD_TILE, GRAD_TILE), GRAD_TILE)
        d_down = dot_tn(d_feed_s[...], act_s[:, there])
        d_up = dot_tn(nb_s[...], d_hidden_s[:, there])
        if orders:
            write_halves(d_down, *grad_refs[:2], core_ref[0], orders[0], ())
            write_halves(d_up, *grad_refs[2:], core_ref[0], orders[1], ())
        else:
            grad_refs[0][...] = d_down
            grad_refs[1][...] = d_up


def feed(
    orders, core, slots, x, cotangent, context, far_context, out_weight, halves, vectors, up, down, far_up, far_down,
    ups, downs,
):
    rows, width = x.shape
    local, units = out_weight.shape[0], up.shape[1]
    tiles = 1
    if orders:
        blocks = 2 ** len(orders[0])
        height = width // (2 * blocks)
        grad_specs = [
            pl.BlockSpec((blocks, height, GRAD_TILE), lambda i: (0, 0, jnp.maximum(i - tiles, 0)))
        ] * 4
        grad_shapes = [shape((blocks, height, units), F32)] * 4
    else:
        grad_specs = [pl.BlockSpec((width, GRAD_TILE), lambda i: (0, jnp.maximum(i - tiles, 0)))] * 2
        grad_shapes = [shape((width, units), F32)] * 2
    scalars = pl.BlockSpec(memory_space=pltpu.SMEM)
    anywhere = pl.BlockSpec(memory_space=pl.ANY)
    depth = len(ups)
    return pl.pallas_call(
        functools.partial(feed_kernel, orders, len(ups)),
        grid=(tiles + units // GRAD_TILE,),
        in_specs=[
            scalars, scalars, whole(rows, width), whole(rows, width), whole(local, rows),
            *[whole(*part.shape) for part in far_context], *[whole(v.shape[0]) for v in vectors],
            *[anywhere] * (7 + len(ups) + len(downs)),
        ],
        out_specs=[
            whole(rows, width), whole(rows, width), whole(rows, width), whole(8, width), whole(1, units),
            *grad_specs,
        ],
        out_shape=[
            shape((rows, width), BF16), shape((rows, width), F32), shape((rows, width), BF16),
            shape((8, width), F32), shape((1, units), F32), *grad_shapes,
        ],
        scratch_shapes=[
            pltpu.VMEM((rows, width), BF16), pltpu.VMEM((rows, units), BF16), pltpu.VMEM((rows, width), BF16),
            pltpu.VMEM((rows, units), BF16), pltpu.VMEM((rows, units), BF16),
            pltpu.VMEM((local, width), BF16), pltpu.VMEM((local, width), BF16),
            pltpu.VMEM((width, units), BF16), pltpu.VMEM((units, width), BF16),
            pltpu.VMEM((width, units), BF16), pltpu.VMEM((units, width), BF16),
            pltpu.VMEM((2,) + halves[0].shape, F32), pltpu.VMEM((depth,) + ups[0].shape[1:], F32),
            pltpu.VMEM((depth,) + downs[0].shape[1:], F32), pltpu.SemaphoreType.DMA((7,)),
            pltpu.SemaphoreType.DMA((depth,)), pltpu.SemaphoreType.DMA((depth,)),
        ],
        compiler_params=params_of(60),
        cost_estimate=cost(25e9, 30e6),
        name="feed",
    )(
        core, slots, x, cotangent, context, *far_context, *vectors, out_weight, *halves, up, down,
        far_up, far_down, *ups, *downs,
    )


def make_body(n_items):
    def body(
        hidden_in,
        cluster_order,
        qkv_weight,
        qv_bias,
        out_weight,
        out_bias,
        norm1_gain,
        norm1_bias,
        up_weight,
        up_bias,
        down_weight,
        down_bias,
        norm2_gain,
        norm2_bias,
        cotangent,
    ):
        rows, width = hidden_in.shape
        units = up_weight.shape[1]
        local = out_weight.shape[0]
        item = lax.axis_index("items")
        core = item & 1
        group = 8
        place = item % group

        def piece(values):
            count = values.shape[0] // group
            return lax.dynamic_slice_in_dim(values, place * count, count, 0).astype(F32)[None]

        up_piece = piece(up_weight)
        down_piece = piece(after(down_weight, up_piece))
        half = local // 2
        far_up = swapped(up_piece)
        far_down = swapped(down_piece)
        ordering = cluster_order[:, 0, :]
        order_rows = ordering.reshape(-1, 2, rows)
        x = after(hidden_in, up_piece, down_piece)
        context, moved, probs = attend(x, qkv_weight, qv_bias.T, order_rows)
        pairs = order_rows.shape[0]
        far_context = [
            swapped(context[p * 128 : (p + 1) * 128].astype(F32)) for p in range(pairs)
        ]
        out_piece = lax.dynamic_slice_in_dim(out_weight, core * half, half, 0)
        out_piece = out_piece.astype(F32)
        far_bias = swapped(up_bias)

        trade = lambda values, step: traded(values, step, n_items)
        at_once = lambda *values: lax.optimization_barrier(values)
        far_half = swapped(after(out_piece, down_piece))
        up0 = after(far_up, context)
        up4, up2 = trade(up0, 4), trade(up0, 2)
        down0 = after(far_down, up0)
        down4, down2 = trade(down0, 4), trade(down0, 2)
        up4, up2, down4, down2, far_half, far_context[0], far_bias = at_once(
            up4, up2, down4, down2, far_half, far_context[0], far_bias
        )
        up6, down6 = trade(up4, 2), trade(down4, 2)
        ups, downs = [up0, up4, up2], [down0, down4, down2]
        ups, downs = [[after(part, down4) for part in parts] for parts in (ups, downs)]
        up_beside = [trade(part, 1) for part in ups]
        down_beside = [trade(part, 1) for part in downs]
        other_half = trade(after(far_half, down4), 1)
        all_slots = lambda ks: jnp.stack([place ^ k ^ c for c in (0, 1) for k in ks]).astype(jnp.int32)
        slots = all_slots((6,))
        far_up, far_down = placed(all_slots((0, 4, 2)), ups + up_beside, downs + down_beside, group)
        up6, down6, far_context[1], far_context[2], far_up = at_once(
            up6, down6, far_context[1], far_context[2], far_up
        )
        ups, downs = [[part, trade(part, 1)] for part in (up6, down6)]
        which = core.astype(jnp.int32).reshape(1)

        split = width % (8 * n_items) == 0
        bits = tuple(range(1, n_items.bit_length() - 1))
        late_y = bits[1:2] + bits[:1] + bits[2:]
        mixed, d_pre, d_attn, sums, up_sums, *grads = feed(
            (bits, late_y) if split else None, which, slots, x, cotangent, context, far_context,
            out_weight, [far_half, other_half],
            [out_bias, norm1_gain, norm1_bias, down_bias, norm2_gain, norm2_bias, up_bias, far_bias],
            up_weight, down_weight, far_up, far_down, ups, downs,
        )

        def packed_of(grad_qv):
            return jnp.concatenate(
                [sums, up_sums.reshape(-1, width), grad_qv.reshape(-1, width)], axis=0
            )

        back = lambda d_attn: attend_back(
            (bits, late_y) if split else None, which, x, d_attn, out_weight, context, qkv_weight,
            order_rows, moved, probs,
        )
        if split:
            halving = lambda keep, send, order: Halving(keep, send, order, n_items).trade()
            down_sum, up_sum = halving(*grads[:2], bits), halving(*grads[2:], late_y)
            sent = arrived([down_sum, up_sum])
            down_sum.trade()
            up_sum.trade()
            part, grad_qv, *halves = back(after(d_attn, *sent))
            far_part = swapped(part)
            first, second = halving(*halves[:2], bits), halving(*halves[2:], late_y)
            sent = arrived([down_sum, up_sum], part)
            down_sum.trade()
            up_sum.trade()
            sent = arrived([first, second], *sent)
            first.extra = packed_of(grad_qv)
            first.extra = first.extra + traded(first.extra, 1, n_items)
            first.trade()
            second.trade()
            sums_all = [down_sum, up_sum, first, second]
            for _ in bits[2:]:
                arrived(sums_all)
                for one in sums_all[::-1]:
                    one.trade()
            summed_down, summed_up, *sent = arrived(sums_all)
            first.trade()
            second.trade()
            far_part = after(far_part, summed_down, summed_up, *sent)
            grad_inputs = (d_pre + part + far_part).astype(BF16)
            summed = arrived([first, second], grad_inputs)
            summed_rest = [summed[c // 2][c % 2] for c in range(4)]
            packed = first.extra
        else:
            part, grad_qv, grad_rest = back(d_attn)
            grad_inputs = (d_pre + part + swapped(part)).astype(BF16)
            summed_down = scattered(grads[0], n_items, 0)
            summed_up = scattered(grads[1], n_items, 0)
            summed_rest = scattered(grad_rest, n_items, 1)
            packed = all_sum(packed_of(grad_qv), n_items)
        small = packed[:8]
        up_small = packed[8 : 8 + units // width].reshape(units)
        qv_small = packed[8 + units // width :].reshape(2, local)
        return (
            mixed,
            grad_inputs,
            jnp.stack([summed_rest[c] for c in range(3)]),
            qv_small,
            summed_rest[3].T,
            small[5],
            small[3],
            small[4],
            summed_up,
            up_small,
            summed_down.T,
            small[2],
            small[0],
            small[1],
        )

    return body


def solution(mesh):
    return jax.shard_map(
        make_body(mesh.shape["items"]),
        mesh=mesh,
        in_specs=(
            P("items", None),
            P("heads", "items", None),
            P(None, None, "heads"),
            P(None, "heads"),
            P("heads", None),
            P(),
            P(),
            P(),
            P(None, "heads"),
            P("heads"),
            P("heads", None),
            P(),
            P(),
            P(),
            P("items", None),
        ),
        out_specs=(
            P("items", None),
            P("items", None),
            P(None, "items", "heads"),
            P(None, "heads"),
            P("heads", "items"),
            P(),
            P(),
            P(),
            P("items", "heads"),
            P("heads"),
            P("heads", "items"),
            P(),
            P(),
            P(),
        ),
        check_vma=False,
    )
```

```python
import functools

import jax
import jax.numpy as jnp
from jax import lax
from jax.experimental import pallas as pl
from jax.experimental.pallas import tpu as pltpu
from jax.sharding import PartitionSpec as P

HEAD_DIM = 64
CLUSTER = 128
SCALE = HEAD_DIM**-0.5
EPSILON = 1e-05
ROW_TILE = 256
GRAD_TILE = 512
UNIT_TILE = 1536
BF16 = jnp.bfloat16
F32 = jnp.float32


def dot(left, right):
    return jnp.dot(left, right, preferred_element_type=F32)


def dot_nt(left, right):
    return lax.dot_general(left, right, (((1,), (1,)), ((), ())), preferred_element_type=F32)


def dot_tn(left, right):
    return lax.dot_general(left, right, (((0,), (0,)), ((), ())), preferred_element_type=F32)


def dot_tt(left, right):
    return lax.dot_general(left, right, (((0,), (1,)), ((), ())), preferred_element_type=F32)


def params_of(mib):
    return pltpu.CompilerParams(vmem_limit_bytes=mib * 1024 * 1024)


def cost(flops, bytes_accessed):
    return pl.CostEstimate(flops=int(flops) // 1000, bytes_accessed=int(bytes_accessed) // 1000, transcendentals=0)


def shape(dims, dtype):
    return jax.ShapeDtypeStruct(dims, dtype)


def whole(*dims):
    return pl.BlockSpec(dims, lambda *_: (0,) * len(dims), pipeline_mode=pl.Buffered(1))


def swapped(values):
    return lax.ppermute(values, "heads", [(0, 1), (1, 0)])


def traded(values, step, n_items):
    return lax.ppermute(values, "items", [(i, i ^ step) for i in range(n_items)])


def all_sum(values, n_items):
    step = 1
    while step < n_items:
        values = values + traded(values, step, n_items)
        step *= 2
    return values


def scattered(values, n_items, axis):
    item = lax.axis_index("items")
    size = n_items
    for bit in range(n_items.bit_length() - 1):
        dims = values.shape
        size //= 2
        halves = values.reshape(dims[:axis] + (size, 2, dims[axis] // (2 * size)) + dims[axis + 1 :])
        mine = (item >> bit) & 1
        send = lax.dynamic_index_in_dim(halves, 1 - mine, axis + 1, keepdims=False)
        keep = lax.dynamic_index_in_dim(halves, mine, axis + 1, keepdims=False)
        values = keep + traded(send, 1 << bit, n_items)
        values = values.reshape(dims[:axis] + (-1,) + dims[axis + 1 :])
    return values


class Halving:
    def __init__(self, keep, send, order, n_items):
        self.order, self.n_items, self.rest = list(order), n_items, keep.shape[1:]
        self.terms = []
        self.hold(keep)
        self.send, self.extra, self.bit = send, None, 0

    def hold(self, values):
        self.terms.append((values.reshape((2,) * len(self.order) + self.rest), []))

    def part(self, term, places):
        values, settled = term
        starts = settled + places
        sizes = (1,) * len(starts) + values.shape[len(starts) :]
        starts = starts + [0] * (values.ndim - len(starts))
        return lax.dynamic_slice(values, starts, sizes).reshape((-1,) + self.rest)

    def trade(self):
        self.got = traded(self.send, 1 << self.bit, self.n_items)
        if self.extra is not None:
            self.more = traded(self.extra, 1 << self.bit, self.n_items)
        return self

    def add(self):
        self.hold(self.got)
        if self.extra is not None:
            self.extra = self.extra + self.more
        if not self.order:
            return sum(self.part(term, []) for term in self.terms).reshape(self.rest)
        self.bit = self.order.pop(0)
        mine = (lax.axis_index("items") >> self.bit) & 1
        self.send = sum(self.part(term, [1 - mine]) for term in self.terms)
        self.terms = [(values, settled + [mine]) for values, settled in self.terms]
        return self.send


def arrived(sums, *before):
    got = [one.got for one in sums] + [one.more for one in sums if one.extra is not None]
    got = list(lax.optimization_barrier(tuple(got) + before))
    for one in sums:
        one.got = got.pop(0)
    for one in sums:
        if one.extra is not None:
            one.more = got.pop(0)
    return [one.add() for one in sums]


def after(values, *others):
    return lax.optimization_barrier((values,) + others)[0]


def selector(row_ref, h, sel_ref, slot):
    rows = sel_ref.shape[1]
    step = 256
    for r in range(0, rows, step):
        subs = lax.broadcasted_iota(jnp.int32, (step, rows), 0) + r
        found = jnp.where(row_ref[0, h : h + 1, :] == subs, 1.0, 0.0)
        sel_ref[slot, r : r + step, :] = found.astype(BF16)


def spans_of(rows):
    return [slice(c, c + CLUSTER) for c in range(0, rows, CLUSTER)]


def attend_kernel(x_ref, w_ref, bias_ref, row_ref, ctx_ref, moved_ref, probs_ref, sel_ref):
    rows = x_ref.shape[0]
    spans = spans_of(rows)
    for h in range(2):
        selector(row_ref, h, sel_ref, h)
    weight = jnp.concatenate([w_ref[c] for c in range(3)], axis=1)
    flat = dot_tt(weight, x_ref[...])
    parts = [flat[:128] + bias_ref[:, 0:1], flat[128:256], flat[256:] + bias_ref[:, 1:2]]
    parts = [part.astype(BF16) for part in parts]
    for h in range(2):
        cut = slice(h * HEAD_DIM, (h + 1) * HEAD_DIM)
        qkv = jnp.concatenate([part[cut] for part in parts], axis=0)
        moved = dot(qkv, sel_ref[h]).astype(BF16)
        moved_ref[h] = moved
        query, key, value = moved[:HEAD_DIM], moved[HEAD_DIM : 2 * HEAD_DIM], moved[2 * HEAD_DIM :]
        scores = jnp.concatenate([dot_tn(query[:, s], key[:, s]) for s in spans], axis=0) * SCALE
        shifted = jnp.exp(scores - jnp.max(scores, axis=-1, keepdims=True))
        probs = shifted / jnp.sum(shifted, axis=-1, keepdims=True)
        probs_b = probs.astype(BF16)
        probs_ref[h] = probs_b
        mixed = jnp.concatenate([dot_nt(value[:, s], probs_b[s]) for s in spans], axis=1)
        context = dot_nt(mixed.astype(BF16), sel_ref[h])
        ctx_ref[cut, :] = context.astype(BF16)


def attend(x, weight, bias_cols, order_rows):
    rows, width = x.shape
    pairs = order_rows.shape[0]
    local = weight.shape[2]
    return pl.pallas_call(
        attend_kernel,
        grid=(pairs,),
        in_specs=[
            whole(rows, width),
            pl.BlockSpec((3, width, 128), lambda p: (0, 0, p)),
            pl.BlockSpec((128, 2), lambda p: (p, 0)),
            pl.BlockSpec((1, 2, rows), lambda p: (p, 0, 0)),
        ],
        out_specs=[
            pl.BlockSpec((128, rows), lambda p: (p, 0)),
            pl.BlockSpec((2, 3 * HEAD_DIM, rows), lambda p: (p, 0, 0)),
            pl.BlockSpec((2, rows, CLUSTER), lambda p: (p, 0, 0)),
        ],
        out_shape=[
            shape((local, rows), BF16),
            shape((2 * pairs, 3 * HEAD_DIM, rows), BF16),
            shape((2 * pairs, rows, CLUSTER), BF16),
        ],
        scratch_shapes=[pltpu.VMEM((2, rows, rows), BF16)],
        compiler_params=params_of(40),
        cost_estimate=cost(12e9, 12e6),
        name="attend",
    )(x, weight, bias_cols, order_rows)


def block_place(j, order):
    place = 0
    for bit in order:
        place = 2 * place + ((j >> bit) & 1)
    return place


def write_halves(values, keep_ref, send_ref, mine, order, at):
    blocks = 2 ** (len(order) + 1)
    rows = values.shape[0] // blocks
    for j in range(0, blocks, 2):
        even, odd = values[j * rows : (j + 1) * rows], values[(j + 1) * rows : (j + 2) * rows]
        place = (block_place(j, order),) + at
        keep_ref[place] = jnp.where(mine == 0, even, odd)
        send_ref[place] = jnp.where(mine == 0, odd, even)


def attend_back_kernel(
    orders, core_ref, x_ref, da_ref, ow_ref, ctx_ref, w_ref, row_ref, moved_ref, probs_ref, part_ref, bias_ref, *refs
):
    *grad_refs, sel_ref = refs
    rows = da_ref.shape[0]
    spans = spans_of(rows)
    for h in range(2):
        selector(row_ref, h, sel_ref, h)
    d_attn = da_ref[...]
    d_context = dot_nt(ow_ref[...], d_attn).astype(BF16)
    d_out = dot_tt(d_attn, ctx_ref[...])
    found = []
    for h in range(2):
        d_moved = dot(d_context[h * HEAD_DIM : (h + 1) * HEAD_DIM], sel_ref[h]).astype(BF16)
        moved = moved_ref[h]
        query, key, value = moved[:HEAD_DIM], moved[HEAD_DIM : 2 * HEAD_DIM], moved[2 * HEAD_DIM :]
        probs_b = probs_ref[h]
        probs = probs_b.astype(F32)
        d_value = jnp.concatenate([dot(d_moved[:, s], probs_b[s]) for s in spans], axis=1)
        d_probs = jnp.concatenate([dot_tn(d_moved[:, s], value[:, s]) for s in spans], axis=0)
        inner = jnp.sum(probs * d_probs, axis=-1, keepdims=True)
        d_scores = (probs * (d_probs - inner)).astype(BF16)
        d_query = jnp.concatenate([dot_nt(key[:, s], d_scores[s]) for s in spans], axis=1) * SCALE
        d_key = jnp.concatenate([dot(query[:, s], d_scores[s]) for s in spans], axis=1) * SCALE
        three = jnp.concatenate([d_query, d_key, d_value], axis=0).astype(BF16)
        found.append(dot_nt(three, sel_ref[h]).astype(BF16))
    d_qkv = jnp.concatenate(
        [f[c * HEAD_DIM : (c + 1) * HEAD_DIM] for c in range(3) for f in found], axis=0
    )
    sums = dot_nt(jnp.ones((8, rows), BF16), d_qkv)
    bias_ref[0:1, :] = sums[0:1, :128]
    bias_ref[1:2, :] = sums[0:1, 256:]
    grads = dot_tt(x_ref[...], d_qkv)
    for c in range(4):
        values = grads[:, c * 128 : (c + 1) * 128] if c < 3 else d_out
        if orders:
            write_halves(values, *grad_refs[c // 2 * 2 :][:2], core_ref[0], orders[c // 2], (c % 2,))
        else:
            grad_refs[0][c] = values
    part = dot_tt(d_qkv, jnp.concatenate([w_ref[c] for c in range(3)], axis=1))

    @pl.when(pl.program_id(0) == 0)
    def _():
        part_ref[...] = part

    @pl.when(pl.program_id(0) > 0)
    def _():
        part_ref[...] += part


def attend_back(orders, core, x, d_attn, out_weight, context, weight, order_rows, moved, probs):
    rows, width = x.shape
    local = weight.shape[2]
    pairs = order_rows.shape[0]
    if orders:
        blocks = 2 ** len(orders[0])
        height = width // (2 * blocks)
        grad_specs = [pl.BlockSpec((blocks, 2, height, 128), lambda p: (0, 0, 0, p))] * 4
        grad_shapes = [shape((blocks, 2, height, local), F32)] * 4
    else:
        grad_specs = [pl.BlockSpec((4, width, 128), lambda p: (0, 0, p))]
        grad_shapes = [shape((4, width, local), F32)]
    return pl.pallas_call(
        functools.partial(attend_back_kernel, orders),
        grid=(pairs,),
        in_specs=[
            pl.BlockSpec(memory_space=pltpu.SMEM),
            whole(rows, width),
            whole(rows, width),
            pl.BlockSpec((128, width), lambda p: (p, 0)),
            pl.BlockSpec((128, rows), lambda p: (p, 0)),
            pl.BlockSpec((3, width, 128), lambda p: (0, 0, p)),
            pl.BlockSpec((1, 2, rows), lambda p: (p, 0, 0)),
            pl.BlockSpec((2, 3 * HEAD_DIM, rows), lambda p: (p, 0, 0)),
            pl.BlockSpec((2, rows, CLUSTER), lambda p: (p, 0, 0)),
        ],
        out_specs=[
            pl.BlockSpec((rows, width), lambda p: (0, 0)), pl.BlockSpec((2, 128), lambda p: (0, p)), *grad_specs
        ],
        out_shape=[shape((rows, width), F32), shape((2, local), F32), *grad_shapes],
        scratch_shapes=[pltpu.VMEM((2, rows, rows), BF16)],
        compiler_params=params_of(30),
        cost_estimate=cost(20e9, 20e6),
        name="attend_back",
    )(core, x, d_attn, out_weight, context, weight, order_rows, moved, probs)


def gelu_both(hidden):
    scale = 0.7978845608028654
    square = hidden * hidden
    bent = jnp.tanh(hidden * (scale + (scale * 0.044715) * square))
    half = 0.5 + 0.5 * bent
    active = hidden * half
    slope = half + 0.5 * hidden * (1.0 - bent * bent) * (scale + (3 * scale * 0.044715) * square)
    return active.astype(BF16), slope.astype(BF16)


def normalized(values):
    centred = values - jnp.mean(values, axis=-1, keepdims=True)
    factor = lax.rsqrt(jnp.mean(centred * centred, axis=-1, keepdims=True) + EPSILON)
    return centred * factor, factor


def norm_back(grad, unit, factor):
    mean = jnp.mean(grad, axis=-1, keepdims=True)
    inner = jnp.mean(grad * unit, axis=-1, keepdims=True)
    return factor * (grad - mean - unit * inner)


def unit_cuts(units):
    return [slice(u, u + UNIT_TILE) for u in range(0, units, UNIT_TILE)]


def narrow_copies(parts, stage, sems, places, out_s):
    depth = stage.shape[0]
    rows = stage.shape[1]

    def copy(k):
        return pltpu.make_async_copy(parts[k].at[0], stage.at[k % depth], sems.at[k % depth])

    def start():
        for k in range(min(depth, len(parts))):
            copy(k).start()

    def finish():
        for k in range(len(parts)):
            copy(k).wait()
            place = pl.multiple_of(places[k] * rows, rows)
            out_s[pl.ds(place, rows), :] = stage[k % depth].astype(BF16)
            if k + depth < len(parts):
                copy(k + depth).start()

    return start, finish


def placed_kernel(count, slots_ref, *refs):
    up_parts, down_parts, refs = refs[:count], refs[count : 2 * count], refs[2 * count :]
    up_ref, down_ref, up_stage, down_stage, up_sems, down_sems = refs
    places = [slots_ref[k] for k in range(count)]
    start_up, finish_up = narrow_copies(up_parts, up_stage, up_sems, places, up_ref)
    start_down, finish_down = narrow_copies(down_parts, down_stage, down_sems, places, down_ref)
    start_up()
    start_down()
    finish_up()
    finish_down()


def placed(slots, ups, downs, group):
    count = len(ups)
    scalars = pl.BlockSpec(memory_space=pltpu.SMEM)
    anywhere = pl.BlockSpec(memory_space=pl.ANY)
    out_shape = [
        shape((group * part[0].shape[1], part[0].shape[2]), BF16) for part in (ups, downs)
    ]
    return pl.pallas_call(
        functools.partial(placed_kernel, count),
        grid=(1,),
        in_specs=[scalars] + [anywhere] * (2 * count),
        out_specs=[whole(*out.shape) for out in out_shape],
        out_shape=out_shape,
        scratch_shapes=[
            pltpu.VMEM((count,) + ups[0].shape[1:], F32), pltpu.VMEM((count,) + downs[0].shape[1:], F32),
            pltpu.SemaphoreType.DMA((count,)), pltpu.SemaphoreType.DMA((count,)),
        ],
        compiler_params=params_of(20),
        cost_estimate=cost(1e6, 1e6),
        name="placed",
    )(slots, *ups, *downs)


def feed_rows(
    x_ref, cot_ref, ctx_ref, far_ctx_refs, vector_refs, ready, out_s, far_out_s, up_s, down_s, far_up_s, far_down_s,
    mixed_ref, d_pre_ref, d_attn_ref, sums_ref, up_sums_ref, nb_s, act_s, d_feed_s, d_hidden_s, here,
):
    units = up_s.shape[1]
    row = lambda ref: ref[...].reshape(1, ref.shape[0])
    out_bias, gain1, bias1, down_bias, gain2, bias2, up_bias, far_bias = map(row, vector_refs)
    ready("out")
    attention = dot_tn(ctx_ref[...], out_s[...])
    far_ctx = jnp.concatenate([ref[...].astype(BF16) for ref in far_ctx_refs], axis=0)
    attention += dot_tn(far_ctx, far_out_s[...])
    unit1, factor1 = normalized(x_ref[...].astype(F32) + attention + out_bias)
    normed = unit1 * gain1 + bias1
    nb = normed.astype(BF16)
    nb_s[here, :] = nb
    total = normed + down_bias
    slopes, far_slopes = [], []
    ready("near")
    for cut in unit_cuts(units):
        active, slope = gelu_both(dot(nb, up_s[:, cut]) + up_bias[:, cut])
        act_s[here, cut] = active
        slopes.append(slope)
        total = total + dot(active, down_s[cut, :])
    ready("far")
    for cut in unit_cuts(units):
        far_active, far_slope = gelu_both(dot(nb, far_up_s[:, cut]) + far_bias[:, cut])
        far_slopes.append(far_slope)
        total = total + dot(far_active, far_down_s[cut, :])
    unit2, factor2 = normalized(total)
    mixed_ref[...] = (unit2 * gain2 + bias2).astype(BF16)
    grad = cot_ref[...].astype(F32)
    sums_ref[0:1, :] += jnp.sum(grad * unit2, axis=0, keepdims=True)
    sums_ref[1:2, :] += jnp.sum(grad, axis=0, keepdims=True)
    d_sum = norm_back(grad * gain2, unit2, factor2)
    d_feed = d_sum.astype(BF16)
    d_feed_s[here, :] = d_feed
    sums_ref[2:3, :] += jnp.sum(d_feed.astype(F32), axis=0, keepdims=True)
    d_normed = d_sum
    for cut, slope, far_slope in zip(unit_cuts(units), slopes, far_slopes):
        d_active = dot_nt(d_feed, down_s[cut, :])
        d_hidden = (d_active * slope.astype(F32)).astype(BF16)
        d_hidden_s[here, cut] = d_hidden
        up_sums_ref[:, cut] += jnp.sum(d_hidden.astype(F32), axis=0, keepdims=True)
        far_d_active = dot_nt(d_feed, far_down_s[cut, :])
        far_d_hidden = (far_d_active * far_slope.astype(F32)).astype(BF16)
        d_normed = d_normed + dot_nt(d_hidden, up_s[:, cut])
        d_normed = d_normed + dot_nt(far_d_hidden, far_up_s[:, cut])
    sums_ref[3:4, :] += jnp.sum(d_normed * unit1, axis=0, keepdims=True)
    sums_ref[4:5, :] += jnp.sum(d_normed, axis=0, keepdims=True)
    d_pre = norm_back(d_normed * gain1, unit1, factor1)
    d_pre_ref[...] = d_pre
    d_attn = d_pre.astype(BF16)
    d_attn_ref[...] = d_attn
    sums_ref[5:6, :] += jnp.sum(d_attn.astype(F32), axis=0, keepdims=True)


def feed_kernel(
    orders, tiles, late_count, core_ref, slots_ref, x_ref, cot_ref, ctx_ref, far0_ref, far1_ref, far2_ref, *refs
):
    vector_refs, refs = refs[:8], refs[8:]
    out_hbm, near_half_hbm, far_half_hbm, up_hbm, down_hbm, far_up_hbm, far_down_hbm, *refs = refs
    up_parts, down_parts, refs = refs[:late_count], refs[late_count : 2 * late_count], refs[2 * late_count :]
    mixed_ref, d_pre_ref, d_attn_ref, sums_ref, up_sums_ref, *refs = refs
    count = 4 if orders else 2
    grad_refs, refs = refs[:count], refs[count:]
    nb_s, act_s, d_feed_s, d_hidden_s, out_s, far_out_s, up_s, down_s, far_up_s, far_down_s, *refs = refs
    half_stage, up_stage, down_stage, sems, up_sems, down_sems = refs
    step = pl.program_id(0)
    tile = x_ref.shape[0]
    copies = [
        pltpu.make_async_copy(source, target, sems.at[k])
        for k, (source, target) in enumerate((
            (out_hbm, out_s), (near_half_hbm, half_stage.at[0]), (far_half_hbm, half_stage.at[1]),
            (up_hbm, up_s), (down_hbm, down_s), (far_up_hbm, far_up_s), (far_down_hbm, far_down_s),
        ))
    ]
    places = [slots_ref[k] for k in range(late_count)]
    start_up, finish_up = narrow_copies(up_parts, up_stage, up_sems, places, far_up_s)
    start_down, finish_down = narrow_copies(down_parts, down_stage, down_sems, places, far_down_s)

    def ready(what):
        @pl.when(step == 0)
        def _():
            if what == "out":
                for copy in copies:
                    copy.start()
                start_up()
                start_down()
                sums_ref[...] = jnp.zeros_like(sums_ref)
                up_sums_ref[...] = jnp.zeros_like(up_sums_ref)
                for copy in copies[:3]:
                    copy.wait()
                half = half_stage.shape[1]
                for k in range(2):
                    place = pl.multiple_of((core_ref[0] ^ k) * half, half)
                    far_out_s[pl.ds(place, half), :] = half_stage[k].astype(BF16)
            elif what == "near":
                for copy in copies[3:5]:
                    copy.wait()
            else:
                for copy in copies[5:]:
                    copy.wait()
                finish_up()
                finish_down()

    @pl.when(step < tiles)
    def _():
        here = pl.ds(pl.multiple_of(step * tile, tile), tile)
        feed_rows(
            x_ref, cot_ref, ctx_ref, (far0_ref, far1_ref, far2_ref), vector_refs, ready, out_s, far_out_s, up_s,
            down_s, far_up_s, far_down_s, mixed_ref, d_pre_ref, d_attn_ref, sums_ref, up_sums_ref, nb_s, act_s,
            d_feed_s, d_hidden_s, here,
        )

    @pl.when(step >= tiles)
    def _():
        there = pl.ds(pl.multiple_of((step - tiles) * GRAD_TILE, GRAD_TILE), GRAD_TILE)
        d_down = dot_tn(d_feed_s[...], act_s[:, there])
        d_up = dot_tn(nb_s[...], d_hidden_s[:, there])
        if orders:
            write_halves(d_down, *grad_refs[:2], core_ref[0], orders[0], ())
            write_halves(d_up, *grad_refs[2:], core_ref[0], orders[1], ())
        else:
            grad_refs[0][...] = d_down
            grad_refs[1][...] = d_up


def feed(
    orders, core, slots, x, cotangent, context, far_context, out_weight, halves, vectors, up, down, far_up, far_down,
    ups, downs,
):
    rows, width = x.shape
    local, units = out_weight.shape[0], up.shape[1]
    tile = ROW_TILE
    tiles = rows // tile
    across = lambda cols: pl.BlockSpec((tile, cols), lambda i: (jnp.minimum(i, tiles - 1), 0))
    along = lambda height: pl.BlockSpec((height, tile), lambda i: (0, jnp.minimum(i, tiles - 1)))
    if orders:
        blocks = 2 ** len(orders[0])
        height = width // (2 * blocks)
        grad_specs = [
            pl.BlockSpec((blocks, height, GRAD_TILE), lambda i: (0, 0, jnp.maximum(i - tiles, 0)))
        ] * 4
        grad_shapes = [shape((blocks, height, units), F32)] * 4
    else:
        grad_specs = [pl.BlockSpec((width, GRAD_TILE), lambda i: (0, jnp.maximum(i - tiles, 0)))] * 2
        grad_shapes = [shape((width, units), F32)] * 2
    scalars = pl.BlockSpec(memory_space=pltpu.SMEM)
    anywhere = pl.BlockSpec(memory_space=pl.ANY)
    depth = len(ups)
    return pl.pallas_call(
        functools.partial(feed_kernel, orders, tiles, len(ups)),
        grid=(tiles + units // GRAD_TILE,),
        in_specs=[
            scalars, scalars, across(width), across(width), along(local),
            *[along(part.shape[0]) for part in far_context], *[whole(v.shape[0]) for v in vectors],
            *[anywhere] * (7 + len(ups) + len(downs)),
        ],
        out_specs=[
            across(width), across(width), across(width), whole(8, width), whole(1, units),
            *grad_specs,
        ],
        out_shape=[
            shape((rows, width), BF16), shape((rows, width), F32), shape((rows, width), BF16),
            shape((8, width), F32), shape((1, units), F32), *grad_shapes,
        ],
        scratch_shapes=[
            pltpu.VMEM((rows, width), BF16), pltpu.VMEM((rows, units), BF16), pltpu.VMEM((rows, width), BF16),
            pltpu.VMEM((rows, units), BF16),
            pltpu.VMEM((local, width), BF16), pltpu.VMEM((local, width), BF16),
            pltpu.VMEM((width, units), BF16), pltpu.VMEM((units, width), BF16),
            pltpu.VMEM((width, units), BF16), pltpu.VMEM((units, width), BF16),
            pltpu.VMEM((2,) + halves[0].shape, F32), pltpu.VMEM((depth,) + ups[0].shape[1:], F32),
            pltpu.VMEM((depth,) + downs[0].shape[1:], F32), pltpu.SemaphoreType.DMA((7,)),
            pltpu.SemaphoreType.DMA((depth,)), pltpu.SemaphoreType.DMA((depth,)),
        ],
        compiler_params=params_of(56),
        cost_estimate=cost(25e9, 30e6),
        name="feed",
    )(
        core, slots, x, cotangent, context, *far_context, *vectors, out_weight, *halves, up, down,
        far_up, far_down, *ups, *downs,
    )


def make_body(n_items):
    def body(
        hidden_in,
        cluster_order,
        qkv_weight,
        qv_bias,
        out_weight,
        out_bias,
        norm1_gain,
        norm1_bias,
        up_weight,
        up_bias,
        down_weight,
        down_bias,
        norm2_gain,
        norm2_bias,
        cotangent,
    ):
        rows, width = hidden_in.shape
        units = up_weight.shape[1]
        local = out_weight.shape[0]
        item = lax.axis_index("items")
        core = item & 1
        group = 8
        place = item % group

        def piece(values):
            count = values.shape[0] // group
            return lax.dynamic_slice_in_dim(values, place * count, count, 0).astype(F32)[None]

        up_piece = piece(up_weight)
        down_piece = piece(after(down_weight, up_piece))
        half = local // 2
        far_up = swapped(up_piece)
        far_down = swapped(down_piece)
        ordering = cluster_order[:, 0, :]
        order_rows = ordering.reshape(-1, 2, rows)
        x = after(hidden_in, up_piece, down_piece)
        context, moved, probs = attend(x, qkv_weight, qv_bias.T, order_rows)
        pairs = order_rows.shape[0]
        far_context = [
            swapped(context[p * 128 : (p + 1) * 128].astype(F32)) for p in range(pairs)
        ]
        out_piece = lax.dynamic_slice_in_dim(out_weight, core * half, half, 0)
        out_piece = out_piece.astype(F32)
        far_bias = swapped(up_bias)

        trade = lambda values, step: traded(values, step, n_items)
        at_once = lambda *values: lax.optimization_barrier(values)
        far_half = swapped(after(out_piece, down_piece))
        up0 = after(far_up, context)
        up4, up2 = trade(up0, 4), trade(up0, 2)
        down0 = after(far_down, up0)
        down4, down2 = trade(down0, 4), trade(down0, 2)
        up4, up2, down4, down2, far_half, far_context[0], far_bias = at_once(
            up4, up2, down4, down2, far_half, far_context[0], far_bias
        )
        up6, down6 = trade(up4, 2), trade(down4, 2)
        ups, downs = [up0, up4, up2], [down0, down4, down2]
        ups, downs = [[after(part, down4) for part in parts] for parts in (ups, downs)]
        up_beside = [trade(part, 1) for part in ups]
        down_beside = [trade(part, 1) for part in downs]
        other_half = trade(after(far_half, down4), 1)
        all_slots = lambda ks: jnp.stack([place ^ k ^ c for c in (0, 1) for k in ks]).astype(jnp.int32)
        slots = all_slots((6,))
        far_up, far_down = placed(all_slots((0, 4, 2)), ups + up_beside, downs + down_beside, group)
        up6, down6, far_context[1], far_context[2], far_up = at_once(
            up6, down6, far_context[1], far_context[2], far_up
        )
        ups, downs = [[part, trade(part, 1)] for part in (up6, down6)]
        which = core.astype(jnp.int32).reshape(1)

        split = width % (8 * n_items) == 0
        bits = tuple(range(1, n_items.bit_length() - 1))
        late_y = bits[1:2] + bits[:1] + bits[2:]
        mixed, d_pre, d_attn, sums, up_sums, *grads = feed(
            (bits, late_y) if split else None, which, slots, x, cotangent, context, far_context,
            out_weight, [far_half, other_half],
            [out_bias, norm1_gain, norm1_bias, down_bias, norm2_gain, norm2_bias, up_bias, far_bias],
            up_weight, down_weight, far_up, far_down, ups, downs,
        )

        def packed_of(grad_qv):
            return jnp.concatenate(
                [sums, up_sums.reshape(-1, width), grad_qv.reshape(-1, width)], axis=0
            )

        back = lambda d_attn: attend_back(
            (bits, late_y) if split else None, which, x, d_attn, out_weight, context, qkv_weight,
            order_rows, moved, probs,
        )
        if split:
            halving = lambda keep, send, order: Halving(keep, send, order, n_items).trade()
            down_sum, up_sum = halving(*grads[:2], bits), halving(*grads[2:], late_y)
            sent = arrived([down_sum, up_sum])
            down_sum.trade()
            up_sum.trade()
            part, grad_qv, *halves = back(after(d_attn, *sent))
            far_part = swapped(part)
            first, second = halving(*halves[:2], bits), halving(*halves[2:], late_y)
            sent = arrived([down_sum, up_sum], part)
            down_sum.trade()
            up_sum.trade()
            sent = arrived([first, second], *sent)
            first.extra = packed_of(grad_qv)
            first.extra = first.extra + traded(first.extra, 1, n_items)
            first.trade()
            second.trade()
            sums_all = [down_sum, up_sum, first, second]
            for _ in bits[2:]:
                arrived(sums_all)
                for one in sums_all[::-1]:
                    one.trade()
            summed_down, summed_up, *sent = arrived(sums_all)
            first.trade()
            second.trade()
            far_part = after(far_part, summed_down, summed_up, *sent)
            grad_inputs = (d_pre + part + far_part).astype(BF16)
            summed = arrived([first, second], grad_inputs)
            summed_rest = [summed[c // 2][c % 2] for c in range(4)]
            packed = first.extra
        else:
            part, grad_qv, grad_rest = back(d_attn)
            grad_inputs = (d_pre + part + swapped(part)).astype(BF16)
            summed_down = scattered(grads[0], n_items, 0)
            summed_up = scattered(grads[1], n_items, 0)
            summed_rest = scattered(grad_rest, n_items, 1)
            packed = all_sum(packed_of(grad_qv), n_items)
        small = packed[:8]
        up_small = packed[8 : 8 + units // width].reshape(units)
        qv_small = packed[8 + units // width :].reshape(2, local)
        return (
            mixed,
            grad_inputs,
            jnp.stack([summed_rest[c] for c in range(3)]),
            qv_small,
            summed_rest[3].T,
            small[5],
            small[3],
            small[4],
            summed_up,
            up_small,
            summed_down.T,
            small[2],
            small[0],
            small[1],
        )

    return body


def solution(mesh):
    return jax.shard_map(
        make_body(mesh.shape["items"]),
        mesh=mesh,
        in_specs=(
            P("items", None),
            P("heads", "items", None),
            P(None, None, "heads"),
            P(None, "heads"),
            P("heads", None),
            P(),
            P(),
            P(),
            P(None, "heads"),
            P("heads"),
            P("heads", None),
            P(),
            P(),
            P(),
            P("items", None),
        ),
        out_specs=(
            P("items", None),
            P("items", None),
            P(None, "items", "heads"),
            P(None, "heads"),
            P("heads", "items"),
            P(),
            P(),
            P(),
            P("items", "heads"),
            P("heads"),
            P("heads", "items"),
            P(),
            P(),
            P(),
        ),
        check_vma=False,
    )
```

```python
import functools

import jax
import jax.numpy as jnp
from jax import lax
from jax.experimental import pallas as pl
from jax.experimental.pallas import tpu as pltpu
from jax.sharding import PartitionSpec as P

HEAD_DIM = 64
CLUSTER = 128
SCALE = HEAD_DIM**-0.5
EPSILON = 1e-05
ROW_TILE = 256
GRAD_TILE = 512
UNIT_TILE = 1536
BF16 = jnp.bfloat16
F32 = jnp.float32


def dot(left, right):
    return jnp.dot(left, right, preferred_element_type=F32)


def dot_nt(left, right):
    return lax.dot_general(left, right, (((1,), (1,)), ((), ())), preferred_element_type=F32)


def dot_tn(left, right):
    return lax.dot_general(left, right, (((0,), (0,)), ((), ())), preferred_element_type=F32)


def dot_tt(left, right):
    return lax.dot_general(left, right, (((0,), (1,)), ((), ())), preferred_element_type=F32)


def params_of(mib):
    return pltpu.CompilerParams(vmem_limit_bytes=mib * 1024 * 1024)


def cost(flops, bytes_accessed):
    return pl.CostEstimate(flops=int(flops) // 1000, bytes_accessed=int(bytes_accessed) // 1000, transcendentals=0)


def shape(dims, dtype):
    return jax.ShapeDtypeStruct(dims, dtype)


def whole(*dims):
    return pl.BlockSpec(dims, lambda *_: (0,) * len(dims), pipeline_mode=pl.Buffered(1))


def swapped(values):
    return lax.ppermute(values, "heads", [(0, 1), (1, 0)])


def traded(values, step, n_items):
    return lax.ppermute(values, "items", [(i, i ^ step) for i in range(n_items)])


def all_sum(values, n_items):
    step = 1
    while step < n_items:
        values = values + traded(values, step, n_items)
        step *= 2
    return values


def scattered(values, n_items, axis):
    item = lax.axis_index("items")
    size = n_items
    for bit in range(n_items.bit_length() - 1):
        dims = values.shape
        size //= 2
        halves = values.reshape(dims[:axis] + (size, 2, dims[axis] // (2 * size)) + dims[axis + 1 :])
        mine = (item >> bit) & 1
        send = lax.dynamic_index_in_dim(halves, 1 - mine, axis + 1, keepdims=False)
        keep = lax.dynamic_index_in_dim(halves, mine, axis + 1, keepdims=False)
        values = keep + traded(send, 1 << bit, n_items)
        values = values.reshape(dims[:axis] + (-1,) + dims[axis + 1 :])
    return values


class Halving:
    def __init__(self, keep, send, order, n_items):
        self.order, self.n_items, self.rest = list(order), n_items, keep.shape[1:]
        self.terms = []
        self.hold(keep)
        self.send, self.extra, self.bit = send, None, 0

    def hold(self, values):
        self.terms.append((values.reshape((2,) * len(self.order) + self.rest), []))

    def part(self, term, places):
        values, settled = term
        starts = settled + places
        sizes = (1,) * len(starts) + values.shape[len(starts) :]
        starts = starts + [0] * (values.ndim - len(starts))
        return lax.dynamic_slice(values, starts, sizes).reshape((-1,) + self.rest)

    def trade(self):
        self.got = traded(self.send, 1 << self.bit, self.n_items)
        if self.extra is not None:
            self.more = traded(self.extra, 1 << self.bit, self.n_items)
        return self

    def add(self):
        self.hold(self.got)
        if self.extra is not None:
            self.extra = self.extra + self.more
        if not self.order:
            return sum(self.part(term, []) for term in self.terms).reshape(self.rest)
        self.bit = self.order.pop(0)
        mine = (lax.axis_index("items") >> self.bit) & 1
        self.send = sum(self.part(term, [1 - mine]) for term in self.terms)
        self.terms = [(values, settled + [mine]) for values, settled in self.terms]
        return self.send


def arrived(sums, *before):
    got = [one.got for one in sums] + [one.more for one in sums if one.extra is not None]
    got = list(lax.optimization_barrier(tuple(got) + before))
    for one in sums:
        one.got = got.pop(0)
    for one in sums:
        if one.extra is not None:
            one.more = got.pop(0)
    return [one.add() for one in sums]


def after(values, *others):
    return lax.optimization_barrier((values,) + others)[0]


def selector(row_ref, h, sel_ref, slot):
    rows = sel_ref.shape[1]
    step = 256
    for r in range(0, rows, step):
        subs = lax.broadcasted_iota(jnp.int32, (step, rows), 0) + r
        found = jnp.where(row_ref[0, h : h + 1, :] == subs, 1.0, 0.0)
        sel_ref[slot, r : r + step, :] = found.astype(BF16)


def spans_of(rows):
    return [slice(c, c + CLUSTER) for c in range(0, rows, CLUSTER)]


def attend_kernel(x_ref, w_ref, bias_ref, row_ref, ctx_ref, moved_ref, probs_ref, sel_ref):
    rows = x_ref.shape[0]
    spans = spans_of(rows)
    for h in range(2):
        selector(row_ref, h, sel_ref, h)
    weight = jnp.concatenate([w_ref[c] for c in range(3)], axis=1)
    flat = dot_tt(weight, x_ref[...])
    parts = [flat[:128] + bias_ref[:, 0:1], flat[128:256], flat[256:] + bias_ref[:, 1:2]]
    parts = [part.astype(BF16) for part in parts]
    for h in range(2):
        cut = slice(h * HEAD_DIM, (h + 1) * HEAD_DIM)
        qkv = jnp.concatenate([part[cut] for part in parts], axis=0)
        moved = dot(qkv, sel_ref[h]).astype(BF16)
        moved_ref[h] = moved
        query, key, value = moved[:HEAD_DIM], moved[HEAD_DIM : 2 * HEAD_DIM], moved[2 * HEAD_DIM :]
        scores = jnp.concatenate([dot_tn(query[:, s], key[:, s]) for s in spans], axis=0) * SCALE
        shifted = jnp.exp(scores - jnp.max(scores, axis=-1, keepdims=True))
        probs = shifted / jnp.sum(shifted, axis=-1, keepdims=True)
        probs_b = probs.astype(BF16)
        probs_ref[h] = probs_b
        mixed = jnp.concatenate([dot_nt(value[:, s], probs_b[s]) for s in spans], axis=1)
        context = dot_nt(mixed.astype(BF16), sel_ref[h])
        ctx_ref[cut, :] = context.astype(BF16)


def attend(x, weight, bias_cols, order_rows):
    rows, width = x.shape
    pairs = order_rows.shape[0]
    local = weight.shape[2]
    return pl.pallas_call(
        attend_kernel,
        grid=(pairs,),
        in_specs=[
            whole(rows, width),
            pl.BlockSpec((3, width, 128), lambda p: (0, 0, p)),
            pl.BlockSpec((128, 2), lambda p: (p, 0)),
            pl.BlockSpec((1, 2, rows), lambda p: (p, 0, 0)),
        ],
        out_specs=[
            pl.BlockSpec((128, rows), lambda p: (p, 0)),
            pl.BlockSpec((2, 3 * HEAD_DIM, rows), lambda p: (p, 0, 0)),
            pl.BlockSpec((2, rows, CLUSTER), lambda p: (p, 0, 0)),
        ],
        out_shape=[
            shape((local, rows), BF16),
            shape((2 * pairs, 3 * HEAD_DIM, rows), BF16),
            shape((2 * pairs, rows, CLUSTER), BF16),
        ],
        scratch_shapes=[pltpu.VMEM((2, rows, rows), BF16)],
        compiler_params=params_of(40),
        cost_estimate=cost(12e9, 12e6),
        name="attend",
    )(x, weight, bias_cols, order_rows)


def block_place(j, order):
    place = 0
    for bit in order:
        place = 2 * place + ((j >> bit) & 1)
    return place


def write_halves(values, keep_ref, send_ref, mine, order, at):
    blocks = 2 ** (len(order) + 1)
    rows = values.shape[0] // blocks
    for j in range(0, blocks, 2):
        even, odd = values[j * rows : (j + 1) * rows], values[(j + 1) * rows : (j + 2) * rows]
        place = (block_place(j, order),) + at
        keep_ref[place] = jnp.where(mine == 0, even, odd)
        send_ref[place] = jnp.where(mine == 0, odd, even)


def attend_back_kernel(
    orders, core_ref, x_ref, da_ref, ow_ref, ctx_ref, w_ref, row_ref, moved_ref, probs_ref, part_ref, bias_ref, *refs
):
    *grad_refs, sel_ref = refs
    rows = da_ref.shape[0]
    spans = spans_of(rows)
    for h in range(2):
        selector(row_ref, h, sel_ref, h)
    d_attn = da_ref[...]
    d_context = dot_nt(ow_ref[...], d_attn).astype(BF16)
    d_out = dot_tt(d_attn, ctx_ref[...])
    found = []
    for h in range(2):
        d_moved = dot(d_context[h * HEAD_DIM : (h + 1) * HEAD_DIM], sel_ref[h]).astype(BF16)
        moved = moved_ref[h]
        query, key, value = moved[:HEAD_DIM], moved[HEAD_DIM : 2 * HEAD_DIM], moved[2 * HEAD_DIM :]
        probs_b = probs_ref[h]
        probs = probs_b.astype(F32)
        d_value = jnp.concatenate([dot(d_moved[:, s], probs_b[s]) for s in spans], axis=1)
        d_probs = jnp.concatenate([dot_tn(d_moved[:, s], value[:, s]) for s in spans], axis=0)
        inner = jnp.sum(probs * d_probs, axis=-1, keepdims=True)
        d_scores = (probs * (d_probs - inner)).astype(BF16)
        d_query = jnp.concatenate([dot_nt(key[:, s], d_scores[s]) for s in spans], axis=1) * SCALE
        d_key = jnp.concatenate([dot(query[:, s], d_scores[s]) for s in spans], axis=1) * SCALE
        three = jnp.concatenate([d_query, d_key, d_value], axis=0).astype(BF16)
        found.append(dot_nt(three, sel_ref[h]).astype(BF16))
    d_qkv = jnp.concatenate(
        [f[c * HEAD_DIM : (c + 1) * HEAD_DIM] for c in range(3) for f in found], axis=0
    )
    sums = dot_nt(jnp.ones((8, rows), BF16), d_qkv)
    bias_ref[0:1, :] = sums[0:1, :128]
    bias_ref[1:2, :] = sums[0:1, 256:]
    grads = dot_tt(x_ref[...], d_qkv)
    for c in range(4):
        values = grads[:, c * 128 : (c + 1) * 128] if c < 3 else d_out
        if orders:
            write_halves(values, *grad_refs[c // 2 * 2 :][:2], core_ref[0], orders[c // 2], (c % 2,))
        else:
            grad_refs[0][c] = values
    part = dot_tt(d_qkv, jnp.concatenate([w_ref[c] for c in range(3)], axis=1))

    @pl.when(pl.program_id(0) == 0)
    def _():
        part_ref[...] = part

    @pl.when(pl.program_id(0) > 0)
    def _():
        part_ref[...] += part


def attend_back(orders, core, x, d_attn, out_weight, context, weight, order_rows, moved, probs):
    rows, width = x.shape
    local = weight.shape[2]
    pairs = order_rows.shape[0]
    if orders:
        blocks = 2 ** len(orders[0])
        height = width // (2 * blocks)
        grad_specs = [pl.BlockSpec((blocks, 2, height, 128), lambda p: (0, 0, 0, p))] * 4
        grad_shapes = [shape((blocks, 2, height, local), F32)] * 4
    else:
        grad_specs = [pl.BlockSpec((4, width, 128), lambda p: (0, 0, p))]
        grad_shapes = [shape((4, width, local), F32)]
    return pl.pallas_call(
        functools.partial(attend_back_kernel, orders),
        grid=(pairs,),
        in_specs=[
            pl.BlockSpec(memory_space=pltpu.SMEM),
            whole(rows, width),
            whole(rows, width),
            pl.BlockSpec((128, width), lambda p: (p, 0)),
            pl.BlockSpec((128, rows), lambda p: (p, 0)),
            pl.BlockSpec((3, width, 128), lambda p: (0, 0, p)),
            pl.BlockSpec((1, 2, rows), lambda p: (p, 0, 0)),
            pl.BlockSpec((2, 3 * HEAD_DIM, rows), lambda p: (p, 0, 0)),
            pl.BlockSpec((2, rows, CLUSTER), lambda p: (p, 0, 0)),
        ],
        out_specs=[
            pl.BlockSpec((rows, width), lambda p: (0, 0)), pl.BlockSpec((2, 128), lambda p: (0, p)), *grad_specs
        ],
        out_shape=[shape((rows, width), F32), shape((2, local), F32), *grad_shapes],
        scratch_shapes=[pltpu.VMEM((2, rows, rows), BF16)],
        compiler_params=params_of(30),
        cost_estimate=cost(20e9, 20e6),
        name="attend_back",
    )(core, x, d_attn, out_weight, context, weight, order_rows, moved, probs)


def gelu_both(hidden):
    scale = 0.7978845608028654
    square = hidden * hidden
    bent = jnp.tanh(hidden * (scale + (scale * 0.044715) * square))
    half = 0.5 + 0.5 * bent
    active = hidden * half
    slope = half + 0.5 * hidden * (1.0 - bent * bent) * (scale + (3 * scale * 0.044715) * square)
    return active.astype(BF16), slope.astype(BF16)


def normalized(values):
    centred = values - jnp.mean(values, axis=-1, keepdims=True)
    factor = lax.rsqrt(jnp.mean(centred * centred, axis=-1, keepdims=True) + EPSILON)
    return centred * factor, factor


def norm_back(grad, unit, factor):
    mean = jnp.mean(grad, axis=-1, keepdims=True)
    inner = jnp.mean(grad * unit, axis=-1, keepdims=True)
    return factor * (grad - mean - unit * inner)


def unit_cuts(units):
    return [slice(u, u + UNIT_TILE) for u in range(0, units, UNIT_TILE)]


def narrow_copies(parts, stage, sems, places, up_out, down_out):
    rows, width = stage.shape[1], down_out.shape[1]
    copies = [
        pltpu.make_async_copy(part.at[0], stage.at[k], sems.at[k]) for k, part in enumerate(parts)
    ]

    def start():
        for copy in copies:
            copy.start()

    def finish():
        count = len(copies) // 2
        for k, copy in enumerate(copies):
            copy.wait()
            if k < count:
                place = pl.multiple_of(places[k] * rows, rows)
                up_out[pl.ds(place, rows), :] = stage[k].astype(BF16)
            else:
                for side in range(2):
                    place = pl.multiple_of((places[k - count] * 2 + side) * rows, rows)
                    cut = slice(side * width, (side + 1) * width)
                    down_out[pl.ds(place, rows), :] = stage[k, :, cut].astype(BF16)

    return start, finish


def placed_kernel(slots_ref, *refs):
    *parts, up_ref, down_ref, stage, sems = refs
    places = [slots_ref[k] for k in range(len(parts) // 2)]
    start, finish = narrow_copies(parts, stage, sems, places, up_ref, down_ref)
    start()
    finish()


def placed(slots, parts, group):
    _, rows, units = parts[0].shape
    width = units // 2
    dims = [(group * rows, units), (2 * group * rows, width)]
    return pl.pallas_call(
        placed_kernel,
        grid=(1,),
        in_specs=[pl.BlockSpec(memory_space=pltpu.SMEM)]
        + [pl.BlockSpec(memory_space=pl.ANY)] * len(parts),
        out_specs=[whole(*out) for out in dims],
        out_shape=[shape(out, BF16) for out in dims],
        scratch_shapes=[
            pltpu.VMEM((len(parts),) + parts[0].shape[1:], F32), pltpu.SemaphoreType.DMA((len(parts),))
        ],
        compiler_params=params_of(56),
        cost_estimate=cost(1e6, 1e6),
        name="placed",
    )(slots, *parts)


def feed_rows(
    x_ref, cot_ref, ctx_ref, far_ctx_refs, vector_refs, ready, out_s, far_out_s, up_s, down_s, far_up_s, far_down_s,
    mixed_ref, d_pre_ref, d_attn_ref, sums_ref, up_sums_ref, nb_s, act_s, d_feed_s, d_hidden_s, here,
):
    units = up_s.shape[1]
    row = lambda ref: ref[...].reshape(1, ref.shape[0])
    out_bias, gain1, bias1, down_bias, gain2, bias2, up_bias, far_bias = map(row, vector_refs)
    ready("out")
    attention = dot_tn(ctx_ref[...], out_s[...])
    far_ctx = jnp.concatenate([ref[...].astype(BF16) for ref in far_ctx_refs], axis=0)
    attention += dot_tn(far_ctx, far_out_s[...])
    unit1, factor1 = normalized(x_ref[...].astype(F32) + attention + out_bias)
    normed = unit1 * gain1 + bias1
    nb = normed.astype(BF16)
    nb_s[here, :] = nb
    total = normed + down_bias
    slopes, far_slopes = [], []
    ready("near")
    for cut in unit_cuts(units):
        active, slope = gelu_both(dot(nb, up_s[:, cut]) + up_bias[:, cut])
        act_s[here, cut] = active
        slopes.append(slope)
        total = total + dot(active, down_s[cut, :])
    ready("far")
    for cut in unit_cuts(units):
        far_active, far_slope = gelu_both(dot(nb, far_up_s[:, cut]) + far_bias[:, cut])
        far_slopes.append(far_slope)
        total = total + dot(far_active, far_down_s[cut, :])
    unit2, factor2 = normalized(total)
    mixed_ref[...] = (unit2 * gain2 + bias2).astype(BF16)
    grad = cot_ref[...].astype(F32)
    sums_ref[0:1, :] += jnp.sum(grad * unit2, axis=0, keepdims=True)
    sums_ref[1:2, :] += jnp.sum(grad, axis=0, keepdims=True)
    d_sum = norm_back(grad * gain2, unit2, factor2)
    d_feed = d_sum.astype(BF16)
    d_feed_s[here, :] = d_feed
    sums_ref[2:3, :] += jnp.sum(d_feed.astype(F32), axis=0, keepdims=True)
    d_normed = d_sum
    for cut, slope, far_slope in zip(unit_cuts(units), slopes, far_slopes):
        d_active = dot_nt(d_feed, down_s[cut, :])
        d_hidden = (d_active * slope.astype(F32)).astype(BF16)
        d_hidden_s[here, cut] = d_hidden
        up_sums_ref[:, cut] += jnp.sum(d_hidden.astype(F32), axis=0, keepdims=True)
        far_d_active = dot_nt(d_feed, far_down_s[cut, :])
        far_d_hidden = (far_d_active * far_slope.astype(F32)).astype(BF16)
        d_normed = d_normed + dot_nt(d_hidden, up_s[:, cut])
        d_normed = d_normed + dot_nt(far_d_hidden, far_up_s[:, cut])
    sums_ref[3:4, :] += jnp.sum(d_normed * unit1, axis=0, keepdims=True)
    sums_ref[4:5, :] += jnp.sum(d_normed, axis=0, keepdims=True)
    d_pre = norm_back(d_normed * gain1, unit1, factor1)
    d_pre_ref[...] = d_pre
    d_attn = d_pre.astype(BF16)
    d_attn_ref[...] = d_attn
    sums_ref[5:6, :] += jnp.sum(d_attn.astype(F32), axis=0, keepdims=True)


def feed_kernel(
    orders, tiles, late_count, core_ref, slots_ref, x_ref, cot_ref, ctx_ref, far0_ref, far1_ref, *refs
):
    vector_refs, refs = refs[:8], refs[8:]
    out_hbm, near_half_hbm, far_half_hbm, up_hbm, down_hbm, far_up_hbm, far_down_hbm, *refs = refs
    late_parts, refs = refs[:late_count], refs[late_count:]
    mixed_ref, d_pre_ref, d_attn_ref, sums_ref, up_sums_ref, *refs = refs
    count = 4 if orders else 2
    grad_refs, refs = refs[:count], refs[count:]
    nb_s, act_s, d_feed_s, d_hidden_s, out_s, far_out_s, up_s, down_s, far_up_s, far_down_s, *refs = refs
    half_stage, late_stage, sems, late_sems = refs
    step = pl.program_id(0)
    tile = x_ref.shape[0]
    copies = [
        pltpu.make_async_copy(source, target, sems.at[k])
        for k, (source, target) in enumerate((
            (out_hbm, out_s), (near_half_hbm, half_stage.at[0]), (far_half_hbm, half_stage.at[1]),
            (up_hbm, up_s), (down_hbm, down_s), (far_up_hbm, far_up_s), (far_down_hbm, far_down_s),
        ))
    ]
    places = [slots_ref[k] for k in range(late_count // 2)]
    start_late, finish_late = narrow_copies(
        late_parts, late_stage, late_sems, places, far_up_s, far_down_s
    )

    def ready(what):
        @pl.when(step == 0)
        def _():
            if what == "out":
                for copy in copies:
                    copy.start()
                start_late()
                sums_ref[...] = jnp.zeros_like(sums_ref)
                up_sums_ref[...] = jnp.zeros_like(up_sums_ref)
                for copy in copies[:3]:
                    copy.wait()
                half = half_stage.shape[1]
                for k in range(2):
                    place = pl.multiple_of((core_ref[0] ^ k) * half, half)
                    far_out_s[pl.ds(place, half), :] = half_stage[k].astype(BF16)
            elif what == "near":
                for copy in copies[3:5]:
                    copy.wait()
            else:
                for copy in copies[5:]:
                    copy.wait()
                finish_late()

    @pl.when(step < tiles)
    def _():
        here = pl.ds(pl.multiple_of(step * tile, tile), tile)
        feed_rows(
            x_ref, cot_ref, ctx_ref, (far0_ref, far1_ref), vector_refs, ready, out_s, far_out_s, up_s,
            down_s, far_up_s, far_down_s, mixed_ref, d_pre_ref, d_attn_ref, sums_ref, up_sums_ref, nb_s, act_s,
            d_feed_s, d_hidden_s, here,
        )

    @pl.when(step >= tiles)
    def _():
        there = pl.ds(pl.multiple_of((step - tiles) * GRAD_TILE, GRAD_TILE), GRAD_TILE)
        d_down = dot_tn(d_feed_s[...], act_s[:, there])
        d_up = dot_tn(nb_s[...], d_hidden_s[:, there])
        if orders:
            write_halves(d_down, *grad_refs[:2], core_ref[0], orders[0], ())
            write_halves(d_up, *grad_refs[2:], core_ref[0], orders[1], ())
        else:
            grad_refs[0][...] = d_down
            grad_refs[1][...] = d_up


def feed(
    orders, core, slots, x, cotangent, context, far_context, out_weight, halves, vectors, up, down, far_up, far_down,
    late,
):
    rows, width = x.shape
    local, units = out_weight.shape[0], up.shape[1]
    tile = ROW_TILE
    tiles = rows // tile
    across = lambda cols: pl.BlockSpec((tile, cols), lambda i: (jnp.minimum(i, tiles - 1), 0))
    along = lambda height: pl.BlockSpec((height, tile), lambda i: (0, jnp.minimum(i, tiles - 1)))
    if orders:
        blocks = 2 ** len(orders[0])
        height = width // (2 * blocks)
        grad_specs = [
            pl.BlockSpec((blocks, height, GRAD_TILE), lambda i: (0, 0, jnp.maximum(i - tiles, 0)))
        ] * 4
        grad_shapes = [shape((blocks, height, units), F32)] * 4
    else:
        grad_specs = [pl.BlockSpec((width, GRAD_TILE), lambda i: (0, jnp.maximum(i - tiles, 0)))] * 2
        grad_shapes = [shape((width, units), F32)] * 2
    scalars = pl.BlockSpec(memory_space=pltpu.SMEM)
    anywhere = pl.BlockSpec(memory_space=pl.ANY)
    return pl.pallas_call(
        functools.partial(feed_kernel, orders, tiles, len(late)),
        grid=(tiles + units // GRAD_TILE,),
        in_specs=[
            scalars, scalars, across(width), across(width), along(local),
            *[along(part.shape[0]) for part in far_context], *[whole(v.shape[0]) for v in vectors],
            *[anywhere] * (7 + len(late)),
        ],
        out_specs=[
            across(width), across(width), across(width), whole(8, width), whole(1, units),
            *grad_specs,
        ],
        out_shape=[
            shape((rows, width), BF16), shape((rows, width), F32), shape((rows, width), BF16),
            shape((8, width), F32), shape((1, units), F32), *grad_shapes,
        ],
        scratch_shapes=[
            pltpu.VMEM((rows, width), BF16), pltpu.VMEM((rows, units), BF16), pltpu.VMEM((rows, width), BF16),
            pltpu.VMEM((rows, units), BF16),
            pltpu.VMEM((local, width), BF16), pltpu.VMEM((local, width), BF16),
            pltpu.VMEM((width, units), BF16), pltpu.VMEM((units, width), BF16),
            pltpu.VMEM((width, units), BF16), pltpu.VMEM((units, width), BF16),
            pltpu.VMEM((2,) + halves[0].shape, F32), pltpu.VMEM((len(late),) + late[0].shape[1:], F32),
            pltpu.SemaphoreType.DMA((7,)), pltpu.SemaphoreType.DMA((len(late),)),
        ],
        compiler_params=params_of(56),
        cost_estimate=cost(25e9, 30e6),
        name="feed",
    )(
        core, slots, x, cotangent, context, *far_context, *vectors, out_weight, *halves, up, down,
        far_up, far_down, *late,
    )


def make_body(n_items):
    def body(
        hidden_in,
        cluster_order,
        qkv_weight,
        qv_bias,
        out_weight,
        out_bias,
        norm1_gain,
        norm1_bias,
        up_weight,
        up_bias,
        down_weight,
        down_bias,
        norm2_gain,
        norm2_bias,
        cotangent,
    ):
        rows, width = hidden_in.shape
        units = up_weight.shape[1]
        local = out_weight.shape[0]
        item = lax.axis_index("items")
        core = item & 1
        group = 8
        place = item % group

        def piece(values):
            count = values.shape[0] // group
            return lax.dynamic_slice_in_dim(values, place * count, count, 0).astype(F32)[None]

        up_piece = piece(up_weight)
        two_rows = piece(after(down_weight, up_piece))
        middle = two_rows.shape[1] // 2
        down_piece = jnp.concatenate([two_rows[:, :middle], two_rows[:, middle:]], axis=2)
        far_a = swapped(up_piece)
        far_b = swapped(down_piece)
        far_bias = swapped(up_bias)
        half = local // 2

        ordering = cluster_order[:, 0, :]
        order_rows = ordering.reshape(-1, 2, rows)
        x = after(hidden_in, up_piece, down_piece)
        context, moved, probs = attend(x, qkv_weight, qv_bias.T, order_rows)
        pairs = order_rows.shape[0]
        far_context = [
            swapped(context[:128].astype(F32)), swapped(context[128:].astype(F32))
        ]
        out_piece = lax.dynamic_slice_in_dim(out_weight, core * half, half, 0).astype(F32)

        trade = lambda values, step: traded(values, step, n_items)
        at_once = lambda *values: lax.optimization_barrier(values)
        a0 = after(far_a, context)
        a4, a2 = trade(a0, 4), trade(a0, 2)
        b0 = after(far_b, a0)
        far_half = swapped(after(out_piece, b0))
        b4, b2 = trade(b0, 4), trade(b0, 2)
        a4, a2, far_context[0], _ = at_once(a4, a2, far_context[0], b0)
        a6 = trade(a4, 2)
        b4, b2, far_half, _ = at_once(b4, b2, far_half, a4)
        b6 = trade(b4, 2)
        all_slots = lambda ks: jnp.stack([place ^ k for k in ks]).astype(jnp.int32)
        come = [part for one in ((a0, a4, a2), (b0, b4, b2)) for part in (*one, *(trade(p, 1) for p in one))]
        far_up, far_down = placed(all_slots((0, 4, 2, 1, 5, 3)), come, group)
        a6, b6, far_context[1], far_bias, far_up = at_once(
            a6, b6, far_context[1], far_bias, far_up
        )
        other_half = trade(far_half, 1)
        late, slots = [a6, trade(a6, 1), b6, trade(b6, 1)], all_slots((6, 7))
        which = core.astype(jnp.int32).reshape(1)

        split = width % (8 * n_items) == 0
        bits = tuple(range(1, n_items.bit_length() - 1))
        late_y = bits[1:2] + bits[:1] + bits[2:]
        mixed, d_pre, d_attn, sums, up_sums, *grads = feed(
            (bits, late_y) if split else None, which, slots, x, cotangent, context, far_context,
            out_weight, [far_half, other_half],
            [out_bias, norm1_gain, norm1_bias, down_bias, norm2_gain, norm2_bias, up_bias, far_bias],
            up_weight, down_weight, far_up, far_down, late,
        )

        def packed_of(grad_qv):
            return jnp.concatenate(
                [sums, up_sums.reshape(-1, width), grad_qv.reshape(-1, width)], axis=0
            )

        back = lambda d_attn: attend_back(
            (bits, late_y) if split else None, which, x, d_attn, out_weight, context, qkv_weight,
            order_rows, moved, probs,
        )
        if split:
            halving = lambda keep, send, order: Halving(keep, send, order, n_items).trade()
            down_sum, up_sum = halving(*grads[:2], bits), halving(*grads[2:], late_y)
            sent = arrived([down_sum, up_sum])
            down_sum.trade()
            up_sum.trade()
            part, grad_qv, *halves = back(after(d_attn, *sent))
            far_part = swapped(part)
            first, second = halving(*halves[:2], bits), halving(*halves[2:], late_y)
            sent = arrived([down_sum, up_sum], part)
            down_sum.trade()
            up_sum.trade()
            sent = arrived([first, second], *sent)
            first.extra = packed_of(grad_qv)
            first.extra = first.extra + traded(first.extra, 1, n_items)
            first.trade()
            second.trade()
            sums_all = [down_sum, up_sum, first, second]
            for _ in bits[2:]:
                arrived(sums_all)
                for one in sums_all[::-1]:
                    one.trade()
            summed_down, summed_up, *sent = arrived(sums_all)
            first.trade()
            second.trade()
            far_part = after(far_part, summed_down, summed_up, *sent)
            grad_inputs = (d_pre + part + far_part).astype(BF16)
            summed = arrived([first, second], grad_inputs)
            summed_rest = [summed[c // 2][c % 2] for c in range(4)]
            packed = first.extra
        else:
            part, grad_qv, grad_rest = back(d_attn)
            grad_inputs = (d_pre + part + swapped(part)).astype(BF16)
            summed_down = scattered(grads[0], n_items, 0)
            summed_up = scattered(grads[1], n_items, 0)
            summed_rest = scattered(grad_rest, n_items, 1)
            packed = all_sum(packed_of(grad_qv), n_items)
        small = packed[:8]
        up_small = packed[8 : 8 + units // width].reshape(units)
        qv_small = packed[8 + units // width :].reshape(2, local)
        return (
            mixed,
            grad_inputs,
            jnp.stack([summed_rest[c] for c in range(3)]),
            qv_small,
            summed_rest[3].T,
            small[5],
            small[3],
            small[4],
            summed_up,
            up_small,
            summed_down.T,
            small[2],
            small[0],
            small[1],
        )

    return body


def solution(mesh):
    return jax.shard_map(
        make_body(mesh.shape["items"]),
        mesh=mesh,
        in_specs=(
            P("items", None),
            P("heads", "items", None),
            P(None, None, "heads"),
            P(None, "heads"),
            P("heads", None),
            P(),
            P(),
            P(),
            P(None, "heads"),
            P("heads"),
            P("heads", None),
            P(),
            P(),
            P(),
            P("items", None),
        ),
        out_specs=(
            P("items", None),
            P("items", None),
            P(None, "items", "heads"),
            P(None, "heads"),
            P("heads", "items"),
            P(),
            P(),
            P(),
            P("items", "heads"),
            P("heads"),
            P("heads", "items"),
            P(),
            P(),
            P(),
        ),
        check_vma=False,
    )
```

```python
import functools

import jax
import jax.numpy as jnp
from jax import lax
from jax.experimental import pallas as pl
from jax.experimental.pallas import tpu as pltpu
from jax.sharding import PartitionSpec as P

HEAD_DIM = 64
CLUSTER = 128
SCALE = HEAD_DIM**-0.5
EPSILON = 1e-05
ROW_TILE = 256
GRAD_TILE = 512
UNIT_TILE = 1536
BF16 = jnp.bfloat16
F32 = jnp.float32


def dot(left, right):
    return jnp.dot(left, right, preferred_element_type=F32)


def dot_nt(left, right):
    return lax.dot_general(left, right, (((1,), (1,)), ((), ())), preferred_element_type=F32)


def dot_tn(left, right):
    return lax.dot_general(left, right, (((0,), (0,)), ((), ())), preferred_element_type=F32)


def dot_tt(left, right):
    return lax.dot_general(left, right, (((0,), (1,)), ((), ())), preferred_element_type=F32)


def params_of(mib):
    return pltpu.CompilerParams(vmem_limit_bytes=mib * 1024 * 1024)


def cost(flops, bytes_accessed):
    return pl.CostEstimate(flops=int(flops) // 1000, bytes_accessed=int(bytes_accessed) // 1000, transcendentals=0)


def shape(dims, dtype):
    return jax.ShapeDtypeStruct(dims, dtype)


def whole(*dims):
    return pl.BlockSpec(dims, lambda *_: (0,) * len(dims), pipeline_mode=pl.Buffered(1))


def swapped(values):
    return lax.ppermute(values, "heads", [(0, 1), (1, 0)])


def traded(values, step, n_items):
    return lax.ppermute(values, "items", [(i, i ^ step) for i in range(n_items)])


def all_sum(values, n_items):
    step = 1
    while step < n_items:
        values = values + traded(values, step, n_items)
        step *= 2
    return values


def scattered(values, n_items, axis):
    item = lax.axis_index("items")
    size = n_items
    for bit in range(n_items.bit_length() - 1):
        dims = values.shape
        size //= 2
        halves = values.reshape(dims[:axis] + (size, 2, dims[axis] // (2 * size)) + dims[axis + 1 :])
        mine = (item >> bit) & 1
        send = lax.dynamic_index_in_dim(halves, 1 - mine, axis + 1, keepdims=False)
        keep = lax.dynamic_index_in_dim(halves, mine, axis + 1, keepdims=False)
        values = keep + traded(send, 1 << bit, n_items)
        values = values.reshape(dims[:axis] + (-1,) + dims[axis + 1 :])
    return values


class Halving:
    def __init__(self, keep, send, order, n_items):
        self.order, self.n_items, self.rest = list(order), n_items, keep.shape[1:]
        self.terms = []
        self.hold(keep)
        self.send, self.extra, self.bit = send, None, 0

    def hold(self, values):
        self.terms.append((values.reshape((2,) * len(self.order) + self.rest), []))

    def part(self, term, places):
        values, settled = term
        starts = settled + places
        sizes = (1,) * len(starts) + values.shape[len(starts) :]
        starts = starts + [0] * (values.ndim - len(starts))
        return lax.dynamic_slice(values, starts, sizes).reshape((-1,) + self.rest)

    def trade(self):
        self.got = traded(self.send, 1 << self.bit, self.n_items)
        if self.extra is not None:
            self.more = traded(self.extra, 1 << self.bit, self.n_items)
        return self

    def add(self):
        self.hold(self.got)
        if self.extra is not None:
            self.extra = self.extra + self.more
        if not self.order:
            return sum(self.part(term, []) for term in self.terms).reshape(self.rest)
        self.bit = self.order.pop(0)
        mine = (lax.axis_index("items") >> self.bit) & 1
        self.send = sum(self.part(term, [1 - mine]) for term in self.terms)
        self.terms = [(values, settled + [mine]) for values, settled in self.terms]
        return self.send


def arrived(sums, *before):
    got = [one.got for one in sums] + [one.more for one in sums if one.extra is not None]
    got = list(lax.optimization_barrier(tuple(got) + before))
    for one in sums:
        one.got = got.pop(0)
    for one in sums:
        if one.extra is not None:
            one.more = got.pop(0)
    return [one.add() for one in sums]


def after(values, *others):
    return lax.optimization_barrier((values,) + others)[0]


def selector(row_ref, h, sel_ref, slot):
    rows = sel_ref.shape[1]
    step = 256
    for r in range(0, rows, step):
        subs = lax.broadcasted_iota(jnp.int32, (step, rows), 0) + r
        found = jnp.where(row_ref[0, h : h + 1, :] == subs, 1.0, 0.0)
        sel_ref[slot, r : r + step, :] = found.astype(BF16)


def spans_of(rows):
    return [slice(c, c + CLUSTER) for c in range(0, rows, CLUSTER)]


def attend_kernel(x_ref, w_ref, bias_ref, row_ref, ctx_ref, moved_ref, probs_ref, sel_ref):
    rows = x_ref.shape[0]
    spans = spans_of(rows)
    for h in range(2):
        selector(row_ref, h, sel_ref, h)
    weight = jnp.concatenate([w_ref[c] for c in range(3)], axis=1)
    flat = dot_tt(weight, x_ref[...])
    parts = [flat[:128] + bias_ref[:, 0:1], flat[128:256], flat[256:] + bias_ref[:, 1:2]]
    parts = [part.astype(BF16) for part in parts]
    for h in range(2):
        cut = slice(h * HEAD_DIM, (h + 1) * HEAD_DIM)
        qkv = jnp.concatenate([part[cut] for part in parts], axis=0)
        moved = dot(qkv, sel_ref[h]).astype(BF16)
        moved_ref[h] = moved
        query, key, value = moved[:HEAD_DIM], moved[HEAD_DIM : 2 * HEAD_DIM], moved[2 * HEAD_DIM :]
        scores = jnp.concatenate([dot_tn(query[:, s], key[:, s]) for s in spans], axis=0) * SCALE
        shifted = jnp.exp(scores - jnp.max(scores, axis=-1, keepdims=True))
        probs = shifted / jnp.sum(shifted, axis=-1, keepdims=True)
        probs_b = probs.astype(BF16)
        probs_ref[h] = probs_b
        mixed = jnp.concatenate([dot_nt(value[:, s], probs_b[s]) for s in spans], axis=1)
        context = dot_nt(mixed.astype(BF16), sel_ref[h])
        ctx_ref[cut, :] = context.astype(BF16)


def attend(x, weight, bias_cols, order_rows):
    rows, width = x.shape
    pairs = order_rows.shape[0]
    local = weight.shape[2]
    return pl.pallas_call(
        attend_kernel,
        grid=(pairs,),
        in_specs=[
            whole(rows, width),
            pl.BlockSpec((3, width, 128), lambda p: (0, 0, p)),
            pl.BlockSpec((128, 2), lambda p: (p, 0)),
            pl.BlockSpec((1, 2, rows), lambda p: (p, 0, 0)),
        ],
        out_specs=[
            pl.BlockSpec((128, rows), lambda p: (p, 0)),
            pl.BlockSpec((2, 3 * HEAD_DIM, rows), lambda p: (p, 0, 0)),
            pl.BlockSpec((2, rows, CLUSTER), lambda p: (p, 0, 0)),
        ],
        out_shape=[
            shape((local, rows), BF16),
            shape((2 * pairs, 3 * HEAD_DIM, rows), BF16),
            shape((2 * pairs, rows, CLUSTER), BF16),
        ],
        scratch_shapes=[pltpu.VMEM((2, rows, rows), BF16)],
        compiler_params=params_of(58),
        cost_estimate=cost(12e9, 12e6),
        name="attend",
    )(x, weight, bias_cols, order_rows)


def block_place(j, order):
    place = 0
    for bit in order:
        place = 2 * place + ((j >> bit) & 1)
    return place


def write_halves(values, keep_ref, send_ref, mine, order, at):
    blocks = 2 ** (len(order) + 1)
    rows = values.shape[0] // blocks
    for j in range(0, blocks, 2):
        even, odd = values[j * rows : (j + 1) * rows], values[(j + 1) * rows : (j + 2) * rows]
        place = (block_place(j, order),) + at
        keep_ref[place] = jnp.where(mine == 0, even, odd)
        send_ref[place] = jnp.where(mine == 0, odd, even)


def attend_back_kernel(
    orders, core_ref, x_ref, da_ref, ow_ref, ctx_ref, w_ref, row_ref, moved_ref, probs_ref, part_ref, bias_ref, *refs
):
    *grad_refs, sel_ref = refs
    rows = da_ref.shape[0]
    spans = spans_of(rows)
    for h in range(2):
        selector(row_ref, h, sel_ref, h)
    d_attn = da_ref[...]
    d_context = dot_nt(ow_ref[...], d_attn).astype(BF16)
    d_out = dot_tt(d_attn, ctx_ref[...])
    found = []
    for h in range(2):
        d_moved = dot(d_context[h * HEAD_DIM : (h + 1) * HEAD_DIM], sel_ref[h]).astype(BF16)
        moved = moved_ref[h]
        query, key, value = moved[:HEAD_DIM], moved[HEAD_DIM : 2 * HEAD_DIM], moved[2 * HEAD_DIM :]
        probs_b = probs_ref[h]
        probs = probs_b.astype(F32)
        d_value = jnp.concatenate([dot(d_moved[:, s], probs_b[s]) for s in spans], axis=1)
        d_probs = jnp.concatenate([dot_tn(d_moved[:, s], value[:, s]) for s in spans], axis=0)
        inner = jnp.sum(probs * d_probs, axis=-1, keepdims=True)
        d_scores = (probs * (d_probs - inner)).astype(BF16)
        d_query = jnp.concatenate([dot_nt(key[:, s], d_scores[s]) for s in spans], axis=1) * SCALE
        d_key = jnp.concatenate([dot(query[:, s], d_scores[s]) for s in spans], axis=1) * SCALE
        three = jnp.concatenate([d_query, d_key, d_value], axis=0).astype(BF16)
        found.append(dot_nt(three, sel_ref[h]).astype(BF16))
    d_qkv = jnp.concatenate(
        [f[c * HEAD_DIM : (c + 1) * HEAD_DIM] for c in range(3) for f in found], axis=0
    )
    sums = dot_nt(jnp.ones((8, rows), BF16), d_qkv)
    bias_ref[0:1, :] = sums[0:1, :128]
    bias_ref[1:2, :] = sums[0:1, 256:]
    grads = dot_tt(x_ref[...], d_qkv)
    for c in range(4):
        values = grads[:, c * 128 : (c + 1) * 128] if c < 3 else d_out
        if orders:
            write_halves(values, *grad_refs[c // 2 * 2 :][:2], core_ref[0], orders[c // 2], (c % 2,))
        else:
            grad_refs[0][c] = values
    part = dot_tt(d_qkv, jnp.concatenate([w_ref[c] for c in range(3)], axis=1))

    @pl.when(pl.program_id(0) == 0)
    def _():
        part_ref[...] = part

    @pl.when(pl.program_id(0) > 0)
    def _():
        part_ref[...] += part


def attend_back(orders, core, x, d_attn, out_weight, context, weight, order_rows, moved, probs):
    rows, width = x.shape
    local = weight.shape[2]
    pairs = order_rows.shape[0]
    if orders:
        blocks = 2 ** len(orders[0])
        height = width // (2 * blocks)
        grad_specs = [pl.BlockSpec((blocks, 2, height, 128), lambda p: (0, 0, 0, p))] * 4
        grad_shapes = [shape((blocks, 2, height, local), F32)] * 4
    else:
        grad_specs = [pl.BlockSpec((4, width, 128), lambda p: (0, 0, p))]
        grad_shapes = [shape((4, width, local), F32)]
    return pl.pallas_call(
        functools.partial(attend_back_kernel, orders),
        grid=(pairs,),
        in_specs=[
            pl.BlockSpec(memory_space=pltpu.SMEM),
            whole(rows, width),
            whole(rows, width),
            pl.BlockSpec((128, width), lambda p: (p, 0)),
            pl.BlockSpec((128, rows), lambda p: (p, 0)),
            pl.BlockSpec((3, width, 128), lambda p: (0, 0, p)),
            pl.BlockSpec((1, 2, rows), lambda p: (p, 0, 0)),
            pl.BlockSpec((2, 3 * HEAD_DIM, rows), lambda p: (p, 0, 0)),
            pl.BlockSpec((2, rows, CLUSTER), lambda p: (p, 0, 0)),
        ],
        out_specs=[
            pl.BlockSpec((rows, width), lambda p: (0, 0)), pl.BlockSpec((2, 128), lambda p: (0, p)), *grad_specs
        ],
        out_shape=[shape((rows, width), F32), shape((2, local), F32), *grad_shapes],
        scratch_shapes=[pltpu.VMEM((2, rows, rows), BF16)],
        compiler_params=params_of(30),
        cost_estimate=cost(20e9, 20e6),
        name="attend_back",
    )(core, x, d_attn, out_weight, context, weight, order_rows, moved, probs)


def gelu_both(hidden):
    scale = 0.7978845608028654
    square = hidden * hidden
    bent = jnp.tanh(hidden * (scale + (scale * 0.044715) * square))
    half = 0.5 + 0.5 * bent
    active = hidden * half
    slope = half + 0.5 * hidden * (1.0 - bent * bent) * (scale + (3 * scale * 0.044715) * square)
    return active.astype(BF16), slope.astype(BF16)


def normalized(values):
    centred = values - jnp.mean(values, axis=-1, keepdims=True)
    factor = lax.rsqrt(jnp.mean(centred * centred, axis=-1, keepdims=True) + EPSILON)
    return centred * factor, factor


def norm_back(grad, unit, factor):
    mean = jnp.mean(grad, axis=-1, keepdims=True)
    inner = jnp.mean(grad * unit, axis=-1, keepdims=True)
    return factor * (grad - mean - unit * inner)


def unit_cuts(units):
    return [slice(u, u + UNIT_TILE) for u in range(0, units, UNIT_TILE)]


def narrow_copies(parts, stage, sems, places, up_out, down_out):
    rows, width = stage.shape[1], down_out.shape[1]
    copies = [
        pltpu.make_async_copy(part.at[0], stage.at[k], sems.at[k]) for k, part in enumerate(parts)
    ]

    def start():
        for copy in copies:
            copy.start()

    def finish():
        count = len(copies) // 2
        for k, copy in enumerate(copies):
            copy.wait()
            if k < count:
                place = pl.multiple_of(places[k] * rows, rows)
                up_out[pl.ds(place, rows), :] = stage[k].astype(BF16)
            else:
                for side in range(2):
                    place = pl.multiple_of((places[k - count] * 2 + side) * rows, rows)
                    cut = slice(side * width, (side + 1) * width)
                    down_out[pl.ds(place, rows), :] = stage[k, :, cut].astype(BF16)

    return start, finish


def placed_kernel(slots_ref, *refs):
    *parts, up_ref, down_ref, stage, sems = refs
    places = [slots_ref[k] for k in range(len(parts) // 2)]
    start, finish = narrow_copies(parts, stage, sems, places, up_ref, down_ref)
    start()
    finish()


def placed(slots, parts, group):
    _, rows, units = parts[0].shape
    width = units // 2
    dims = [(group * rows, units), (2 * group * rows, width)]
    return pl.pallas_call(
        placed_kernel,
        grid=(1,),
        in_specs=[pl.BlockSpec(memory_space=pltpu.SMEM)]
        + [pl.BlockSpec(memory_space=pl.ANY)] * len(parts),
        out_specs=[whole(*out) for out in dims],
        out_shape=[shape(out, BF16) for out in dims],
        scratch_shapes=[
            pltpu.VMEM((len(parts),) + parts[0].shape[1:], F32), pltpu.SemaphoreType.DMA((len(parts),))
        ],
        compiler_params=params_of(56),
        cost_estimate=cost(1e6, 1e6),
        name="placed",
    )(slots, *parts)


def feed_rows(
    x_ref, cot_ref, ctx_ref, far_ctx_refs, vector_refs, ready, out_s, far_out_s, up_s, down_s, far_up_s, far_down_s,
    mixed_ref, d_pre_ref, d_attn_ref, sums_ref, up_sums_ref, nb_s, act_s, d_feed_s, d_hidden_s, here,
):
    units = up_s.shape[1]
    row = lambda ref: ref[...].reshape(1, ref.shape[0])
    out_bias, gain1, bias1, down_bias, gain2, bias2, up_bias, far_bias = map(row, vector_refs)
    ready("out")
    attention = dot_tn(ctx_ref[...], out_s[...])
    far_ctx = jnp.concatenate([ref[...].astype(BF16) for ref in far_ctx_refs], axis=0)
    attention += dot_tn(far_ctx, far_out_s[...])
    unit1, factor1 = normalized(x_ref[...].astype(F32) + attention + out_bias)
    normed = unit1 * gain1 + bias1
    nb = normed.astype(BF16)
    nb_s[here, :] = nb
    total = normed + down_bias
    slopes, far_slopes = [], []
    ready("near")
    for cut in unit_cuts(units):
        active, slope = gelu_both(dot(nb, up_s[:, cut]) + up_bias[:, cut])
        act_s[here, cut] = active
        slopes.append(slope)
        total = total + dot(active, down_s[cut, :])
    ready("far")
    for cut in unit_cuts(units):
        far_active, far_slope = gelu_both(dot(nb, far_up_s[:, cut]) + far_bias[:, cut])
        far_slopes.append(far_slope)
        total = total + dot(far_active, far_down_s[cut, :])
    unit2, factor2 = normalized(total)
    mixed_ref[...] = (unit2 * gain2 + bias2).astype(BF16)
    grad = cot_ref[...].astype(F32)
    sums_ref[0:1, :] += jnp.sum(grad * unit2, axis=0, keepdims=True)
    sums_ref[1:2, :] += jnp.sum(grad, axis=0, keepdims=True)
    d_sum = norm_back(grad * gain2, unit2, factor2)
    d_feed = d_sum.astype(BF16)
    d_feed_s[here, :] = d_feed
    sums_ref[2:3, :] += jnp.sum(d_feed.astype(F32), axis=0, keepdims=True)
    d_normed = d_sum
    for cut, slope, far_slope in zip(unit_cuts(units), slopes, far_slopes):
        d_active = dot_nt(d_feed, down_s[cut, :])
        d_hidden = (d_active * slope.astype(F32)).astype(BF16)
        d_hidden_s[here, cut] = d_hidden
        up_sums_ref[:, cut] += jnp.sum(d_hidden.astype(F32), axis=0, keepdims=True)
        far_d_active = dot_nt(d_feed, far_down_s[cut, :])
        far_d_hidden = (far_d_active * far_slope.astype(F32)).astype(BF16)
        d_normed = d_normed + dot_nt(d_hidden, up_s[:, cut])
        d_normed = d_normed + dot_nt(far_d_hidden, far_up_s[:, cut])
    sums_ref[3:4, :] += jnp.sum(d_normed * unit1, axis=0, keepdims=True)
    sums_ref[4:5, :] += jnp.sum(d_normed, axis=0, keepdims=True)
    d_pre = norm_back(d_normed * gain1, unit1, factor1)
    d_pre_ref[...] = d_pre
    d_attn = d_pre.astype(BF16)
    d_attn_ref[...] = d_attn
    sums_ref[5:6, :] += jnp.sum(d_attn.astype(F32), axis=0, keepdims=True)


def feed_kernel(
    orders, tiles, late_count, core_ref, slots_ref, x_ref, cot_ref, ctx_ref, far0_ref, far1_ref, *refs
):
    vector_refs, refs = refs[:8], refs[8:]
    out_hbm, near_half_hbm, far_half_hbm, up_hbm, down_hbm, far_up_hbm, far_down_hbm, *refs = refs
    late_parts, refs = refs[:late_count], refs[late_count:]
    mixed_ref, d_pre_ref, d_attn_ref, sums_ref, up_sums_ref, *refs = refs
    count = 4 if orders else 2
    grad_refs, refs = refs[:count], refs[count:]
    nb_s, act_s, d_feed_s, d_hidden_s, out_s, far_out_s, up_s, down_s, far_up_s, far_down_s, *refs = refs
    half_stage, late_stage, sems, late_sems = refs
    step = pl.program_id(0)
    tile = x_ref.shape[0]
    copies = [
        pltpu.make_async_copy(source, target, sems.at[k])
        for k, (source, target) in enumerate((
            (out_hbm, out_s), (near_half_hbm, half_stage.at[0]), (far_half_hbm, half_stage.at[1]),
            (up_hbm, up_s), (down_hbm, down_s), (far_up_hbm, far_up_s), (far_down_hbm, far_down_s),
        ))
    ]
    places = [slots_ref[k] for k in range(late_count // 2)]
    start_late, finish_late = narrow_copies(
        late_parts, late_stage, late_sems, places, far_up_s, far_down_s
    )

    def ready(what):
        @pl.when(step == 0)
        def _():
            if what == "out":
                for copy in copies:
                    copy.start()
                start_late()
                sums_ref[...] = jnp.zeros_like(sums_ref)
                up_sums_ref[...] = jnp.zeros_like(up_sums_ref)
                for copy in copies[:3]:
                    copy.wait()
                half = half_stage.shape[1]
                for k in range(2):
                    place = pl.multiple_of((core_ref[0] ^ k) * half, half)
                    far_out_s[pl.ds(place, half), :] = half_stage[k].astype(BF16)
            elif what == "near":
                for copy in copies[3:5]:
                    copy.wait()
            else:
                for copy in copies[5:]:
                    copy.wait()
                finish_late()

    @pl.when(step < tiles)
    def _():
        here = pl.ds(pl.multiple_of(step * tile, tile), tile)
        feed_rows(
            x_ref, cot_ref, ctx_ref, (far0_ref, far1_ref), vector_refs, ready, out_s, far_out_s, up_s,
            down_s, far_up_s, far_down_s, mixed_ref, d_pre_ref, d_attn_ref, sums_ref, up_sums_ref, nb_s, act_s,
            d_feed_s, d_hidden_s, here,
        )

    @pl.when(step >= tiles)
    def _():
        there = pl.ds(pl.multiple_of((step - tiles) * GRAD_TILE, GRAD_TILE), GRAD_TILE)
        d_down = dot_tn(d_feed_s[...], act_s[:, there])
        d_up = dot_tn(nb_s[...], d_hidden_s[:, there])
        if orders:
            write_halves(d_down, *grad_refs[:2], core_ref[0], orders[0], ())
            write_halves(d_up, *grad_refs[2:], core_ref[0], orders[1], ())
        else:
            grad_refs[0][...] = d_down
            grad_refs[1][...] = d_up


def feed(
    orders, core, slots, x, cotangent, context, far_context, out_weight, halves, vectors, up, down, far_up, far_down,
    late,
):
    rows, width = x.shape
    local, units = out_weight.shape[0], up.shape[1]
    tile = ROW_TILE
    tiles = rows // tile
    across = lambda cols: pl.BlockSpec((tile, cols), lambda i: (jnp.minimum(i, tiles - 1), 0))
    along = lambda height: pl.BlockSpec((height, tile), lambda i: (0, jnp.minimum(i, tiles - 1)))
    if orders:
        blocks = 2 ** len(orders[0])
        height = width // (2 * blocks)
        grad_specs = [
            pl.BlockSpec((blocks, height, GRAD_TILE), lambda i: (0, 0, jnp.maximum(i - tiles, 0)))
        ] * 4
        grad_shapes = [shape((blocks, height, units), F32)] * 4
    else:
        grad_specs = [pl.BlockSpec((width, GRAD_TILE), lambda i: (0, jnp.maximum(i - tiles, 0)))] * 2
        grad_shapes = [shape((width, units), F32)] * 2
    scalars = pl.BlockSpec(memory_space=pltpu.SMEM)
    anywhere = pl.BlockSpec(memory_space=pl.ANY)
    return pl.pallas_call(
        functools.partial(feed_kernel, orders, tiles, len(late)),
        grid=(tiles + units // GRAD_TILE,),
        in_specs=[
            scalars, scalars, across(width), across(width), along(local),
            *[along(part.shape[0]) for part in far_context], *[whole(v.shape[0]) for v in vectors],
            *[anywhere] * (7 + len(late)),
        ],
        out_specs=[
            across(width), across(width), across(width), whole(8, width), whole(1, units),
            *grad_specs,
        ],
        out_shape=[
            shape((rows, width), BF16), shape((rows, width), F32), shape((rows, width), BF16),
            shape((8, width), F32), shape((1, units), F32), *grad_shapes,
        ],
        scratch_shapes=[
            pltpu.VMEM((rows, width), BF16), pltpu.VMEM((rows, units), BF16), pltpu.VMEM((rows, width), BF16),
            pltpu.VMEM((rows, units), BF16),
            pltpu.VMEM((local, width), BF16), pltpu.VMEM((local, width), BF16),
            pltpu.VMEM((width, units), BF16), pltpu.VMEM((units, width), BF16),
            pltpu.VMEM((width, units), BF16), pltpu.VMEM((units, width), BF16),
            pltpu.VMEM((2,) + halves[0].shape, F32), pltpu.VMEM((len(late),) + late[0].shape[1:], F32),
            pltpu.SemaphoreType.DMA((7,)), pltpu.SemaphoreType.DMA((len(late),)),
        ],
        compiler_params=params_of(56),
        cost_estimate=cost(25e9, 30e6),
        name="feed",
    )(
        core, slots, x, cotangent, context, *far_context, *vectors, out_weight, *halves, up, down,
        far_up, far_down, *late,
    )


def make_body(n_items):
    def body(
        hidden_in,
        cluster_order,
        qkv_weight,
        qv_bias,
        out_weight,
        out_bias,
        norm1_gain,
        norm1_bias,
        up_weight,
        up_bias,
        down_weight,
        down_bias,
        norm2_gain,
        norm2_bias,
        cotangent,
    ):
        rows, width = hidden_in.shape
        units = up_weight.shape[1]
        local = out_weight.shape[0]
        item = lax.axis_index("items")
        core = item & 1
        group = 8
        place = item % group

        def piece(values):
            count = values.shape[0] // group
            return lax.dynamic_slice_in_dim(values, place * count, count, 0).astype(F32)[None]

        up_piece = piece(up_weight)
        two_rows = piece(after(down_weight, up_piece))
        middle = two_rows.shape[1] // 2
        down_piece = jnp.concatenate([two_rows[:, :middle], two_rows[:, middle:]], axis=2)
        far_a = swapped(up_piece)
        far_b = swapped(down_piece)
        far_bias = swapped(up_bias)
        half = local // 2

        ordering = cluster_order[:, 0, :]
        order_rows = ordering.reshape(-1, 2, rows)
        x = after(hidden_in, up_piece, down_piece)
        context, moved, probs = attend(x, qkv_weight, qv_bias.T, order_rows)
        pairs = order_rows.shape[0]
        far_context = [
            swapped(context[:128].astype(F32)), swapped(context[128:].astype(F32))
        ]
        out_piece = lax.dynamic_slice_in_dim(out_weight, core * half, half, 0).astype(F32)

        trade = lambda values, step: traded(values, step, n_items)
        at_once = lambda *values: lax.optimization_barrier(values)
        a0 = after(far_a, context)
        a4, a2 = trade(a0, 4), trade(a0, 2)
        b0 = after(far_b, a0)
        far_half = swapped(after(out_piece, b0))
        b4, b2 = trade(b0, 4), trade(b0, 2)
        a4, a2, far_context[0], _ = at_once(a4, a2, far_context[0], b0)
        a6 = trade(a4, 2)
        b4, b2, far_half, _ = at_once(b4, b2, far_half, a4)
        b6 = trade(b4, 2)
        all_slots = lambda ks: jnp.stack([place ^ k for k in ks]).astype(jnp.int32)
        come = [part for one in ((a0, a4, a2), (b0, b4, b2)) for part in (*one, *(trade(p, 1) for p in one))]
        far_up, far_down = placed(all_slots((0, 4, 2, 1, 5, 3)), come, group)
        a6, b6, far_context[1], far_bias, far_up = at_once(
            a6, b6, far_context[1], far_bias, far_up
        )
        other_half = trade(far_half, 1)
        late, slots = [a6, trade(a6, 1), b6, trade(b6, 1)], all_slots((6, 7))
        which = core.astype(jnp.int32).reshape(1)

        split = width % (8 * n_items) == 0
        bits = tuple(range(1, n_items.bit_length() - 1))
        late_y = bits[1:2] + bits[:1] + bits[2:]
        mixed, d_pre, d_attn, sums, up_sums, *grads = feed(
            (bits, late_y) if split else None, which, slots, x, cotangent, context, far_context,
            out_weight, [far_half, other_half],
            [out_bias, norm1_gain, norm1_bias, down_bias, norm2_gain, norm2_bias, up_bias, far_bias],
            up_weight, down_weight, far_up, far_down, late,
        )

        def packed_of(grad_qv):
            return jnp.concatenate(
                [sums, up_sums.reshape(-1, width), grad_qv.reshape(-1, width)], axis=0
            )

        back = lambda d_attn: attend_back(
            (bits, late_y) if split else None, which, x, d_attn, out_weight, context, qkv_weight,
            order_rows, moved, probs,
        )
        if split:
            halving = lambda keep, send, order: Halving(keep, send, order, n_items).trade()
            down_sum, up_sum = halving(*grads[:2], bits), halving(*grads[2:], late_y)
            sent = arrived([down_sum, up_sum])
            down_sum.trade()
            up_sum.trade()
            part, grad_qv, *halves = back(after(d_attn, *sent))
            far_part = swapped(part)
            first, second = halving(*halves[:2], bits), halving(*halves[2:], late_y)
            sent = arrived([down_sum, up_sum], part)
            down_sum.trade()
            up_sum.trade()
            sent = arrived([first, second], *sent)
            first.trade()
            second.trade()
            first.extra = packed_of(after(grad_qv, *sent))
            first.extra = first.extra + traded(first.extra, 1, n_items)
            first.more = traded(first.extra, 1 << first.bit, n_items)
            sums_all = [down_sum, up_sum, first, second]
            for _ in bits[3:]:
                arrived(sums_all)
                for one in sums_all[::-1]:
                    one.trade()
            arrived(sums_all)
            first.trade()
            second.trade()
            together = traded(
                jnp.concatenate([down_sum.send, up_sum.send]), 1 << down_sum.bit, n_items
            )
            together, first.got, second.got, first.more = at_once(
                together, first.got, second.got, first.more
            )
            sent = [first.add(), second.add()]
            rest = traded(jnp.concatenate(sent), 1 << first.bit, n_items)
            first.more = traded(first.extra, 1 << first.bit, n_items)
            down_sum.got, up_sum.got = together[:1], together[1:]
            summed_down, summed_up = down_sum.add(), up_sum.add()
            far_part = after(far_part, summed_down, summed_up, *sent)
            grad_inputs = (d_pre + part + far_part).astype(BF16)
            rest, first.more, _ = at_once(rest, first.more, grad_inputs)
            first.got, second.got = rest[:1], rest[1:]
            summed = [first.add(), second.add()]
            summed_rest = [summed[c // 2][c % 2] for c in range(4)]
            packed = first.extra
        else:
            part, grad_qv, grad_rest = back(d_attn)
            grad_inputs = (d_pre + part + swapped(part)).astype(BF16)
            summed_down = scattered(grads[0], n_items, 0)
            summed_up = scattered(grads[1], n_items, 0)
            summed_rest = scattered(grad_rest, n_items, 1)
            packed = all_sum(packed_of(grad_qv), n_items)
        small = packed[:8]
        up_small = packed[8 : 8 + units // width].reshape(units)
        qv_small = packed[8 + units // width :].reshape(2, local)
        return (
            mixed,
            grad_inputs,
            jnp.stack([summed_rest[c] for c in range(3)]),
            qv_small,
            summed_rest[3].T,
            small[5],
            small[3],
            small[4],
            summed_up,
            up_small,
            summed_down.T,
            small[2],
            small[0],
            small[1],
        )

    return body


def solution(mesh):
    return jax.shard_map(
        make_body(mesh.shape["items"]),
        mesh=mesh,
        in_specs=(
            P("items", None),
            P("heads", "items", None),
            P(None, None, "heads"),
            P(None, "heads"),
            P("heads", None),
            P(),
            P(),
            P(),
            P(None, "heads"),
            P("heads"),
            P("heads", None),
            P(),
            P(),
            P(),
            P("items", None),
        ),
        out_specs=(
            P("items", None),
            P("items", None),
            P(None, "items", "heads"),
            P(None, "heads"),
            P("heads", "items"),
            P(),
            P(),
            P(),
            P("items", "heads"),
            P("heads"),
            P("heads", "items"),
            P(),
            P(),
            P(),
        ),
        check_vma=False,
    )
```

```python
import functools

import jax
import jax.numpy as jnp
from jax import lax
from jax.experimental import pallas as pl
from jax.experimental.pallas import tpu as pltpu
from jax.sharding import PartitionSpec as P

HEAD_DIM = 64
CLUSTER = 128
SCALE = HEAD_DIM**-0.5
EPSILON = 1e-05
ROW_TILE = 256
GRAD_TILE = 512
UNIT_TILE = 1536
BF16 = jnp.bfloat16
F32 = jnp.float32


def dot(left, right):
    return jnp.dot(left, right, preferred_element_type=F32)


def dot_nt(left, right):
    return lax.dot_general(left, right, (((1,), (1,)), ((), ())), preferred_element_type=F32)


def dot_tn(left, right):
    return lax.dot_general(left, right, (((0,), (0,)), ((), ())), preferred_element_type=F32)


def dot_tt(left, right):
    return lax.dot_general(left, right, (((0,), (1,)), ((), ())), preferred_element_type=F32)


def params_of(mib):
    return pltpu.CompilerParams(vmem_limit_bytes=mib * 1024 * 1024)


def cost(flops, bytes_accessed):
    return pl.CostEstimate(flops=int(flops) // 1000, bytes_accessed=int(bytes_accessed) // 1000, transcendentals=0)


def shape(dims, dtype):
    return jax.ShapeDtypeStruct(dims, dtype)


def whole(*dims):
    return pl.BlockSpec(dims, lambda *_: (0,) * len(dims), pipeline_mode=pl.Buffered(1))


def swapped(values):
    return lax.ppermute(values, "heads", [(0, 1), (1, 0)])


def traded(values, step, n_items):
    return lax.ppermute(values, "items", [(i, i ^ step) for i in range(n_items)])


def all_sum(values, n_items):
    step = 1
    while step < n_items:
        values = values + traded(values, step, n_items)
        step *= 2
    return values


def scattered(values, n_items, axis):
    item = lax.axis_index("items")
    size = n_items
    for bit in range(n_items.bit_length() - 1):
        dims = values.shape
        size //= 2
        halves = values.reshape(dims[:axis] + (size, 2, dims[axis] // (2 * size)) + dims[axis + 1 :])
        mine = (item >> bit) & 1
        send = lax.dynamic_index_in_dim(halves, 1 - mine, axis + 1, keepdims=False)
        keep = lax.dynamic_index_in_dim(halves, mine, axis + 1, keepdims=False)
        values = keep + traded(send, 1 << bit, n_items)
        values = values.reshape(dims[:axis] + (-1,) + dims[axis + 1 :])
    return values


class Halving:
    def __init__(self, keep, send, order, n_items):
        self.order, self.n_items, self.rest = list(order), n_items, keep.shape[1:]
        self.terms = []
        self.hold(keep)
        self.send, self.extra, self.bit = send, None, 0

    def hold(self, values):
        self.terms.append((values.reshape((2,) * len(self.order) + self.rest), []))

    def part(self, term, places):
        values, settled = term
        starts = settled + places
        sizes = (1,) * len(starts) + values.shape[len(starts) :]
        starts = starts + [0] * (values.ndim - len(starts))
        return lax.dynamic_slice(values, starts, sizes).reshape((-1,) + self.rest)

    def trade(self):
        self.got = traded(self.send, 1 << self.bit, self.n_items)
        if self.extra is not None:
            self.more = traded(self.extra, 1 << self.bit, self.n_items)
        return self

    def add(self):
        self.hold(self.got)
        if self.extra is not None:
            self.extra = self.extra + self.more
        if not self.order:
            return sum(self.part(term, []) for term in self.terms).reshape(self.rest)
        self.bit = self.order.pop(0)
        mine = (lax.axis_index("items") >> self.bit) & 1
        self.send = sum(self.part(term, [1 - mine]) for term in self.terms)
        self.terms = [(values, settled + [mine]) for values, settled in self.terms]
        return self.send


def arrived(sums, *before):
    got = [one.got for one in sums] + [one.more for one in sums if one.extra is not None]
    got = list(lax.optimization_barrier(tuple(got) + before))
    for one in sums:
        one.got = got.pop(0)
    for one in sums:
        if one.extra is not None:
            one.more = got.pop(0)
    return [one.add() for one in sums]


def after(values, *others):
    return lax.optimization_barrier((values,) + others)[0]


def selector(row_ref, h, sel_ref, slot):
    rows = sel_ref.shape[1]
    step = 256
    for r in range(0, rows, step):
        subs = lax.broadcasted_iota(jnp.int32, (step, rows), 0) + r
        found = jnp.where(row_ref[0, h : h + 1, :] == subs, 1.0, 0.0)
        sel_ref[slot, r : r + step, :] = found.astype(BF16)


def spans_of(rows):
    return [slice(c, c + CLUSTER) for c in range(0, rows, CLUSTER)]


def attend_kernel(x_ref, w_ref, bias_ref, row_ref, ctx_ref, moved_ref, probs_ref, sel_ref):
    rows = x_ref.shape[0]
    spans = spans_of(rows)
    for h in range(2):
        selector(row_ref, h, sel_ref, h)
    weight = jnp.concatenate([w_ref[c] for c in range(3)], axis=1)
    flat = dot_tt(weight, x_ref[...])
    parts = [flat[:128] + bias_ref[:, 0:1], flat[128:256], flat[256:] + bias_ref[:, 1:2]]
    parts = [part.astype(BF16) for part in parts]
    for h in range(2):
        cut = slice(h * HEAD_DIM, (h + 1) * HEAD_DIM)
        qkv = jnp.concatenate([part[cut] for part in parts], axis=0)
        moved = dot(qkv, sel_ref[h]).astype(BF16)
        moved_ref[h] = moved
        query, key, value = moved[:HEAD_DIM], moved[HEAD_DIM : 2 * HEAD_DIM], moved[2 * HEAD_DIM :]
        scores = jnp.concatenate([dot_tn(query[:, s], key[:, s]) for s in spans], axis=0) * SCALE
        shifted = jnp.exp(scores - jnp.max(scores, axis=-1, keepdims=True))
        probs = shifted / jnp.sum(shifted, axis=-1, keepdims=True)
        probs_b = probs.astype(BF16)
        probs_ref[h] = probs_b
        mixed = jnp.concatenate([dot_nt(value[:, s], probs_b[s]) for s in spans], axis=1)
        context = dot_nt(mixed.astype(BF16), sel_ref[h])
        ctx_ref[cut, :] = context.astype(BF16)


def attend(x, weight, bias_cols, order_rows):
    rows, width = x.shape
    pairs = order_rows.shape[0]
    local = weight.shape[2]
    return pl.pallas_call(
        attend_kernel,
        grid=(pairs,),
        in_specs=[
            whole(rows, width),
            pl.BlockSpec((3, width, 128), lambda p: (0, 0, p)),
            pl.BlockSpec((128, 2), lambda p: (p, 0)),
            pl.BlockSpec((1, 2, rows), lambda p: (p, 0, 0)),
        ],
        out_specs=[
            pl.BlockSpec((128, rows), lambda p: (p, 0)),
            pl.BlockSpec((2, 3 * HEAD_DIM, rows), lambda p: (p, 0, 0)),
            pl.BlockSpec((2, rows, CLUSTER), lambda p: (p, 0, 0)),
        ],
        out_shape=[
            shape((local, rows), BF16),
            shape((2 * pairs, 3 * HEAD_DIM, rows), BF16),
            shape((2 * pairs, rows, CLUSTER), BF16),
        ],
        scratch_shapes=[pltpu.VMEM((2, rows, rows), BF16)],
        compiler_params=params_of(58),
        cost_estimate=cost(12e9, 12e6),
        name="attend",
    )(x, weight, bias_cols, order_rows)


def block_place(j, order):
    place = 0
    for bit in order:
        place = 2 * place + ((j >> bit) & 1)
    return place


def write_halves(values, keep_ref, send_ref, mine, order, at):
    blocks = 2 ** (len(order) + 1)
    rows = values.shape[0] // blocks
    for j in range(0, blocks, 2):
        even, odd = values[j * rows : (j + 1) * rows], values[(j + 1) * rows : (j + 2) * rows]
        place = (block_place(j, order),) + at
        keep_ref[place] = jnp.where(mine == 0, even, odd)
        send_ref[place] = jnp.where(mine == 0, odd, even)


def attend_back_kernel(
    orders, core_ref, x_ref, da_ref, ow_ref, ctx_ref, w_ref, row_ref, moved_ref, probs_ref, part_ref, bias_ref, *refs
):
    *grad_refs, sel_ref = refs
    rows = da_ref.shape[0]
    spans = spans_of(rows)
    for h in range(2):
        selector(row_ref, h, sel_ref, h)
    d_attn = da_ref[...]
    d_context = dot_nt(ow_ref[...], d_attn).astype(BF16)
    d_out = dot_tt(d_attn, ctx_ref[...])
    found = []
    for h in range(2):
        d_moved = dot(d_context[h * HEAD_DIM : (h + 1) * HEAD_DIM], sel_ref[h]).astype(BF16)
        moved = moved_ref[h]
        query, key, value = moved[:HEAD_DIM], moved[HEAD_DIM : 2 * HEAD_DIM], moved[2 * HEAD_DIM :]
        probs_b = probs_ref[h]
        probs = probs_b.astype(F32)
        d_value = jnp.concatenate([dot(d_moved[:, s], probs_b[s]) for s in spans], axis=1)
        d_probs = jnp.concatenate([dot_tn(d_moved[:, s], value[:, s]) for s in spans], axis=0)
        inner = jnp.sum(probs * d_probs, axis=-1, keepdims=True)
        d_scores = (probs * (d_probs - inner)).astype(BF16)
        d_query = jnp.concatenate([dot_nt(key[:, s], d_scores[s]) for s in spans], axis=1) * SCALE
        d_key = jnp.concatenate([dot(query[:, s], d_scores[s]) for s in spans], axis=1) * SCALE
        three = jnp.concatenate([d_query, d_key, d_value], axis=0).astype(BF16)
        found.append(dot_nt(three, sel_ref[h]).astype(BF16))
    d_qkv = jnp.concatenate(
        [f[c * HEAD_DIM : (c + 1) * HEAD_DIM] for c in range(3) for f in found], axis=0
    )
    sums = dot_nt(jnp.ones((8, rows), BF16), d_qkv)
    bias_ref[0:1, :] = sums[0:1, :128]
    bias_ref[1:2, :] = sums[0:1, 256:]
    grads = dot_tt(x_ref[...], d_qkv)
    for c in range(4):
        values = grads[:, c * 128 : (c + 1) * 128] if c < 3 else d_out
        if orders:
            write_halves(values, *grad_refs[c // 2 * 2 :][:2], core_ref[0], orders[c // 2], (c % 2,))
        else:
            grad_refs[0][c] = values
    part = dot_tt(d_qkv, jnp.concatenate([w_ref[c] for c in range(3)], axis=1))

    @pl.when(pl.program_id(0) == 0)
    def _():
        part_ref[...] = part

    @pl.when(pl.program_id(0) > 0)
    def _():
        part_ref[...] += part


def attend_back(orders, core, x, d_attn, out_weight, context, weight, order_rows, moved, probs):
    rows, width = x.shape
    local = weight.shape[2]
    pairs = order_rows.shape[0]
    if orders:
        blocks = 2 ** len(orders[0])
        height = width // (2 * blocks)
        grad_specs = [pl.BlockSpec((blocks, 2, height, 128), lambda p: (0, 0, 0, p))] * 4
        grad_shapes = [shape((blocks, 2, height, local), F32)] * 4
    else:
        grad_specs = [pl.BlockSpec((4, width, 128), lambda p: (0, 0, p))]
        grad_shapes = [shape((4, width, local), F32)]
    return pl.pallas_call(
        functools.partial(attend_back_kernel, orders),
        grid=(pairs,),
        in_specs=[
            pl.BlockSpec(memory_space=pltpu.SMEM),
            whole(rows, width),
            whole(rows, width),
            pl.BlockSpec((128, width), lambda p: (p, 0)),
            pl.BlockSpec((128, rows), lambda p: (p, 0)),
            pl.BlockSpec((3, width, 128), lambda p: (0, 0, p)),
            pl.BlockSpec((1, 2, rows), lambda p: (p, 0, 0)),
            pl.BlockSpec((2, 3 * HEAD_DIM, rows), lambda p: (p, 0, 0)),
            pl.BlockSpec((2, rows, CLUSTER), lambda p: (p, 0, 0)),
        ],
        out_specs=[
            pl.BlockSpec((rows, width), lambda p: (0, 0)), pl.BlockSpec((2, 128), lambda p: (0, p)), *grad_specs
        ],
        out_shape=[shape((rows, width), F32), shape((2, local), F32), *grad_shapes],
        scratch_shapes=[pltpu.VMEM((2, rows, rows), BF16)],
        compiler_params=params_of(30),
        cost_estimate=cost(20e9, 20e6),
        name="attend_back",
    )(core, x, d_attn, out_weight, context, weight, order_rows, moved, probs)


def gelu_both(hidden):
    scale = 0.7978845608028654
    square = hidden * hidden
    bent = jnp.tanh(hidden * (scale + (scale * 0.044715) * square))
    half = 0.5 + 0.5 * bent
    active = hidden * half
    slope = half + 0.5 * hidden * (1.0 - bent * bent) * (scale + (3 * scale * 0.044715) * square)
    return active.astype(BF16), slope.astype(BF16)


def normalized(values):
    centred = values - jnp.mean(values, axis=-1, keepdims=True)
    factor = lax.rsqrt(jnp.mean(centred * centred, axis=-1, keepdims=True) + EPSILON)
    return centred * factor, factor


def norm_back(grad, unit, factor):
    mean = jnp.mean(grad, axis=-1, keepdims=True)
    inner = jnp.mean(grad * unit, axis=-1, keepdims=True)
    return factor * (grad - mean - unit * inner)


def unit_cuts(units):
    return [slice(u, u + UNIT_TILE) for u in range(0, units, UNIT_TILE)]


def narrow_copies(parts, stage, sems, places, up_out, down_out):
    rows, width = stage.shape[1], down_out.shape[1]
    copies = [
        pltpu.make_async_copy(part.at[0], stage.at[k], sems.at[k]) for k, part in enumerate(parts)
    ]

    def start():
        for copy in copies:
            copy.start()

    def finish():
        count = len(copies) // 2
        for k, copy in enumerate(copies):
            copy.wait()
            if k < count:
                place = pl.multiple_of(places[k] * rows, rows)
                up_out[pl.ds(place, rows), :] = stage[k].astype(BF16)
            else:
                for side in range(2):
                    place = pl.multiple_of((places[k - count] * 2 + side) * rows, rows)
                    cut = slice(side * width, (side + 1) * width)
                    down_out[pl.ds(place, rows), :] = stage[k, :, cut].astype(BF16)

    return start, finish


def placed_kernel(slots_ref, *refs):
    *parts, up_ref, down_ref, stage, sems = refs
    places = [slots_ref[k] for k in range(len(parts) // 2)]
    start, finish = narrow_copies(parts, stage, sems, places, up_ref, down_ref)
    start()
    finish()


def placed(slots, parts, group):
    _, rows, units = parts[0].shape
    width = units // 2
    dims = [(group * rows, units), (2 * group * rows, width)]
    return pl.pallas_call(
        placed_kernel,
        grid=(1,),
        in_specs=[pl.BlockSpec(memory_space=pltpu.SMEM)]
        + [pl.BlockSpec(memory_space=pl.ANY)] * len(parts),
        out_specs=[whole(*out) for out in dims],
        out_shape=[shape(out, BF16) for out in dims],
        scratch_shapes=[
            pltpu.VMEM((len(parts),) + parts[0].shape[1:], F32), pltpu.SemaphoreType.DMA((len(parts),))
        ],
        compiler_params=params_of(56),
        cost_estimate=cost(1e6, 1e6),
        name="placed",
    )(slots, *parts)


def feed_rows(
    x_ref, cot_ref, ctx_ref, far_ctx_refs, vector_refs, ready, out_s, far_out_s, up_s, down_s, far_up_s, far_down_s,
    mixed_ref, d_pre_ref, d_attn_ref, sums_ref, up_sums_ref, nb_s, act_s, d_feed_s, d_hidden_s, here,
):
    units = up_s.shape[1]
    row = lambda ref: ref[...].reshape(1, ref.shape[0])
    out_bias, gain1, bias1, down_bias, gain2, bias2, up_bias, far_bias = map(row, vector_refs)
    ready("out")
    attention = dot_tn(ctx_ref[...], out_s[...])
    far_ctx = jnp.concatenate([ref[...].astype(BF16) for ref in far_ctx_refs], axis=0)
    attention += dot_tn(far_ctx, far_out_s[...])
    unit1, factor1 = normalized(x_ref[...].astype(F32) + attention + out_bias)
    normed = unit1 * gain1 + bias1
    nb = normed.astype(BF16)
    nb_s[here, :] = nb
    total = normed + down_bias
    slopes, far_slopes = [], []
    ready("near")
    for cut in unit_cuts(units):
        active, slope = gelu_both(dot(nb, up_s[:, cut]) + up_bias[:, cut])
        act_s[here, cut] = active
        slopes.append(slope)
        total = total + dot(active, down_s[cut, :])
    ready("far")
    for cut in unit_cuts(units):
        far_active, far_slope = gelu_both(dot(nb, far_up_s[:, cut]) + far_bias[:, cut])
        far_slopes.append(far_slope)
        total = total + dot(far_active, far_down_s[cut, :])
    unit2, factor2 = normalized(total)
    mixed_ref[...] = (unit2 * gain2 + bias2).astype(BF16)
    grad = cot_ref[...].astype(F32)
    sums_ref[0:1, :] += jnp.sum(grad * unit2, axis=0, keepdims=True)
    sums_ref[1:2, :] += jnp.sum(grad, axis=0, keepdims=True)
    d_sum = norm_back(grad * gain2, unit2, factor2)
    d_feed = d_sum.astype(BF16)
    d_feed_s[here, :] = d_feed
    sums_ref[2:3, :] += jnp.sum(d_feed.astype(F32), axis=0, keepdims=True)
    d_normed = d_sum
    for cut, slope, far_slope in zip(unit_cuts(units), slopes, far_slopes):
        d_active = dot_nt(d_feed, down_s[cut, :])
        d_hidden = (d_active * slope.astype(F32)).astype(BF16)
        d_hidden_s[here, cut] = d_hidden
        up_sums_ref[:, cut] += jnp.sum(d_hidden.astype(F32), axis=0, keepdims=True)
        far_d_active = dot_nt(d_feed, far_down_s[cut, :])
        far_d_hidden = (far_d_active * far_slope.astype(F32)).astype(BF16)
        d_normed = d_normed + dot_nt(d_hidden, up_s[:, cut])
        d_normed = d_normed + dot_nt(far_d_hidden, far_up_s[:, cut])
    sums_ref[3:4, :] += jnp.sum(d_normed * unit1, axis=0, keepdims=True)
    sums_ref[4:5, :] += jnp.sum(d_normed, axis=0, keepdims=True)
    d_pre = norm_back(d_normed * gain1, unit1, factor1)
    d_pre_ref[...] = d_pre
    d_attn = d_pre.astype(BF16)
    d_attn_ref[...] = d_attn
    sums_ref[5:6, :] += jnp.sum(d_attn.astype(F32), axis=0, keepdims=True)


def feed_kernel(
    orders, tiles, late_count, core_ref, slots_ref, x_ref, cot_ref, ctx_ref, far_ctx_ref, *refs
):
    vector_refs, refs = refs[:8], refs[8:]
    out_hbm, near_half_hbm, far_half_hbm, up_hbm, down_hbm, far_up_hbm, far_down_hbm, *refs = refs
    late_parts, refs = refs[:late_count], refs[late_count:]
    mixed_ref, d_pre_ref, d_attn_ref, sums_ref, up_sums_ref, *refs = refs
    count = 4 if orders else 2
    grad_refs, refs = refs[:count], refs[count:]
    nb_s, act_s, d_feed_s, d_hidden_s, out_s, far_out_s, up_s, down_s, far_up_s, far_down_s, *refs = refs
    half_stage, late_stage, sems, late_sems = refs
    step = pl.program_id(0)
    tile = x_ref.shape[0]
    copies = [
        pltpu.make_async_copy(source, target, sems.at[k])
        for k, (source, target) in enumerate((
            (out_hbm, out_s), (near_half_hbm, half_stage.at[0]), (far_half_hbm, half_stage.at[1]),
            (up_hbm, up_s), (down_hbm, down_s), (far_up_hbm, far_up_s), (far_down_hbm, far_down_s),
        ))
    ]
    places = [slots_ref[k] for k in range(late_count // 2)]
    start_late, finish_late = narrow_copies(
        late_parts, late_stage, late_sems, places, far_up_s, far_down_s
    )

    def ready(what):
        @pl.when(step == 0)
        def _():
            if what == "out":
                for copy in copies:
                    copy.start()
                start_late()
                sums_ref[...] = jnp.zeros_like(sums_ref)
                up_sums_ref[...] = jnp.zeros_like(up_sums_ref)
                for copy in copies[:3]:
                    copy.wait()
                half = half_stage.shape[1]
                for k in range(2):
                    place = pl.multiple_of((core_ref[0] ^ k) * half, half)
                    far_out_s[pl.ds(place, half), :] = half_stage[k].astype(BF16)
            elif what == "near":
                for copy in copies[3:5]:
                    copy.wait()
            else:
                for copy in copies[5:]:
                    copy.wait()
                finish_late()

    @pl.when(step < tiles)
    def _():
        here = pl.ds(pl.multiple_of(step * tile, tile), tile)
        feed_rows(
            x_ref, cot_ref, ctx_ref, (far_ctx_ref,), vector_refs, ready, out_s, far_out_s, up_s,
            down_s, far_up_s, far_down_s, mixed_ref, d_pre_ref, d_attn_ref, sums_ref, up_sums_ref, nb_s, act_s,
            d_feed_s, d_hidden_s, here,
        )

    @pl.when(step >= tiles)
    def _():
        there = pl.ds(pl.multiple_of((step - tiles) * GRAD_TILE, GRAD_TILE), GRAD_TILE)
        d_down = dot_tn(d_feed_s[...], act_s[:, there])
        d_up = dot_tn(nb_s[...], d_hidden_s[:, there])
        if orders:
            write_halves(d_down, *grad_refs[:2], core_ref[0], orders[0], ())
            write_halves(d_up, *grad_refs[2:], core_ref[0], orders[1], ())
        else:
            grad_refs[0][...] = d_down
            grad_refs[1][...] = d_up


def feed(
    orders, core, slots, x, cotangent, context, far_context, out_weight, halves, vectors, up, down, far_up, far_down,
    late,
):
    rows, width = x.shape
    local, units = out_weight.shape[0], up.shape[1]
    tile = ROW_TILE
    tiles = rows // tile
    across = lambda cols: pl.BlockSpec((tile, cols), lambda i: (jnp.minimum(i, tiles - 1), 0))
    along = lambda height: pl.BlockSpec((height, tile), lambda i: (0, jnp.minimum(i, tiles - 1)))
    if orders:
        blocks = 2 ** len(orders[0])
        height = width // (2 * blocks)
        grad_specs = [
            pl.BlockSpec((blocks, height, GRAD_TILE), lambda i: (0, 0, jnp.maximum(i - tiles, 0)))
        ] * 4
        grad_shapes = [shape((blocks, height, units), F32)] * 4
    else:
        grad_specs = [pl.BlockSpec((width, GRAD_TILE), lambda i: (0, jnp.maximum(i - tiles, 0)))] * 2
        grad_shapes = [shape((width, units), F32)] * 2
    scalars = pl.BlockSpec(memory_space=pltpu.SMEM)
    anywhere = pl.BlockSpec(memory_space=pl.ANY)
    return pl.pallas_call(
        functools.partial(feed_kernel, orders, tiles, len(late)),
        grid=(tiles + units // GRAD_TILE,),
        in_specs=[
            scalars, scalars, across(width), across(width), along(local),
            *[along(part.shape[0]) for part in far_context], *[whole(v.shape[0]) for v in vectors],
            *[anywhere] * (7 + len(late)),
        ],
        out_specs=[
            across(width), across(width), across(width), whole(8, width), whole(1, units),
            *grad_specs,
        ],
        out_shape=[
            shape((rows, width), BF16), shape((rows, width), F32), shape((rows, width), BF16),
            shape((8, width), F32), shape((1, units), F32), *grad_shapes,
        ],
        scratch_shapes=[
            pltpu.VMEM((rows, width), BF16), pltpu.VMEM((rows, units), BF16), pltpu.VMEM((rows, width), BF16),
            pltpu.VMEM((rows, units), BF16),
            pltpu.VMEM((local, width), BF16), pltpu.VMEM((local, width), BF16),
            pltpu.VMEM((width, units), BF16), pltpu.VMEM((units, width), BF16),
            pltpu.VMEM((width, units), BF16), pltpu.VMEM((units, width), BF16),
            pltpu.VMEM((2,) + halves[0].shape, F32), pltpu.VMEM((len(late),) + late[0].shape[1:], F32),
            pltpu.SemaphoreType.DMA((7,)), pltpu.SemaphoreType.DMA((len(late),)),
        ],
        compiler_params=params_of(56),
        cost_estimate=cost(25e9, 30e6),
        name="feed",
    )(
        core, slots, x, cotangent, context, *far_context, *vectors, out_weight, *halves, up, down,
        far_up, far_down, *late,
    )


def make_body(n_items):
    def body(
        hidden_in,
        cluster_order,
        qkv_weight,
        qv_bias,
        out_weight,
        out_bias,
        norm1_gain,
        norm1_bias,
        up_weight,
        up_bias,
        down_weight,
        down_bias,
        norm2_gain,
        norm2_bias,
        cotangent,
    ):
        rows, width = hidden_in.shape
        units = up_weight.shape[1]
        local = out_weight.shape[0]
        item = lax.axis_index("items")
        core = item & 1
        group = 8
        place = item % group

        def piece(values):
            count = values.shape[0] // group
            return lax.dynamic_slice_in_dim(values, place * count, count, 0).astype(F32)[None]

        up_piece = piece(up_weight)
        two_rows = piece(after(down_weight, up_piece))
        middle = two_rows.shape[1] // 2
        down_piece = jnp.concatenate([two_rows[:, :middle], two_rows[:, middle:]], axis=2)
        far_a = swapped(up_piece)
        far_b = swapped(down_piece)
        far_bias = swapped(up_bias)
        half = local // 2

        ordering = cluster_order[:, 0, :]
        order_rows = ordering.reshape(-1, 2, rows)
        x = after(hidden_in, up_piece, down_piece)
        context, moved, probs = attend(x, qkv_weight, qv_bias.T, order_rows)
        pairs = order_rows.shape[0]
        far_context = [swapped(context.astype(F32))]
        out_piece = lax.dynamic_slice_in_dim(out_weight, core * half, half, 0).astype(F32)

        trade = lambda values, step: traded(values, step, n_items)
        at_once = lambda *values: lax.optimization_barrier(values)
        a0 = after(far_a, context)
        a4, a2 = trade(a0, 4), trade(a0, 2)
        b0 = after(far_b, a0)
        b4, b2 = trade(b0, 4), trade(b0, 2)
        a4, a2, _ = at_once(a4, a2, b0)
        a6 = trade(a4, 2)
        b4, b2, a6, far_context[0] = at_once(b4, b2, a6, far_context[0])
        b6 = trade(b4, 2)
        far_half = swapped(after(out_piece, b4))
        all_slots = lambda ks: jnp.stack([place ^ k for k in ks]).astype(jnp.int32)
        come = [part for one in ((a0, a4, a2), (b0, b4, b2)) for part in (*one, *(trade(p, 1) for p in one))]
        far_up, far_down = placed(all_slots((0, 4, 2, 1, 5, 3)), come, group)
        b6, far_half, far_bias, far_up = at_once(b6, far_half, far_bias, far_up)
        other_half = trade(far_half, 1)
        late, slots = [a6, trade(a6, 1), b6, trade(b6, 1)], all_slots((6, 7))
        which = core.astype(jnp.int32).reshape(1)

        split = width % (8 * n_items) == 0
        bits = tuple(range(1, n_items.bit_length() - 1))
        late_y = bits[1:2] + bits[:1] + bits[2:]
        mixed, d_pre, d_attn, sums, up_sums, *grads = feed(
            (bits, late_y) if split else None, which, slots, x, cotangent, context, far_context,
            out_weight, [far_half, other_half],
            [out_bias, norm1_gain, norm1_bias, down_bias, norm2_gain, norm2_bias, up_bias, far_bias],
            up_weight, down_weight, far_up, far_down, late,
        )

        def packed_of(grad_qv):
            return jnp.concatenate(
                [sums, up_sums.reshape(-1, width), grad_qv.reshape(-1, width)], axis=0
            )

        back = lambda d_attn: attend_back(
            (bits, late_y) if split else None, which, x, d_attn, out_weight, context, qkv_weight,
            order_rows, moved, probs,
        )
        if split:
            halving = lambda keep, send, order: Halving(keep, send, order, n_items).trade()
            down_sum, up_sum = halving(*grads[:2], bits), halving(*grads[2:], late_y)
            sent = arrived([down_sum, up_sum])
            down_sum.trade()
            up_sum.trade()
            part, grad_qv, *halves = back(after(d_attn, *sent))
            far_part = swapped(part)
            first, second = halving(*halves[:2], bits), halving(*halves[2:], late_y)
            sent = arrived([down_sum, up_sum], part)
            down_sum.trade()
            up_sum.trade()
            sent = arrived([first, second], *sent)
            first.trade()
            second.trade()
            first.extra = packed_of(after(grad_qv, *sent))
            first.extra = first.extra + traded(first.extra, 1, n_items)
            first.more = traded(first.extra, 1 << first.bit, n_items)
            sums_all = [down_sum, up_sum, first, second]
            for _ in bits[3:]:
                arrived(sums_all)
                for one in sums_all[::-1]:
                    one.trade()
            arrived(sums_all)
            first.trade()
            second.trade()
            together = traded(
                jnp.concatenate([down_sum.send, up_sum.send]), 1 << down_sum.bit, n_items
            )
            together, first.got, second.got, first.more = at_once(
                together, first.got, second.got, first.more
            )
            sent = [first.add(), second.add()]
            rest = traded(jnp.concatenate(sent), 1 << first.bit, n_items)
            first.more = traded(first.extra, 1 << first.bit, n_items)
            down_sum.got, up_sum.got = together[:1], together[1:]
            summed_down, summed_up = down_sum.add(), up_sum.add()
            far_part = after(far_part, summed_down, summed_up, *sent)
            grad_inputs = (d_pre + part + far_part).astype(BF16)
            rest, first.more, _ = at_once(rest, first.more, grad_inputs)
            first.got, second.got = rest[:1], rest[1:]
            summed = [first.add(), second.add()]
            summed_rest = [summed[c // 2][c % 2] for c in range(4)]
            packed = first.extra
        else:
            part, grad_qv, grad_rest = back(d_attn)
            grad_inputs = (d_pre + part + swapped(part)).astype(BF16)
            summed_down = scattered(grads[0], n_items, 0)
            summed_up = scattered(grads[1], n_items, 0)
            summed_rest = scattered(grad_rest, n_items, 1)
            packed = all_sum(packed_of(grad_qv), n_items)
        small = packed[:8]
        up_small = packed[8 : 8 + units // width].reshape(units)
        qv_small = packed[8 + units // width :].reshape(2, local)
        return (
            mixed,
            grad_inputs,
            jnp.stack([summed_rest[c] for c in range(3)]),
            qv_small,
            summed_rest[3].T,
            small[5],
            small[3],
            small[4],
            summed_up,
            up_small,
            summed_down.T,
            small[2],
            small[0],
            small[1],
        )

    return body


def solution(mesh):
    return jax.shard_map(
        make_body(mesh.shape["items"]),
        mesh=mesh,
        in_specs=(
            P("items", None),
            P("heads", "items", None),
            P(None, None, "heads"),
            P(None, "heads"),
            P("heads", None),
            P(),
            P(),
            P(),
            P(None, "heads"),
            P("heads"),
            P("heads", None),
            P(),
            P(),
            P(),
            P("items", None),
        ),
        out_specs=(
            P("items", None),
            P("items", None),
            P(None, "items", "heads"),
            P(None, "heads"),
            P("heads", "items"),
            P(),
            P(),
            P(),
            P("items", "heads"),
            P("heads"),
            P("heads", "items"),
            P(),
            P(),
            P(),
        ),
        check_vma=False,
    )
```

```python
import functools

import jax
import jax.numpy as jnp
from jax import lax
from jax.experimental import pallas as pl
from jax.experimental.pallas import tpu as pltpu
from jax.sharding import PartitionSpec as P

HEAD_DIM = 64
CLUSTER = 128
SCALE = HEAD_DIM**-0.5
EPSILON = 1e-05
ROW_TILE = 256
GRAD_TILE = 512
UNIT_TILE = 1536
BF16 = jnp.bfloat16
F32 = jnp.float32


def dot(left, right):
    return jnp.dot(left, right, preferred_element_type=F32)


def dot_nt(left, right):
    return lax.dot_general(left, right, (((1,), (1,)), ((), ())), preferred_element_type=F32)


def dot_tn(left, right):
    return lax.dot_general(left, right, (((0,), (0,)), ((), ())), preferred_element_type=F32)


def dot_tt(left, right):
    return lax.dot_general(left, right, (((0,), (1,)), ((), ())), preferred_element_type=F32)


def params_of(mib):
    return pltpu.CompilerParams(vmem_limit_bytes=mib * 1024 * 1024)


def cost(flops, bytes_accessed):
    return pl.CostEstimate(flops=int(flops) // 1000, bytes_accessed=int(bytes_accessed) // 1000, transcendentals=0)


def shape(dims, dtype):
    return jax.ShapeDtypeStruct(dims, dtype)


def whole(*dims):
    return pl.BlockSpec(dims, lambda *_: (0,) * len(dims), pipeline_mode=pl.Buffered(1))


def swapped(values):
    return lax.ppermute(values, "heads", [(0, 1), (1, 0)])


def traded(values, step, n_items):
    return lax.ppermute(values, "items", [(i, i ^ step) for i in range(n_items)])


def all_sum(values, n_items):
    step = 1
    while step < n_items:
        values = values + traded(values, step, n_items)
        step *= 2
    return values


def scattered(values, n_items, axis):
    item = lax.axis_index("items")
    size = n_items
    for bit in range(n_items.bit_length() - 1):
        dims = values.shape
        size //= 2
        halves = values.reshape(dims[:axis] + (size, 2, dims[axis] // (2 * size)) + dims[axis + 1 :])
        mine = (item >> bit) & 1
        send = lax.dynamic_index_in_dim(halves, 1 - mine, axis + 1, keepdims=False)
        keep = lax.dynamic_index_in_dim(halves, mine, axis + 1, keepdims=False)
        values = keep + traded(send, 1 << bit, n_items)
        values = values.reshape(dims[:axis] + (-1,) + dims[axis + 1 :])
    return values


class Halving:
    def __init__(self, keep, send, order, n_items):
        self.order, self.n_items, self.rest = list(order), n_items, keep.shape[1:]
        self.terms = []
        self.hold(keep)
        self.send, self.extra, self.bit = send, None, 0

    def hold(self, values):
        self.terms.append((values.reshape((2,) * len(self.order) + self.rest), []))

    def part(self, term, places):
        values, settled = term
        starts = settled + places
        sizes = (1,) * len(starts) + values.shape[len(starts) :]
        starts = starts + [0] * (values.ndim - len(starts))
        return lax.dynamic_slice(values, starts, sizes).reshape((-1,) + self.rest)

    def trade(self):
        self.got = traded(self.send, 1 << self.bit, self.n_items)
        if self.extra is not None:
            self.more = traded(self.extra, 1 << self.bit, self.n_items)
        return self

    def add(self):
        self.hold(self.got)
        if self.extra is not None:
            self.extra = self.extra + self.more
        if not self.order:
            return sum(self.part(term, []) for term in self.terms).reshape(self.rest)
        self.bit = self.order.pop(0)
        mine = (lax.axis_index("items") >> self.bit) & 1
        self.send = sum(self.part(term, [1 - mine]) for term in self.terms)
        self.terms = [(values, settled + [mine]) for values, settled in self.terms]
        return self.send


def arrived(sums, *before):
    got = [one.got for one in sums] + [one.more for one in sums if one.extra is not None]
    got = list(lax.optimization_barrier(tuple(got) + before))
    for one in sums:
        one.got = got.pop(0)
    for one in sums:
        if one.extra is not None:
            one.more = got.pop(0)
    return [one.add() for one in sums]


def after(values, *others):
    return lax.optimization_barrier((values,) + others)[0]


def selector(row_ref, h, sel_ref, slot):
    rows = sel_ref.shape[1]
    step = 256
    for r in range(0, rows, step):
        subs = lax.broadcasted_iota(jnp.int32, (step, rows), 0) + r
        found = jnp.where(row_ref[0, h : h + 1, :] == subs, 1.0, 0.0)
        sel_ref[slot, r : r + step, :] = found.astype(BF16)


def spans_of(rows):
    return [slice(c, c + CLUSTER) for c in range(0, rows, CLUSTER)]


def attend_kernel(x_ref, w_ref, bias_ref, row_ref, ctx_ref, moved_ref, probs_ref, sel_ref):
    rows = x_ref.shape[0]
    spans = spans_of(rows)
    for h in range(2):
        selector(row_ref, h, sel_ref, h)
    weight = jnp.concatenate([w_ref[c] for c in range(3)], axis=1)
    flat = dot_tt(weight, x_ref[...])
    parts = [flat[:128] + bias_ref[:, 0:1], flat[128:256], flat[256:] + bias_ref[:, 1:2]]
    parts = [part.astype(BF16) for part in parts]
    for h in range(2):
        cut = slice(h * HEAD_DIM, (h + 1) * HEAD_DIM)
        qkv = jnp.concatenate([part[cut] for part in parts], axis=0)
        moved = dot(qkv, sel_ref[h]).astype(BF16)
        moved_ref[h] = moved
        query, key, value = moved[:HEAD_DIM], moved[HEAD_DIM : 2 * HEAD_DIM], moved[2 * HEAD_DIM :]
        scores = jnp.concatenate([dot_tn(query[:, s], key[:, s]) for s in spans], axis=0) * SCALE
        shifted = jnp.exp(scores - jnp.max(scores, axis=-1, keepdims=True))
        probs = shifted / jnp.sum(shifted, axis=-1, keepdims=True)
        probs_b = probs.astype(BF16)
        probs_ref[h] = probs_b
        mixed = jnp.concatenate([dot_nt(value[:, s], probs_b[s]) for s in spans], axis=1)
        context = dot_nt(mixed.astype(BF16), sel_ref[h])
        ctx_ref[cut, :] = context.astype(BF16)


def attend(x, weight, bias_cols, order_rows):
    rows, width = x.shape
    pairs = order_rows.shape[0]
    local = weight.shape[2]
    return pl.pallas_call(
        attend_kernel,
        grid=(pairs,),
        in_specs=[
            whole(rows, width),
            pl.BlockSpec((3, width, 128), lambda p: (0, 0, p)),
            pl.BlockSpec((128, 2), lambda p: (p, 0)),
            pl.BlockSpec((1, 2, rows), lambda p: (p, 0, 0)),
        ],
        out_specs=[
            pl.BlockSpec((128, rows), lambda p: (p, 0)),
            pl.BlockSpec((2, 3 * HEAD_DIM, rows), lambda p: (p, 0, 0)),
            pl.BlockSpec((2, rows, CLUSTER), lambda p: (p, 0, 0)),
        ],
        out_shape=[
            shape((local, rows), BF16),
            shape((2 * pairs, 3 * HEAD_DIM, rows), BF16),
            shape((2 * pairs, rows, CLUSTER), BF16),
        ],
        scratch_shapes=[pltpu.VMEM((2, rows, rows), BF16)],
        compiler_params=params_of(58),
        cost_estimate=cost(12e9, 12e6),
        name="attend",
    )(x, weight, bias_cols, order_rows)


def block_place(j, order):
    place = 0
    for bit in order:
        place = 2 * place + ((j >> bit) & 1)
    return place


def write_halves(values, keep_ref, send_ref, mine, order, at):
    blocks = 2 ** (len(order) + 1)
    rows = values.shape[0] // blocks
    for j in range(0, blocks, 2):
        even, odd = values[j * rows : (j + 1) * rows], values[(j + 1) * rows : (j + 2) * rows]
        place = (block_place(j, order),) + at
        keep_ref[place] = jnp.where(mine == 0, even, odd)
        send_ref[place] = jnp.where(mine == 0, odd, even)


def attend_back_kernel(
    orders, core_ref, x_ref, da_ref, ow_ref, ctx_ref, w_ref, row_ref, moved_ref, probs_ref, part_ref, bias_ref, *refs
):
    *grad_refs, sel_ref = refs
    rows = da_ref.shape[0]
    spans = spans_of(rows)
    for h in range(2):
        selector(row_ref, h, sel_ref, h)
    d_attn = da_ref[...]
    d_context = dot_nt(ow_ref[...], d_attn).astype(BF16)
    d_out = dot_tt(d_attn, ctx_ref[...])
    found = []
    for h in range(2):
        d_moved = dot(d_context[h * HEAD_DIM : (h + 1) * HEAD_DIM], sel_ref[h]).astype(BF16)
        moved = moved_ref[h]
        query, key, value = moved[:HEAD_DIM], moved[HEAD_DIM : 2 * HEAD_DIM], moved[2 * HEAD_DIM :]
        probs_b = probs_ref[h]
        probs = probs_b.astype(F32)
        d_value = jnp.concatenate([dot(d_moved[:, s], probs_b[s]) for s in spans], axis=1)
        d_probs = jnp.concatenate([dot_tn(d_moved[:, s], value[:, s]) for s in spans], axis=0)
        inner = jnp.sum(probs * d_probs, axis=-1, keepdims=True)
        d_scores = (probs * (d_probs - inner)).astype(BF16)
        d_query = jnp.concatenate([dot_nt(key[:, s], d_scores[s]) for s in spans], axis=1) * SCALE
        d_key = jnp.concatenate([dot(query[:, s], d_scores[s]) for s in spans], axis=1) * SCALE
        three = jnp.concatenate([d_query, d_key, d_value], axis=0).astype(BF16)
        found.append(dot_nt(three, sel_ref[h]).astype(BF16))
    d_qkv = jnp.concatenate(
        [f[c * HEAD_DIM : (c + 1) * HEAD_DIM] for c in range(3) for f in found], axis=0
    )
    sums = dot_nt(jnp.ones((8, rows), BF16), d_qkv)
    bias_ref[0:1, :] = sums[0:1, :128]
    bias_ref[1:2, :] = sums[0:1, 256:]
    grads = dot_tt(x_ref[...], d_qkv)
    for c in range(4):
        values = grads[:, c * 128 : (c + 1) * 128] if c < 3 else d_out
        if orders:
            write_halves(values, *grad_refs[c // 2 * 2 :][:2], core_ref[0], orders[c // 2], (c % 2,))
        else:
            grad_refs[0][c] = values
    part = dot_tt(d_qkv, jnp.concatenate([w_ref[c] for c in range(3)], axis=1))

    @pl.when(pl.program_id(0) == 0)
    def _():
        part_ref[...] = part

    @pl.when(pl.program_id(0) > 0)
    def _():
        part_ref[...] += part


def attend_back(orders, core, x, d_attn, out_weight, context, weight, order_rows, moved, probs):
    rows, width = x.shape
    local = weight.shape[2]
    pairs = order_rows.shape[0]
    if orders:
        blocks = 2 ** len(orders[0])
        height = width // (2 * blocks)
        grad_specs = [pl.BlockSpec((blocks, 2, height, 128), lambda p: (0, 0, 0, p))] * 4
        grad_shapes = [shape((blocks, 2, height, local), F32)] * 4
    else:
        grad_specs = [pl.BlockSpec((4, width, 128), lambda p: (0, 0, p))]
        grad_shapes = [shape((4, width, local), F32)]
    return pl.pallas_call(
        functools.partial(attend_back_kernel, orders),
        grid=(pairs,),
        in_specs=[
            pl.BlockSpec(memory_space=pltpu.SMEM),
            whole(rows, width),
            whole(rows, width),
            pl.BlockSpec((128, width), lambda p: (p, 0)),
            pl.BlockSpec((128, rows), lambda p: (p, 0)),
            pl.BlockSpec((3, width, 128), lambda p: (0, 0, p)),
            pl.BlockSpec((1, 2, rows), lambda p: (p, 0, 0)),
            pl.BlockSpec((2, 3 * HEAD_DIM, rows), lambda p: (p, 0, 0)),
            pl.BlockSpec((2, rows, CLUSTER), lambda p: (p, 0, 0)),
        ],
        out_specs=[
            pl.BlockSpec((rows, width), lambda p: (0, 0)), pl.BlockSpec((2, 128), lambda p: (0, p)), *grad_specs
        ],
        out_shape=[shape((rows, width), F32), shape((2, local), F32), *grad_shapes],
        scratch_shapes=[pltpu.VMEM((2, rows, rows), BF16)],
        compiler_params=params_of(30),
        cost_estimate=cost(20e9, 20e6),
        name="attend_back",
    )(core, x, d_attn, out_weight, context, weight, order_rows, moved, probs)


def gelu_both(hidden):
    scale = 0.7978845608028654
    square = hidden * hidden
    bent = jnp.tanh(hidden * (scale + (scale * 0.044715) * square))
    half = 0.5 + 0.5 * bent
    active = hidden * half
    slope = half + 0.5 * hidden * (1.0 - bent * bent) * (scale + (3 * scale * 0.044715) * square)
    return active.astype(BF16), slope.astype(BF16)


def normalized(values):
    centred = values - jnp.mean(values, axis=-1, keepdims=True)
    factor = lax.rsqrt(jnp.mean(centred * centred, axis=-1, keepdims=True) + EPSILON)
    return centred * factor, factor


def norm_back(grad, unit, factor):
    mean = jnp.mean(grad, axis=-1, keepdims=True)
    inner = jnp.mean(grad * unit, axis=-1, keepdims=True)
    return factor * (grad - mean - unit * inner)


def unit_cuts(units):
    return [slice(u, u + UNIT_TILE) for u in range(0, units, UNIT_TILE)]


def narrow_copies(parts, stage, sems, places, up_out, down_out):
    rows, width = stage.shape[1], down_out.shape[1]
    copies = [
        pltpu.make_async_copy(part.at[0], stage.at[k], sems.at[k]) for k, part in enumerate(parts)
    ]

    def start():
        for copy in copies:
            copy.start()

    def finish():
        count = len(copies) // 2
        for k, copy in enumerate(copies):
            copy.wait()
            if k < count:
                place = pl.multiple_of(places[k] * rows, rows)
                up_out[pl.ds(place, rows), :] = stage[k].astype(BF16)
            else:
                for side in range(2):
                    place = pl.multiple_of((places[k - count] * 2 + side) * rows, rows)
                    cut = slice(side * width, (side + 1) * width)
                    down_out[pl.ds(place, rows), :] = stage[k, :, cut].astype(BF16)

    return start, finish


def placed_kernel(slots_ref, *refs):
    *parts, up_ref, down_ref, stage, sems = refs
    places = [slots_ref[k] for k in range(len(parts) // 2)]
    start, finish = narrow_copies(parts, stage, sems, places, up_ref, down_ref)
    start()
    finish()


def placed(slots, parts, group):
    _, rows, units = parts[0].shape
    width = units // 2
    dims = [(group * rows, units), (2 * group * rows, width)]
    return pl.pallas_call(
        placed_kernel,
        grid=(1,),
        in_specs=[pl.BlockSpec(memory_space=pltpu.SMEM)]
        + [pl.BlockSpec(memory_space=pl.ANY)] * len(parts),
        out_specs=[whole(*out) for out in dims],
        out_shape=[shape(out, BF16) for out in dims],
        scratch_shapes=[
            pltpu.VMEM((len(parts),) + parts[0].shape[1:], F32), pltpu.SemaphoreType.DMA((len(parts),))
        ],
        compiler_params=params_of(56),
        cost_estimate=cost(1e6, 1e6),
        name="placed",
    )(slots, *parts)


def feed_rows(
    x_ref, cot_ref, ctx_ref, far_ctx_refs, vector_refs, ready, out_s, far_out_s, up_s, down_s, far_up_s, far_down_s,
    mixed_ref, d_pre_ref, d_attn_ref, sums_ref, up_sums_ref, nb_s, act_s, d_feed_s, d_hidden_s, here,
):
    units = up_s.shape[1]
    row = lambda ref: ref[...].reshape(1, ref.shape[0])
    out_bias, gain1, bias1, down_bias, gain2, bias2, up_bias, far_bias = map(row, vector_refs)
    ready("out")
    attention = dot_tn(ctx_ref[...], out_s[...])
    far_ctx = jnp.concatenate([ref[...].astype(BF16) for ref in far_ctx_refs], axis=0)
    attention += dot_tn(far_ctx, far_out_s[...])
    unit1, factor1 = normalized(x_ref[...].astype(F32) + attention + out_bias)
    normed = unit1 * gain1 + bias1
    nb = normed.astype(BF16)
    nb_s[here, :] = nb
    total = normed + down_bias
    slopes, far_slopes = [], []
    ready("near")
    for cut in unit_cuts(units):
        active, slope = gelu_both(dot(nb, up_s[:, cut]) + up_bias[:, cut])
        act_s[here, cut] = active
        slopes.append(slope)
        total = total + dot(active, down_s[cut, :])
    ready("far")
    for cut in unit_cuts(units):
        far_active, far_slope = gelu_both(dot(nb, far_up_s[:, cut]) + far_bias[:, cut])
        far_slopes.append(far_slope)
        total = total + dot(far_active, far_down_s[cut, :])
    unit2, factor2 = normalized(total)
    mixed_ref[...] = (unit2 * gain2 + bias2).astype(BF16)
    grad = cot_ref[...].astype(F32)
    sums_ref[0:1, :] += jnp.sum(grad * unit2, axis=0, keepdims=True)
    sums_ref[1:2, :] += jnp.sum(grad, axis=0, keepdims=True)
    d_sum = norm_back(grad * gain2, unit2, factor2)
    d_feed = d_sum.astype(BF16)
    d_feed_s[here, :] = d_feed
    sums_ref[2:3, :] += jnp.sum(d_feed.astype(F32), axis=0, keepdims=True)
    d_normed = d_sum
    for cut, slope, far_slope in zip(unit_cuts(units), slopes, far_slopes):
        d_active = dot_nt(d_feed, down_s[cut, :])
        d_hidden = (d_active * slope.astype(F32)).astype(BF16)
        d_hidden_s[here, cut] = d_hidden
        up_sums_ref[:, cut] += jnp.sum(d_hidden.astype(F32), axis=0, keepdims=True)
        far_d_active = dot_nt(d_feed, far_down_s[cut, :])
        far_d_hidden = (far_d_active * far_slope.astype(F32)).astype(BF16)
        d_normed = d_normed + dot_nt(d_hidden, up_s[:, cut])
        d_normed = d_normed + dot_nt(far_d_hidden, far_up_s[:, cut])
    sums_ref[3:4, :] += jnp.sum(d_normed * unit1, axis=0, keepdims=True)
    sums_ref[4:5, :] += jnp.sum(d_normed, axis=0, keepdims=True)
    d_pre = norm_back(d_normed * gain1, unit1, factor1)
    d_pre_ref[...] = d_pre
    d_attn = d_pre.astype(BF16)
    d_attn_ref[...] = d_attn
    sums_ref[5:6, :] += jnp.sum(d_attn.astype(F32), axis=0, keepdims=True)


def feed_kernel(
    orders, tiles, late_count, core_ref, slots_ref, x_ref, cot_ref, ctx_ref, far_ctx_ref, *refs
):
    vector_refs, refs = refs[:8], refs[8:]
    out_hbm, near_half_hbm, far_half_hbm, up_hbm, down_hbm, far_up_hbm, far_down_hbm, *refs = refs
    late_parts, refs = refs[:late_count], refs[late_count:]
    mixed_ref, d_pre_ref, d_attn_ref, sums_ref, up_sums_ref, *refs = refs
    count = 4 if orders else 2
    grad_refs, refs = refs[:count], refs[count:]
    nb_s, act_s, d_feed_s, d_hidden_s, out_s, far_out_s, up_s, down_s, far_up_s, far_down_s, *refs = refs
    half_stage, late_stage, sems, late_sems = refs
    step = pl.program_id(0)
    tile = x_ref.shape[0]
    copies = [
        pltpu.make_async_copy(source, target, sems.at[k])
        for k, (source, target) in enumerate((
            (out_hbm, out_s), (near_half_hbm, half_stage.at[0]), (far_half_hbm, half_stage.at[1]),
            (up_hbm, up_s), (down_hbm, down_s), (far_up_hbm, far_up_s), (far_down_hbm, far_down_s),
        ))
    ]
    places = [slots_ref[k] for k in range(late_count // 2)]
    start_late, finish_late = narrow_copies(
        late_parts, late_stage, late_sems, places, far_up_s, far_down_s
    )

    def ready(what):
        @pl.when(step == 0)
        def _():
            if what == "out":
                for copy in copies:
                    copy.start()
                start_late()
                sums_ref[...] = jnp.zeros_like(sums_ref)
                up_sums_ref[...] = jnp.zeros_like(up_sums_ref)
                for copy in copies[:3]:
                    copy.wait()
                half = half_stage.shape[1]
                for k in range(2):
                    place = pl.multiple_of((core_ref[0] ^ k) * half, half)
                    far_out_s[pl.ds(place, half), :] = half_stage[k].astype(BF16)
            elif what == "near":
                for copy in copies[3:5]:
                    copy.wait()
            else:
                for copy in copies[5:]:
                    copy.wait()
                finish_late()

    @pl.when(step < tiles)
    def _():
        here = pl.ds(pl.multiple_of(step * tile, tile), tile)
        feed_rows(
            x_ref, cot_ref, ctx_ref, (far_ctx_ref,), vector_refs, ready, out_s, far_out_s, up_s,
            down_s, far_up_s, far_down_s, mixed_ref, d_pre_ref, d_attn_ref, sums_ref, up_sums_ref, nb_s, act_s,
            d_feed_s, d_hidden_s, here,
        )

    @pl.when(step >= tiles)
    def _():
        there = pl.ds(pl.multiple_of((step - tiles) * GRAD_TILE, GRAD_TILE), GRAD_TILE)
        d_down = dot_tn(d_feed_s[...], act_s[:, there])
        d_up = dot_tn(nb_s[...], d_hidden_s[:, there])
        if orders:
            write_halves(d_down, *grad_refs[:2], core_ref[0], orders[0], ())
            write_halves(d_up, *grad_refs[2:], core_ref[0], orders[1], ())
        else:
            grad_refs[0][...] = d_down
            grad_refs[1][...] = d_up


def feed(
    orders, core, slots, x, cotangent, context, far_context, out_weight, halves, vectors, up, down, far_up, far_down,
    late,
):
    rows, width = x.shape
    local, units = out_weight.shape[0], up.shape[1]
    tile = ROW_TILE
    tiles = rows // tile
    across = lambda cols: pl.BlockSpec((tile, cols), lambda i: (jnp.minimum(i, tiles - 1), 0))
    along = lambda height: pl.BlockSpec((height, tile), lambda i: (0, jnp.minimum(i, tiles - 1)))
    if orders:
        blocks = 2 ** len(orders[0])
        height = width // (2 * blocks)
        grad_specs = [
            pl.BlockSpec((blocks, height, GRAD_TILE), lambda i: (0, 0, jnp.maximum(i - tiles, 0)))
        ] * 4
        grad_shapes = [shape((blocks, height, units), F32)] * 4
    else:
        grad_specs = [pl.BlockSpec((width, GRAD_TILE), lambda i: (0, jnp.maximum(i - tiles, 0)))] * 2
        grad_shapes = [shape((width, units), F32)] * 2
    scalars = pl.BlockSpec(memory_space=pltpu.SMEM)
    anywhere = pl.BlockSpec(memory_space=pl.ANY)
    return pl.pallas_call(
        functools.partial(feed_kernel, orders, tiles, len(late)),
        grid=(tiles + units // GRAD_TILE,),
        in_specs=[
            scalars, scalars, across(width), across(width), along(local),
            *[along(part.shape[0]) for part in far_context], *[whole(v.shape[0]) for v in vectors],
            *[anywhere] * (7 + len(late)),
        ],
        out_specs=[
            across(width), across(width), across(width), whole(8, width), whole(1, units),
            *grad_specs,
        ],
        out_shape=[
            shape((rows, width), BF16), shape((rows, width), F32), shape((rows, width), BF16),
            shape((8, width), F32), shape((1, units), F32), *grad_shapes,
        ],
        scratch_shapes=[
            pltpu.VMEM((rows, width), BF16), pltpu.VMEM((rows, units), BF16), pltpu.VMEM((rows, width), BF16),
            pltpu.VMEM((rows, units), BF16),
            pltpu.VMEM((local, width), BF16), pltpu.VMEM((local, width), BF16),
            pltpu.VMEM((width, units), BF16), pltpu.VMEM((units, width), BF16),
            pltpu.VMEM((width, units), BF16), pltpu.VMEM((units, width), BF16),
            pltpu.VMEM((2,) + halves[0].shape, F32), pltpu.VMEM((len(late),) + late[0].shape[1:], F32),
            pltpu.SemaphoreType.DMA((7,)), pltpu.SemaphoreType.DMA((len(late),)),
        ],
        compiler_params=params_of(56),
        cost_estimate=cost(25e9, 30e6),
        name="feed",
    )(
        core, slots, x, cotangent, context, *far_context, *vectors, out_weight, *halves, up, down,
        far_up, far_down, *late,
    )


def make_body(n_items):
    def body(
        hidden_in,
        cluster_order,
        qkv_weight,
        qv_bias,
        out_weight,
        out_bias,
        norm1_gain,
        norm1_bias,
        up_weight,
        up_bias,
        down_weight,
        down_bias,
        norm2_gain,
        norm2_bias,
        cotangent,
    ):
        rows, width = hidden_in.shape
        units = up_weight.shape[1]
        local = out_weight.shape[0]
        item = lax.axis_index("items")
        core = item & 1
        group = 8
        place = item % group

        def piece(values):
            count = values.shape[0] // group
            return lax.dynamic_slice_in_dim(values, place * count, count, 0).astype(F32)[None]

        up_piece = piece(up_weight)
        two_rows = piece(after(down_weight, up_piece))
        middle = two_rows.shape[1] // 2
        down_piece = jnp.concatenate([two_rows[:, :middle], two_rows[:, middle:]], axis=2)
        far_a = swapped(up_piece)
        far_b = swapped(down_piece)
        far_bias = swapped(up_bias)
        half = local // 2

        ordering = cluster_order[:, 0, :]
        order_rows = ordering.reshape(-1, 2, rows)
        x = after(hidden_in, up_piece, down_piece)
        context, moved, probs = attend(x, qkv_weight, qv_bias.T, order_rows)
        pairs = order_rows.shape[0]
        far_context = [swapped(context.astype(F32))]
        out_piece = lax.dynamic_slice_in_dim(out_weight, core * half, half, 0).astype(F32)

        trade = lambda values, step: traded(values, step, n_items)
        at_once = lambda *values: lax.optimization_barrier(values)
        a0 = after(far_a, context)
        a4, a2 = trade(a0, 4), trade(a0, 2)
        b0 = after(far_b, a0)
        b4, b2 = trade(b0, 4), trade(b0, 2)
        a4, a2, _ = at_once(a4, a2, b0)
        a6 = trade(a4, 2)
        b4, b2, a6, far_context[0] = at_once(b4, b2, a6, far_context[0])
        b6 = trade(b4, 2)
        far_half = swapped(after(out_piece, b4))
        all_slots = lambda ks: jnp.stack([place ^ k for k in ks]).astype(jnp.int32)
        come = [part for one in ((a0, a4, a2), (b0, b4, b2)) for part in (*one, *(trade(p, 1) for p in one))]
        far_up, far_down = placed(all_slots((0, 4, 2, 1, 5, 3)), come, group)
        b6, far_half, far_bias, far_up = at_once(b6, far_half, far_bias, far_up)
        other_half = trade(far_half, 1)
        late, slots = [a6, trade(a6, 1), b6, trade(b6, 1)], all_slots((6, 7))
        which = core.astype(jnp.int32).reshape(1)

        split = width % (8 * n_items) == 0
        bits = tuple(range(1, n_items.bit_length() - 1))
        late_y = bits[1:2] + bits[:1] + bits[2:]
        mixed, d_pre, d_attn, sums, up_sums, *grads = feed(
            (bits, late_y) if split else None, which, slots, x, cotangent, context, far_context,
            out_weight, [far_half, other_half],
            [out_bias, norm1_gain, norm1_bias, down_bias, norm2_gain, norm2_bias, up_bias, far_bias],
            up_weight, down_weight, far_up, far_down, late,
        )

        def packed_of(grad_qv):
            return jnp.concatenate(
                [sums, up_sums.reshape(-1, width), grad_qv.reshape(-1, width)], axis=0
            )

        back = lambda d_attn: attend_back(
            (bits, late_y) if split else None, which, x, d_attn, out_weight, context, qkv_weight,
            order_rows, moved, probs,
        )
        if split:
            halving = lambda keep, send, order: Halving(keep, send, order, n_items).trade()
            down_sum, up_sum = halving(*grads[:2], bits), halving(*grads[2:], late_y)
            sent = arrived([down_sum])
            down_sum.trade()
            sent += arrived([up_sum], *sent)
            up_sum.trade()
            part, grad_qv, *halves = back(after(d_attn, *sent))
            far_part = swapped(part)
            first, second = halving(*halves[:2], bits), halving(*halves[2:], late_y)
            sent = arrived([down_sum, up_sum], part)
            down_sum.trade()
            up_sum.trade()
            sent = arrived([first, second], *sent)
            first.trade()
            second.trade()
            first.extra = packed_of(after(grad_qv, *sent))
            first.extra = first.extra + traded(first.extra, 1, n_items)
            first.more = traded(first.extra, 1 << first.bit, n_items)
            sums_all = [down_sum, up_sum, first, second]
            for _ in bits[3:]:
                arrived(sums_all)
                for one in sums_all[::-1]:
                    one.trade()
            arrived(sums_all)
            first.trade()
            second.trade()
            together = traded(
                jnp.concatenate([down_sum.send, up_sum.send]), 1 << down_sum.bit, n_items
            )
            together, first.got, second.got, first.more = at_once(
                together, first.got, second.got, first.more
            )
            sent = [first.add(), second.add()]
            rest = traded(jnp.concatenate(sent), 1 << first.bit, n_items)
            first.more = traded(first.extra, 1 << first.bit, n_items)
            down_sum.got, up_sum.got = together[:1], together[1:]
            summed_down, summed_up = down_sum.add(), up_sum.add()
            far_part = after(far_part, summed_down, summed_up, *sent)
            grad_inputs = (d_pre + part + far_part).astype(BF16)
            rest, first.more, _ = at_once(rest, first.more, grad_inputs)
            first.got, second.got = rest[:1], rest[1:]
            summed = [first.add(), second.add()]
            summed_rest = [summed[c // 2][c % 2] for c in range(4)]
            packed = first.extra
        else:
            part, grad_qv, grad_rest = back(d_attn)
            grad_inputs = (d_pre + part + swapped(part)).astype(BF16)
            summed_down = scattered(grads[0], n_items, 0)
            summed_up = scattered(grads[1], n_items, 0)
            summed_rest = scattered(grad_rest, n_items, 1)
            packed = all_sum(packed_of(grad_qv), n_items)
        small = packed[:8]
        up_small = packed[8 : 8 + units // width].reshape(units)
        qv_small = packed[8 + units // width :].reshape(2, local)
        return (
            mixed,
            grad_inputs,
            jnp.stack([summed_rest[c] for c in range(3)]),
            qv_small,
            summed_rest[3].T,
            small[5],
            small[3],
            small[4],
            summed_up,
            up_small,
            summed_down.T,
            small[2],
            small[0],
            small[1],
        )

    return body


def solution(mesh):
    return jax.shard_map(
        make_body(mesh.shape["items"]),
        mesh=mesh,
        in_specs=(
            P("items", None),
            P("heads", "items", None),
            P(None, None, "heads"),
            P(None, "heads"),
            P("heads", None),
            P(),
            P(),
            P(),
            P(None, "heads"),
            P("heads"),
            P("heads", None),
            P(),
            P(),
            P(),
            P("items", None),
        ),
        out_specs=(
            P("items", None),
            P("items", None),
            P(None, "items", "heads"),
            P(None, "heads"),
            P("heads", "items"),
            P(),
            P(),
            P(),
            P("items", "heads"),
            P("heads"),
            P("heads", "items"),
            P(),
            P(),
            P(),
        ),
        check_vma=False,
    )
```
